32 devices in a mesh: seq: 8 (over z, x), tensor: 4 (over y, core).
Axes of the slice: x: 2, y: 2, z: 4, core: 2. Of those that a mesh axis runs over, the one named last changes fastest.
Arguments:
- x_in: bfloat16 [8192, 2048], P('seq'), may hold values from -6 to 6
- norm_gain: float32 [2048], replicated, may hold values from 0.5 to 1.5
- w_zx: bfloat16 [2048, 2, 4096], P(None, None, 'tensor'), may hold values from -0.125 to 0.125
- w_bc: bfloat16 [2048, 256], replicated, may hold values from -0.125 to 0.125
- w_dt: bfloat16 [2048, 64], P(None, 'tensor'), may hold values from -0.125 to 0.125
- conv_x: float32 [5, 4096], P(None, 'tensor'), may hold values from -0.6 to 0.6
- conv_bc: float32 [5, 256], replicated, may hold values from -0.6 to 0.6
- head_params: float32 [3, 64], P(None, 'tensor'), may hold values from -8 to 1.5
- gate_gain: float32 [4096], P('tensor'), may hold values from 0.5 to 1.5
- w_out: bfloat16 [4096, 2048], P('tensor'), may hold values from -0.09375 to 0.09375
- lengths: int32 [6], replicated, may hold values from 256 to 4096, as said below
- grad_out: bfloat16 [8192, 2048], P('seq', 'tensor'), may hold values from -6 to 6
Outputs:
- block_out: bfloat16 [8192, 2048], P('seq', 'tensor')
- grad_x: float32 [8192, 2048], P('seq', 'tensor')
- grad_norm_gain: float32 [2048], replicated
- grad_w_zx: float32 [2048, 2, 4096], P('seq', None, 'tensor')
- grad_w_bc: float32 [2048, 256], replicated
- grad_w_dt: float32 [2048, 64], P('seq', 'tensor')
- grad_conv_x: float32 [5, 4096], P(None, 'tensor')
- grad_conv_bc: float32 [5, 256], replicated
- grad_head: float32 [3, 64], P(None, 'tensor')
- grad_gate_gain: float32 [4096], P('tensor')
- grad_w_out: float32 [4096, 2048], P('tensor', 'seq')
The draws below stay inside these ranges and needn't reach their ends.
Inputs may be any that keep to these rules, and one draw needn't show every extreme that they name: Each sequence holds at most 4096 tokens, and some sequence holds exactly 4096. The lengths sum to 8192.
All inputs are finite; a program needn't handle non-finite values.
Results may differ from the reference program's by a relative error of at most 0.014.
The reference program's roundings to bfloat16 on the way count: a program that leaves them out, or rounds other values in their place, can miss the bound.
Values may be sent and summed in bfloat16 or wider, within the bound.
No kernel may reach another device: no remote copies, remote signals or barrier semaphores. Data moves between devices by JAX's collectives and lax.ppermute only.
A program may use at most 192 MiB of HBM per device.

```python
import math
from functools import partial
import jax
import jax.numpy as jnp
from jax import lax

D = 2048
HEADS = 64
HEAD_DIM = 64
STATE = 128
WIDTH = 4
SPAN = 256
TOK_DEV = 1024
LONG = 4096
SEQS = 6
INNER = 4096
TOKENS = 8192


def draw_head_params(key, part):
    key = jax.random.fold_in(key, 7)
    keys = jax.random.split(key, 4)
    bias_row = jax.random.uniform(keys[0], (HEADS,), jnp.float32, -1.5, -0.5)
    slow_share = 0.5
    slow_top = 4.4
    slow_pick = jax.random.uniform(keys[1], (HEADS,), jnp.float32) < slow_share
    spread = jax.random.uniform(keys[2], (HEADS,), jnp.float32, 0.0, 1.0)
    slow_low = math.log(2.2 / TOK_DEV)
    slow_high = math.log(slow_top / TOK_DEV)
    slow_log = slow_low + (slow_high - slow_low) * spread
    fast_log = math.log(0.05) + (math.log(0.2) - math.log(0.05)) * spread
    rate_row = jnp.where(slow_pick, slow_log, fast_log)
    skip_row = jax.random.uniform(keys[3], (HEADS,), jnp.float32, 0.5, 1.5)
    return jnp.stack([bias_row, rate_row, skip_row]).astype(jnp.float32)


def draw_lengths(key, part):
    key = jax.random.fold_in(key, 11)
    keys = jax.random.split(key, 2)
    group_count = (SEQS - 1) // 5
    head_len = jax.random.randint(keys[0], (), TOK_DEV // 4, 3 * TOK_DEV // 4 + 1).astype(jnp.int32)
    long_place = jax.random.randint(keys[1], (group_count,), 0, 4).astype(jnp.int32)
    slots = jnp.arange(5, dtype=jnp.int32)
    group_lens = jnp.where(slots[None, :] == long_place[:, None], LONG, TOK_DEV).astype(jnp.int32)
    flat = group_lens.reshape(group_count * 5)
    flat = flat.at[group_count * 5 - 1].add(-head_len)
    return jnp.concatenate([head_len[None], flat]).astype(jnp.int32)


def raised(result, own_key, source, target, parts, factor):
    def block_of(dim):
        return (jnp.arange(result.shape[dim]) // (result.shape[dim] // parts)).reshape((-1,) + (1,) * (result.ndim - 1 - dim))

    one_side = jax.random.permutation(own_key, parts)[block_of(target)]
    second = (block_of(target) + parts // 2) % parts
    return jnp.where((block_of(source) == one_side) | (block_of(source) == second), factor * result, result)


def shard_levels(stream_key, dims, cuts, low, top_value):
    def one(axis_at, parts):
        heights = jax.random.uniform(jax.random.fold_in(jax.random.fold_in(stream_key, 6), axis_at), (parts,), jnp.float32, low / len(cuts), top_value / len(cuts))
        return jnp.repeat(jnp.exp(heights), dims[axis_at] // parts).reshape((-1,) + (1,) * (len(dims) - axis_at - 1))

    loudness = one(*cuts[0])
    for cut in cuts[1:]:
        loudness = loudness * one(*cut)
    return loudness


def scatter_about(own_key, shape, scale, most, shards=(), kind=jnp.bfloat16):
    gain = shard_levels(own_key, shape, shards, -0.22, 0.18) if shards else 1.0
    array = jax.random.normal(own_key, shape, jnp.float32) * scale * gain
    return jnp.minimum(jnp.maximum(array, -most), most).astype(kind)


def heavy_noise(stream_key, extent, scale, reach, shards, heavy, kind=jnp.bfloat16):
    array = scale * jax.random.normal(stream_key, extent, jnp.float32)
    if shards:
        array = array * shard_levels(stream_key, extent, shards, -0.22, 0.18)
    return jnp.clip(raised(array, jax.random.fold_in(stream_key, 3), *heavy), -reach, reach).astype(kind)


def setup_inputs(seed: int = 0) -> dict:
    key_list = jax.random.split(jax.random.key(seed), 13)
    x_in = heavy_noise(key_list[0], (TOKENS, D), 1.0, 6.0, ((0, 8),), (0, 1, 8, 2.0))
    norm_gain = jnp.clip(1.0 + 0.1 * jax.random.normal(key_list[1], (D,), jnp.float32), 0.5, 1.5)
    w_zx = scatter_about(key_list[2], (D, 2, INNER), D ** -0.5, 0.125, ((2, 4),))
    w_bc = scatter_about(key_list[3], (D, 2 * STATE), D ** -0.5, 0.125)
    w_dt = scatter_about(key_list[4], (D, HEADS), D ** -0.5, 0.125, ((1, 4),))
    conv_x = jnp.clip(jax.random.uniform(key_list[5], (WIDTH + 1, INNER), jnp.float32, -0.6, 0.6) * shard_levels(key_list[5], (WIDTH + 1, INNER), ((1, 4),), -0.4, 0.0), -0.6, 0.6)
    conv_bc = jnp.clip(jax.random.uniform(key_list[6], (WIDTH + 1, 2 * STATE), jnp.float32, -0.6, 0.6), -0.6, 0.6)
    head_params = draw_head_params(jax.random.fold_in(key_list[12], 71), 0)
    gate_gain = jnp.clip(1.0 + 0.1 * jax.random.normal(key_list[8], (INNER,), jnp.float32), 0.5, 1.5)
    w_out = scatter_about(key_list[9], (INNER, D), INNER ** -0.5, 0.09375, ((0, 4),))
    lengths = draw_lengths(jax.random.fold_in(key_list[12], 71), 0)
    grad_out = heavy_noise(key_list[11], (TOKENS, D), 1.0, 6.0, ((0, 8), (1, 4)), (0, 1, 8, 2.0))
    return {"x_in": x_in, "norm_gain": norm_gain, "w_zx": w_zx, "w_bc": w_bc, "w_dt": w_dt, "conv_x": conv_x, "conv_bc": conv_bc, "head_params": head_params, "gate_gain": gate_gain, "w_out": w_out, "lengths": lengths, "grad_out": grad_out}


eps = 1e-05
highest = lax.Precision.HIGHEST

@jax.custom_vjp
def low(v):
    return lax.optimization_barrier(v.astype(jnp.bfloat16)).astype(jnp.float32)

@jax.custom_vjp
def low_back(v):
    return v

def low_keep(v):
    return (low(v), None)

def low_pass(kept, grad):
    return (grad,)

def back_keep(v):
    return (v, None)

def back_low(kept, grad):
    return (low(grad),)
low.defvjp(low_keep, low_pass)
low_back.defvjp(back_keep, back_low)

def segment_ids(lengths):
    starts = (jnp.cumsum(lengths) - lengths).astype(jnp.int32)
    places = jnp.arange(TOKENS, dtype=jnp.int32)
    return (lax.optimization_barrier(jnp.sum((places[:, None] >= starts[None, :]).astype(jnp.int32), axis=1)) - 1).astype(jnp.int32)

def causal_conv(seg_ids, inputs, weights):
    summed = weights[WIDTH][None, :] + weights[WIDTH - 1][None, :] * inputs
    for back_step in range(1, WIDTH):
        shifted = jnp.pad(inputs, ((back_step, 0), (0, 0)))[:TOKENS]
        earlier = jnp.pad(seg_ids, (back_step, 0), constant_values=-1)[:TOKENS]
        is_valid = (earlier == seg_ids).astype(jnp.float32)[:, None]
        summed = summed + weights[WIDTH - 1 - back_step][None, :] * shifted * is_valid
    return jax.nn.silu(summed)

def span_apply(decay_rate, held_state, block):
    x_block, b_block, c_block, dt_block, seg_block, prev_seg = block
    log_decay = jnp.cumsum(-dt_block * decay_rate[None, :], axis=0)
    positions = jnp.arange(SPAN, dtype=jnp.int32)
    same_seq = (seg_block[:, None] == seg_block[None, :]) & (positions[:, None] >= positions[None, :])
    decay_t = log_decay.T
    gap_log = decay_t[:, :, None] - decay_t[:, None, :]
    decay_matrix = jnp.where(same_seq[None], jnp.exp(jnp.minimum(gap_log, 0.0)), 0.0)
    gram_matrix = jnp.dot(c_block, b_block.T, precision=highest)
    mixing = decay_matrix * gram_matrix[None] * dt_block.T[:, None, :]
    inside = jnp.einsum('hij,jhp->ihp', mixing, x_block, precision=highest)
    keep_in = (seg_block == prev_seg).astype(jnp.float32)
    in_weight = jnp.exp(log_decay) * keep_in[:, None]
    carried = jnp.einsum('in,hpn->ihp', c_block, held_state, precision=highest) * in_weight[:, :, None]
    keep_out = (seg_block == seg_block[SPAN - 1]).astype(jnp.float32)
    out_weight = jnp.exp(log_decay[SPAN - 1][None, :] - log_decay) * keep_out[:, None] * dt_block
    local_state = jnp.einsum('jhp,jn->hpn', out_weight[:, :, None] * x_block, b_block, precision=highest)
    decays = jnp.exp(log_decay[SPAN - 1]) * keep_in[SPAN - 1]
    new_state = decays[:, None, None] * held_state + local_state
    return (new_state, inside + carried)

def state_space(seg_ids, x_heads, b_vals, c_vals, step_size, decay_rate):
    blocks_n = TOKENS // SPAN
    previous = jnp.concatenate([jnp.full((1,), -1, jnp.int32), seg_ids[:-1]])
    blocks = (x_heads.reshape(blocks_n, SPAN, HEADS, HEAD_DIM), b_vals.reshape(blocks_n, SPAN, STATE), c_vals.reshape(blocks_n, SPAN, STATE), step_size.reshape(blocks_n, SPAN, HEADS), seg_ids.reshape(blocks_n, SPAN), previous.reshape(blocks_n, SPAN)[:, 0])
    initial = jnp.zeros((HEADS, HEAD_DIM, STATE), jnp.float32)
    _, outputs = lax.scan(jax.checkpoint(partial(span_apply, decay_rate)), initial, blocks)
    return outputs.reshape(TOKENS, HEADS, HEAD_DIM)

def forward(seg_ids, x_float, norm_gain, w_zx, w_bc, w_dt, conv_x, conv_bc, head_params, gate_gain, w_out):
    unit = x_float * lax.rsqrt(lax.optimization_barrier(jnp.mean(x_float * x_float, axis=1, keepdims=True)) + eps)
    normed = low(unit * norm_gain[None, :])
    zx_proj = jnp.dot(normed, w_zx.reshape(D, 2 * INNER), precision=highest)
    gate_in = low_back(zx_proj[:, :INNER])
    x_proj = low(low_back(zx_proj[:, INNER:]))
    bc_proj = low(low_back(jnp.dot(normed, w_bc, precision=highest)))
    dt_raw = low_back(jnp.dot(normed, w_dt, precision=highest))
    x_conv = low(causal_conv(seg_ids, x_proj, conv_x))
    bc_conv = low(causal_conv(seg_ids, bc_proj, conv_bc))
    step_size = jax.nn.softplus(dt_raw + head_params[0][None, :])
    decay_rate = jnp.exp(head_params[1])
    x_heads = x_conv.reshape(TOKENS, HEADS, HEAD_DIM)
    mixed = state_space(seg_ids, x_heads, bc_conv[:, :STATE], bc_conv[:, STATE:], step_size, decay_rate)
    mixed = (mixed + head_params[2][None, :, None] * x_heads).reshape(TOKENS, INNER)
    gated = mixed * jax.nn.silu(gate_in)
    gate_unit = gated * lax.rsqrt(lax.optimization_barrier(jnp.mean(gated * gated, axis=1, keepdims=True)) + eps)
    gate_normed = low(gate_unit * gate_gain[None, :])
    return x_float + jnp.dot(gate_normed, w_out, precision=highest)

def reference(x_in, norm_gain, w_zx, w_bc, w_dt, conv_x, conv_bc, head_params, gate_gain, w_out, lengths, grad_out):
    seg_ids = segment_ids(lengths)
    inputs = (x_in.astype(jnp.float32), norm_gain, w_zx.astype(jnp.float32), w_bc.astype(jnp.float32), w_dt.astype(jnp.float32), conv_x, conv_bc, head_params, gate_gain, w_out.astype(jnp.float32))
    block_out, pull_back = jax.vjp(partial(forward, seg_ids), *inputs)
    gradients = pull_back(grad_out.astype(jnp.float32))
    return (block_out.astype(jnp.bfloat16), gradients[0], gradients[1], gradients[2], gradients[3], gradients[4], gradients[5], gradients[6], gradients[7], gradients[8], gradients[9])
```

```python
from functools import partial

import jax
import jax.numpy as jnp
from jax import lax
from jax.experimental import pallas as pl
from jax.experimental.pallas import tpu as pltpu
from jax.sharding import PartitionSpec as P

HEAD_DIM = 64
STATE = 128
WIDTH = 4
CHUNK = 128
REACH = 4096
PAD = 8
HALO = 16

eps = 1e-05
f32 = jnp.float32
bf16 = jnp.bfloat16
highest = lax.Precision.HIGHEST
vmem_limit = 56 * 1024 * 1024


def nn(a, b):
    return lax.dot_general(a, b, (((1,), (0,)), ((), ())), preferred_element_type=f32)


def nt(a, b):
    return lax.dot_general(a, b, (((1,), (1,)), ((), ())), preferred_element_type=f32)


def exact(a, b):
    return lax.dot_general(
        a, b, (((1,), (0,)), ((), ())), precision=highest, preferred_element_type=f32
    )


def head_map(heads):
    row = lax.broadcasted_iota(jnp.int32, (heads, heads * HEAD_DIM), 0)
    col = lax.broadcasted_iota(jnp.int32, (heads, heads * HEAD_DIM), 1)
    return jnp.where((col >> 6) == row, 1.0, 0.0).astype(bf16)


def spread(v, member):
    high = v.astype(bf16)
    rest = (v - high.astype(f32)).astype(bf16)
    return nn(high, member) + nn(rest, member)


def spread_row(v, member):
    return spread(jnp.broadcast_to(v, (PAD, v.shape[1])), member)[0:1]


def per_head(v, member):
    return nt(v.astype(bf16), member)


def triangle(strict, upper):
    row = lax.broadcasted_iota(jnp.int32, (CHUNK, CHUNK), 0)
    col = lax.broadcasted_iota(jnp.int32, (CHUNK, CHUNK), 1)
    if upper:
        row, col = col, row
    keep = (row > col) if strict else (row >= col)
    return jnp.where(keep, 1.0, 0.0).astype(f32)


def softplus(v):
    return jnp.maximum(v, 0.0) + jnp.log1p(jnp.exp(-jnp.abs(v)))


def sigmoid(v):
    return 1.0 / (1.0 + jnp.exp(-v))


def seg_bounds(info_ref, chunk):
    info = info_ref[...] - chunk * CHUNK
    return info[:, 0:1], info[:, 1:2]


def row_ids():
    return lax.broadcasted_iota(jnp.int32, (CHUNK, 1), 0)


def flag(v):
    return jnp.where(v, 1.0, 0.0).astype(f32)


def conv_pre(ext_ref, w_ref, masks, base, lo, wide):
    cols = slice(base + lo, base + lo + wide)
    taps = slice(lo, lo + wide)
    total = w_ref[WIDTH : WIDTH + 1, taps] + w_ref[WIDTH - 1 : WIDTH, taps] * ext_ref[
        PAD : PAD + CHUNK, cols
    ]
    for back in range(1, WIDTH):
        total = total + w_ref[WIDTH - 1 - back : WIDTH - back, taps] * (
            ext_ref[PAD - back : PAD - back + CHUNK, cols] * masks[back]
        )
    return total


def fwd_kernel(
    ux_ref, ubc_ref, hx_ref, hbc_ref, cx_ref, cbc_ref, dtr_ref, hp_ref, info_ref,
    xa_ref, bca_ref, dt_ref, log_ref, sloc_ref, send_ref,
    ext, held, drun,
):
    chunk = pl.program_id(0)
    inner = ux_ref.shape[1]
    heads = dtr_ref.shape[1]

    @pl.when(chunk == 0)
    def _():
        ext[0:PAD, 0:inner] = hx_ref[...].astype(f32)[HALO - PAD : HALO]
        ext[0:PAD, inner:] = hbc_ref[...].astype(f32)[HALO - PAD : HALO]
        held[...] = jnp.zeros_like(held)
        drun[...] = jnp.ones_like(drun)

    @pl.when(chunk > 0)
    def _():
        ext[0:PAD, :] = ext[CHUNK : CHUNK + PAD, :]

    ext[PAD:, 0:inner] = ux_ref[...].astype(f32)
    ext[PAD:, inner:] = ubc_ref[...].astype(f32)
    first, last = seg_bounds(info_ref, chunk)
    rows = row_ids()
    wide = 256
    masks = [None] + [
        jnp.broadcast_to(flag(rows - back >= first), (CHUNK, wide)) for back in range(1, WIDTH)
    ]
    for lo in range(0, inner, wide):
        pre = conv_pre(ext, cx_ref, masks, 0, lo, wide)
        xa_ref[:, lo : lo + wide] = (pre * sigmoid(pre)).astype(bf16)
    pre = conv_pre(ext, cbc_ref, masks, inner, 0, 2 * STATE)
    bca_ref[...] = (pre * sigmoid(pre)).astype(bf16)

    member = head_map(heads)
    dt = softplus(dtr_ref[...] + hp_ref[0:1, :])
    rate = jnp.exp(hp_ref[1:2, :])
    logs = exact(triangle(False, False), -dt * rate)
    dt_ref[...] = dt
    log_ref[...] = logs
    tail = logs[CHUNK - 1 : CHUNK, :]
    keep_in = flag(first < 0)
    keep_out = flag(last >= CHUNK)
    weight = jnp.exp(tail - logs) * keep_out * dt
    decay = jnp.exp(tail) * keep_in[CHUNK - 1 : CHUNK, :]
    x_in = (xa_ref[...].astype(f32) * spread(weight, member)).astype(bf16)
    b_cols = jnp.transpose(bca_ref[:, 0:STATE].astype(f32)).astype(bf16)
    local = nn(b_cols, x_in)
    decay_all = spread_row(decay, member)
    sloc_ref[...] = held[...].astype(bf16)[None]
    held[...] = decay_all * held[...] + local
    drun[...] = drun[...] * decay_all

    @pl.when(chunk == pl.num_programs(0) - 1)
    def _():
        total = drun[...]
        high = total.astype(bf16)
        send_ref[0:STATE, :] = held[...].astype(bf16)
        send_ref[STATE:, :] = jnp.concatenate(
            [total, total - high.astype(f32)], axis=0
        ).astype(bf16)


def intra_kernel(xa_ref, bca_ref, dt_ref, log_ref, sloc_ref, hp_ref, info_ref, y_ref):
    chunk = pl.program_id(0)
    heads = dt_ref.shape[1]
    member = head_map(heads)
    first, _ = seg_bounds(info_ref, chunk)
    rows = lax.broadcasted_iota(jnp.int32, (CHUNK, CHUNK), 0)
    cols = lax.broadcasted_iota(jnp.int32, (CHUNK, CHUNK), 1)
    b = bca_ref[:, 0:STATE]
    c = bca_ref[:, STATE:]
    mixed = jnp.where((cols <= rows) & (cols >= first), nt(c, b), 0.0)
    logs = log_ref[...]
    keep_in = flag(first < 0)
    logs_t = jnp.transpose(logs)
    x = xa_ref[...].astype(f32)
    xd = x * spread(dt_ref[...], member)
    skip = spread_row(hp_ref[2:3, :], member)
    carried = spread(jnp.exp(logs) * keep_in, member) * nn(c, sloc_ref[0]) + skip * x
    lane = lax.broadcasted_iota(jnp.int32, (1, 2 * HEAD_DIM), 1)
    left = flag(lane < HEAD_DIM)
    right = 1.0 - left
    for pair in range(heads // 2):
        mats = []
        for h in (2 * pair, 2 * pair + 1):
            gap = logs[:, h : h + 1] - logs_t[h : h + 1, :]
            mats.append((jnp.exp(jnp.minimum(gap, 0.0)) * mixed).astype(bf16))
        at = slice(2 * pair * HEAD_DIM, 2 * (pair + 1) * HEAD_DIM)
        xp = xd[:, at]
        block = jnp.concatenate([(xp * left).astype(bf16), (xp * right).astype(bf16)], axis=0)
        y_ref[:, at] = carried[:, at] + nn(jnp.concatenate(mats, axis=1), block)


def gate_sums_kernel(
    yl_ref, bca_ref, log_ref, sloc_ref, sin_ref, z_ref, gg_ref, gain_ref, info_ref,
    y_ref, sent_ref, sums_ref,
    dpre,
):
    chunk = pl.program_id(0)
    heads = log_ref.shape[1]
    member = head_map(heads)

    @pl.when(chunk == 0)
    def _():
        dpre[...] = jnp.ones_like(dpre)

    first, _ = seg_bounds(info_ref, chunk)
    keep_in = flag(first < 0)
    before = dpre[0:1, :]
    gate = jnp.exp(log_ref[...]) * keep_in
    state = sin_ref[...]
    sent_ref[...] = (sloc_ref[0].astype(f32) + spread_row(before, member) * state).astype(bf16)[None]
    carried = spread(gate * before, member) * nn(bca_ref[:, STATE:], state.astype(bf16))
    y = yl_ref[...] + carried
    y_ref[...] = y
    z = z_ref[...]
    gated = y * z * sigmoid(z)
    squares = jnp.sum(gated * gated, axis=1, keepdims=True)
    dots = jnp.sum(gated * gg_ref[...] * gain_ref[...], axis=1, keepdims=True)
    lane = lax.broadcasted_iota(jnp.int32, (CHUNK, STATE), 1)
    both = jnp.where(lane == 0, squares, jnp.where(lane == 1, dots, 0.0))
    sums_ref[...] = jnp.transpose(both)[0:PAD][None]
    dpre[...] = dpre[...] * gate[CHUNK - 1 : CHUNK, :]


def gate_back_kernel(
    y_ref, z_ref, gg_ref, sums_ref, gain_ref, xa_ref, bca_ref, log_ref, info_ref,
    gn_ref, gz_ref, gy_ref, lloc_ref, send_ref, ggain_ref, gskip_ref,
    held, *, inner_all,
):
    step = pl.program_id(0)
    chunk = pl.num_programs(0) - 1 - step
    heads = log_ref.shape[1]
    member = head_map(heads)

    @pl.when(step == 0)
    def _():
        held[...] = jnp.zeros_like(held)
        ggain_ref[...] = jnp.zeros_like(ggain_ref)
        gskip_ref[...] = jnp.zeros_like(gskip_ref)

    sums = jnp.transpose(jnp.concatenate([sums_ref[0]] * (CHUNK // PAD), axis=0))
    scale = lax.rsqrt(sums[:, 0:1] * (1.0 / inner_all) + eps)
    mean = sums[:, 1:2] * scale * (1.0 / inner_all)
    z = z_ref[...]
    y = y_ref[...]
    s = sigmoid(z)
    act = z * s
    gain = gain_ref[...]
    gg = gg_ref[...]
    unit = y * act * scale
    gn_ref[...] = (unit * gain).astype(bf16)
    ggain_ref[...] += jnp.sum(gg * unit, axis=0, keepdims=True)
    g_gated = scale * (gg * gain - unit * mean)
    gz_ref[...] = (g_gated * y * s * (1.0 + z * (1.0 - s))).astype(bf16)
    gy = g_gated * act
    gy_ref[...] = gy.astype(bf16)
    gskip_ref[...] += jnp.sum(gy * xa_ref[...].astype(f32), axis=0, keepdims=True)
    first, _ = seg_bounds(info_ref, chunk)
    into = jnp.exp(log_ref[...]) * flag(first < 0)
    weighted = (gy * spread(into, member)).astype(bf16)
    c_cols = jnp.transpose(bca_ref[:, STATE:].astype(f32)).astype(bf16)
    lloc_ref[...] = held[...].astype(bf16)[None]
    held[...] = spread_row(into[CHUNK - 1 : CHUNK, :], member) * held[...] + nn(c_cols, weighted)

    @pl.when(step == pl.num_programs(0) - 1)
    def _():
        send_ref[...] = held[...].astype(bf16)


def bwd_kernel(
    gy_ref, xa_ref, bca_ref, dt_ref, log_ref, dtr_ref, sent_ref, lloc_ref, lin_ref,
    ux_ref, ubc_ref, px_ref, pbc_ref, hx_ref, hbc_ref, cx_ref, cbc_ref, hp_ref, info_ref,
    gux_ref, gubc_ref, gdt_ref, tailx_ref, tailbc_ref, hgx_ref, hgbc_ref,
    gcx_ref, gcbc_ref, ghead_ref,
    ext, gext, dsuf, rows_scr, head_ext,
):
    step = pl.program_id(0)
    chunk = pl.num_programs(0) - 1 - step
    inner = gy_ref.shape[1]
    heads = log_ref.shape[1]
    member = head_map(heads)
    total_cols = inner + 2 * STATE

    @pl.when(step == 0)
    def _():
        dsuf[...] = jnp.ones_like(dsuf)
        gcx_ref[...] = jnp.zeros_like(gcx_ref)
        gcbc_ref[...] = jnp.zeros_like(gcbc_ref)
        ghead_ref[...] = jnp.zeros_like(ghead_ref)
        gext[CHUNK:, :] = jnp.zeros((PAD, total_cols), f32)

    @pl.when(step > 0)
    def _():
        gext[CHUNK:, :] = gext[0:PAD, :]

    first, last = seg_bounds(info_ref, chunk)
    logs = log_ref[...]
    logs_t = jnp.transpose(logs)
    dt = dt_ref[...]
    tail = logs[CHUNK - 1 : CHUNK, :]
    into = jnp.exp(logs) * flag(first < 0)
    out = jnp.exp(tail - logs) * flag(last >= CHUNK)
    decay = into[CHUNK - 1 : CHUNK, :]
    rate = jnp.exp(hp_ref[1:2, :])

    b = bca_ref[:, 0:STATE]
    c = bca_ref[:, STATE:]
    rows = lax.broadcasted_iota(jnp.int32, (CHUNK, CHUNK), 0)
    cols = lax.broadcasted_iota(jnp.int32, (CHUNK, CHUNK), 1)
    keep = (cols >= rows) & (cols < last)
    mixed = jnp.where(keep, nt(b, c), 0.0)

    lam = lloc_ref[0].astype(f32) + spread_row(dsuf[0:1, :], member) * lin_ref[...]
    lam_low = lam.astype(bf16)
    dsuf[...] = dsuf[...] * decay
    state = sent_ref[0]
    decay_sum = jnp.sum(lam * state.astype(f32), axis=0, keepdims=True) * spread_row(decay, member)
    z_head = per_head(jnp.broadcast_to(decay_sum, (PAD, inner)), member)[0:1]

    x = xa_ref[...].astype(f32)
    gy_low = gy_ref[...]
    gy = gy_low.astype(f32)
    dt_all = spread(dt, member)
    xd = x * dt_all
    out_all = spread(out, member)
    g_out = out_all * nn(b, lam_low)
    into_all = spread(into, member)
    e_head = per_head(xd * g_out, member)
    gy_in = gy * into_all
    f_head = per_head(gy_in * nn(c, state), member)
    g_c = nt(gy_in.astype(bf16), state)
    g_b = nt((xd * out_all).astype(bf16), lam_low)
    skip = spread_row(hp_ref[2:3, :], member)

    lane = lax.broadcasted_iota(jnp.int32, (1, 2 * HEAD_DIM), 1)
    left = flag(lane < HEAD_DIM).astype(bf16)
    right = flag(lane >= HEAD_DIM).astype(bf16)
    side = lax.broadcasted_iota(jnp.int32, (2 * CHUNK, CHUNK), 0) >> 7
    place = lax.broadcasted_iota(jnp.int32, (2 * CHUNK, CHUNK), 1)
    ones = jnp.ones((PAD, CHUNK), bf16)
    mixed2 = jnp.concatenate([mixed, mixed], axis=1)
    d_mixed = jnp.zeros((CHUNK, CHUNK), f32)
    k_sum = jnp.zeros((CHUNK, CHUNK), f32)
    t_head = jnp.zeros((CHUNK, heads), f32)
    for pair in range(heads // 2):
        at = slice(2 * pair * HEAD_DIM, 2 * (pair + 1) * HEAD_DIM)
        gyp = gy_low[:, at]
        block = jnp.concatenate([gyp * left, gyp * right], axis=0)
        d_m = nt(xd[:, at].astype(bf16), block)
        gaps = [logs_t[h : h + 1, :] - logs[:, h : h + 1] for h in (2 * pair, 2 * pair + 1)]
        decays = jnp.exp(jnp.minimum(jnp.concatenate(gaps, axis=1), 0.0))
        w = d_m * decays
        d_mixed = d_mixed + w[:, 0:CHUNK] + w[:, CHUNK:]
        g = (w * mixed2).astype(bf16)
        g_in = nn((decays * mixed2).astype(bf16), block)
        select = jnp.where(place == 2 * pair + side, 1.0, 0.0).astype(bf16)
        k_sum = k_sum + nn(g, select)
        r_pair = nn(ones, g)
        rows_scr[2 * pair : 2 * pair + 1, :] = r_pair[0:1, 0:CHUNK]
        rows_scr[2 * pair + 1 : 2 * pair + 2, :] = r_pair[0:1, CHUNK:]
        g_xd = g_in + g_out[:, at]
        gext[0:CHUNK, at] = dt_all[:, at] * g_xd + skip[:, at] * gy[:, at]
        t_head = t_head + per_head(x[:, at] * g_xd, member[:, at])
    d_mixed = jnp.where(keep, d_mixed, 0.0)
    g_b = g_b + nn(d_mixed.astype(bf16), c)
    g_c = g_c + nn(jnp.transpose(d_mixed).astype(bf16), b)
    gext[0:CHUNK, inner : inner + STATE] = g_b
    gext[0:CHUNK, inner + STATE :] = g_c

    r_head = jnp.transpose(rows_scr[...])[:, 0:heads]
    g_log = r_head - k_sum[:, 0:heads] + f_head
    g_a = exact(triangle(False, True), g_log) + exact(triangle(True, False), e_head) + z_head
    g_dt = (t_head - rate * g_a) * sigmoid(dtr_ref[...] + hp_ref[0:1, :])
    gdt_ref[...] = g_dt.astype(bf16)
    ghead_ref[0:1, :] += jnp.sum(g_dt, axis=0, keepdims=True)
    ghead_ref[1:2, :] += -rate * jnp.sum(dt * g_a, axis=0, keepdims=True)

    start = chunk == 0
    ext[0:PAD, 0:inner] = jnp.where(start, hx_ref[...].astype(f32), px_ref[...].astype(f32))[
        HALO - PAD : HALO
    ]
    ext[0:PAD, inner:] = jnp.where(start, hbc_ref[...].astype(f32), pbc_ref[...].astype(f32))[
        HALO - PAD : HALO
    ]
    ext[PAD:, 0:inner] = ux_ref[...].astype(f32)
    ext[PAD:, inner:] = ubc_ref[...].astype(f32)
    wide = 256
    ids = row_ids()
    masks = [None] + [
        jnp.broadcast_to(flag(ids - back >= first), (CHUNK, wide)) for back in range(1, WIDTH)
    ]
    ahead = [None] + [
        jnp.broadcast_to(flag(ids + back < last), (CHUNK, wide)) for back in range(1, WIDTH)
    ]
    for lo in range(0, total_cols, wide):
        on_x = lo < inner
        w_ref, base = (cx_ref, 0) if on_x else (cbc_ref, inner)
        gc_ref, gu_ref = (gcx_ref, gux_ref) if on_x else (gcbc_ref, gubc_ref)
        tail_ref, hg_ref = (tailx_ref, hgx_ref) if on_x else (tailbc_ref, hgbc_ref)
        here = slice(lo, lo + wide)
        taps = slice(lo - base, lo - base + wide)
        pre = conv_pre(ext, w_ref, masks, base, lo - base, wide)
        s = sigmoid(pre)
        g_pre = gext[0:CHUNK, here] * s * (1.0 + pre * (1.0 - s))
        gext[0:CHUNK, here] = g_pre
        gc_ref[WIDTH : WIDTH + 1, taps] += jnp.sum(g_pre, axis=0, keepdims=True)
        gc_ref[WIDTH - 1 : WIDTH, taps] += jnp.sum(
            g_pre * ext[PAD : PAD + CHUNK, here], axis=0, keepdims=True
        )
        g_u = w_ref[WIDTH - 1 : WIDTH, taps] * g_pre
        for back in range(1, WIDTH):
            tap = WIDTH - 1 - back
            masked = g_pre * masks[back]
            gc_ref[tap : tap + 1, taps] += jnp.sum(
                masked * ext[PAD - back : PAD - back + CHUNK, here], axis=0, keepdims=True
            )
            g_u = g_u + w_ref[tap : tap + 1, taps] * (
                gext[back : back + CHUNK, here] * ahead[back]
            )
        gu_ref[:, taps] = g_u.astype(bf16)

        @pl.when(step == 0)
        def _(g_u=g_u, tail_ref=tail_ref, taps=taps):
            tail_ref[:, taps] = g_u[CHUNK - HALO :, :]

        @pl.when(start)
        def _(g_pre=g_pre, hg_ref=hg_ref, taps=taps, w_ref=w_ref):
            halo = jnp.zeros((PAD, wide), f32)
            head_ext[0:PAD, :] = jnp.zeros((PAD, wide), f32)
            for back in range(1, WIDTH):
                tap = WIDTH - 1 - back
                head_ext[PAD:, :] = g_pre[0:PAD, :] * masks[back][0:PAD, :]
                halo = halo + w_ref[tap : tap + 1, taps] * head_ext[back : back + PAD, :]
            hg_ref[0:PAD, taps] = jnp.zeros((PAD, wide), f32)
            hg_ref[PAD:, taps] = halo


def along(value, axis, distance):
    count = lax.axis_size(axis)
    route = [(i, i + distance) for i in range(count) if 0 <= i + distance < count]
    return lax.ppermute(value, axis, route)


def swapped(value, axis, bit):
    return lax.ppermute(value, axis, [(i, i ^ bit) for i in range(lax.axis_size(axis))])


def all_sum(value, axis):
    bit = 1
    while bit < lax.axis_size(axis):
        value = value + swapped(value, axis, bit)
        bit *= 2
    return value


def gather_columns(value, axis):
    count = lax.axis_size(axis)
    me = lax.axis_index(axis)
    wide = value.shape[1]
    whole = jnp.zeros((value.shape[0], count * wide), value.dtype)
    bit = count // 2
    held = [(0, value)]
    while bit:
        held = held + [(mask ^ bit, swapped(part, axis, bit)) for mask, part in held]
        bit //= 2
    for mask, part in held:
        whole = lax.dynamic_update_slice_in_dim(whole, part, (me ^ mask) * wide, 1)
    return whole


def scatter_columns(value, axis):
    count = lax.axis_size(axis)
    me = lax.axis_index(axis)
    wide = value.shape[1] // count
    parts = {
        mask: lax.dynamic_slice_in_dim(value, (me ^ mask) * wide, wide, 1) for mask in range(count)
    }
    bit = 1
    while bit < count:
        kept = {}
        for mask in parts:
            if not mask & bit:
                other = swapped(parts[mask | bit].astype(bf16), axis, bit)
                kept[mask] = parts[mask].astype(f32) + other.astype(f32)
        parts = kept
        bit *= 2
    return parts[0]


def ring_order(count):
    return list(range(0, count, 2)) + list(range(count - 1, 0, -2))


def ring_scatter(value, axis):
    count = lax.axis_size(axis)
    rows = value.shape[0] // count
    half = value.shape[1] // 2
    order = ring_order(count)
    spot = [order.index(i) for i in range(count)]
    me = lax.axis_index(axis)
    my_spot = jnp.asarray(spot, jnp.int32)[me]
    table = jnp.asarray(order, jnp.int32)
    outs = []
    for sign, cols in ((1, slice(0, half)), (-1, slice(half, value.shape[1]))):
        route = [(order[i], order[(i + sign) % count]) for i in range(count)]
        moving = None
        for hop in range(count):
            owner = table[(my_spot + sign * (count - 1 - hop) + 2 * count) % count]
            mine = lax.dynamic_slice_in_dim(value[:, cols], owner * rows, rows, 0)
            if moving is None:
                moving = mine
            else:
                moving = moving.astype(f32) + mine.astype(f32)
                if hop < count - 1:
                    moving = moving.astype(bf16)
            if hop < count - 1:
                moving = lax.ppermute(moving, axis, route)
        outs.append(moving)
    return jnp.concatenate(outs, axis=1)


def window_chain(sent, decay, axis, sign, reach):
    arrived = [along(sent, axis, sign * hop) for hop in range(1, reach + 1)]
    fades = [along(decay, axis, sign * hop) for hop in range(1, reach)]
    total = arrived[-1].astype(f32)
    for hop in range(reach - 2, -1, -1):
        total = arrived[hop].astype(f32) + fades[hop] * total
    return total


def call(kernel, grid, in_specs, out_specs, out_shape, scratch, flops, moved, **names):
    return pl.pallas_call(
        kernel,
        grid=grid,
        in_specs=in_specs,
        out_specs=out_specs,
        out_shape=out_shape,
        scratch_shapes=scratch,
        compiler_params=pltpu.CompilerParams(
            dimension_semantics=("arbitrary",), vmem_limit_bytes=vmem_limit
        ),
        cost_estimate=pl.CostEstimate(flops=flops, bytes_accessed=moved, transcendentals=0),
        **names,
    )


def per_device(
    x_in, norm_gain, w_zx, w_bc, w_dt, conv_x, conv_bc, head_params, gate_gain, w_out, lengths,
    grad_out,
):
    tokens, width = x_in.shape
    heads = head_params.shape[1]
    inner = gate_gain.shape[0]
    members = lax.axis_size("tensor")
    inner_all = inner * members
    chunks = tokens // CHUNK
    reach = min(-(-REACH // tokens), lax.axis_size("seq") - 1)
    device = lax.axis_index("seq")
    member = lax.axis_index("tensor")

    shape = jax.ShapeDtypeStruct
    rows = lambda wide: pl.BlockSpec((CHUNK, wide), lambda i: (i, 0))
    back = lambda wide: pl.BlockSpec((CHUNK, wide), lambda i: (chunks - 1 - i, 0))
    whole = lambda *dims: pl.BlockSpec(dims, lambda i: (0,) * len(dims))
    stack = lambda *dims: pl.BlockSpec((1,) + dims, lambda i: (i,) + (0,) * len(dims))
    stack_back = lambda *dims: pl.BlockSpec(
        (1,) + dims, lambda i: (chunks - 1 - i,) + (0,) * len(dims)
    )

    ends = jnp.cumsum(lengths)
    starts = ends - lengths
    places = device * tokens + jnp.arange(tokens, dtype=jnp.int32)[:, None]
    seg_first = jnp.max(jnp.where(starts[None, :] <= places, starts[None, :], 0), axis=1)
    seg_last = jnp.min(
        jnp.where(ends[None, :] > places, ends[None, :], jnp.iinfo(jnp.int32).max // 2), axis=1
    )
    info = jnp.stack([seg_first, seg_last], axis=1) - device * tokens

    cotangent = gather_columns(grad_out, "tensor")

    x_float = x_in.astype(f32)
    x_scale = lax.rsqrt(jnp.mean(x_float * x_float, axis=1, keepdims=True) + eps)
    unit = x_float * x_scale
    normed = (unit * norm_gain[None, :]).astype(bf16)
    w_z, w_x = w_zx[:, 0, :], w_zx[:, 1, :]
    u_x = jnp.dot(normed, w_x, preferred_element_type=f32).astype(bf16)
    u_bc = jnp.dot(normed, w_bc, preferred_element_type=f32).astype(bf16)
    dt_raw = jnp.dot(normed, w_dt, preferred_element_type=f32)
    halo_x = along(u_x[tokens - HALO :], "seq", 1)
    halo_bc = along(u_bc[tokens - HALO :], "seq", 1)
    gate_in = jnp.dot(normed, w_z, preferred_element_type=f32)

    acts_x, acts_bc, dt, logs, local_in, leaving = call(
        fwd_kernel, (chunks,),
        [rows(inner), rows(2 * STATE), whole(HALO, inner), whole(HALO, 2 * STATE),
         whole(WIDTH + 1, inner), whole(WIDTH + 1, 2 * STATE), rows(heads), whole(3, heads), rows(2)],
        [rows(inner), rows(2 * STATE), rows(heads), rows(heads), stack(STATE, inner),
         whole(STATE + 2 * PAD, inner)],
        [shape((tokens, inner), bf16), shape((tokens, 2 * STATE), bf16), shape((tokens, heads), f32),
         shape((tokens, heads), f32), shape((chunks, STATE, inner), bf16),
         shape((STATE + 2 * PAD, inner), bf16)],
        [pltpu.VMEM((CHUNK + PAD, inner + 2 * STATE), f32), pltpu.VMEM((STATE, inner), f32),
         pltpu.VMEM((PAD, inner), f32)],
        2 * tokens * inner * STATE, 8 * tokens * inner, name="conv_states",
    )(u_x, u_bc, halo_x, halo_bc, conv_x, conv_bc, dt_raw, head_params, info)

    fade = leaving[STATE:]
    arrived = [along(leaving, "seq", hop) for hop in range(1, reach + 1)]
    state_in = arrived[-1][:STATE].astype(f32)
    for hop in range(reach - 2, -1, -1):
        block = arrived[hop].astype(f32)
        state_in = block[:STATE] + (block[STATE : STATE + 1] + block[STATE + PAD : STATE + PAD + 1]) * state_in

    back_dims = (((1,), (1,)), ((), ()))
    weight_dims = (((0,), (0,)), ((), ()))
    grad_gate = lax.dot_general(cotangent, w_out, back_dims, preferred_element_type=f32)

    y_local = call(
        intra_kernel, (chunks,),
        [rows(inner), rows(2 * STATE), rows(heads), rows(heads), stack(STATE, inner),
         whole(3, heads), rows(2)],
        rows(inner), shape((tokens, inner), f32), [],
        4 * tokens * inner * STATE, 8 * tokens * inner, name="intra",
    )(acts_x, acts_bc, dt, logs, local_in, head_params, info)

    gain_row = gate_gain[None, :]
    mixed, entering, sums = call(
        gate_sums_kernel, (chunks,),
        [rows(inner), rows(2 * STATE), rows(heads), stack(STATE, inner), whole(STATE, inner),
         rows(inner), rows(inner), whole(1, inner), rows(2)],
        [rows(inner), stack(STATE, inner), stack(PAD, CHUNK)],
        [shape((tokens, inner), f32), shape((chunks, STATE, inner), bf16),
         shape((chunks, PAD, CHUNK), f32)],
        [pltpu.VMEM((PAD, heads), f32)],
        2 * tokens * inner * STATE, 20 * tokens * inner, name="gate_sums",
    )(y_local, acts_bc, logs, local_in, state_in, gate_in, grad_gate, gain_row, info)

    sums = all_sum(sums, "tensor")

    gate_normed, grad_gate_in, grad_mixed, grad_local, grad_leaving, grad_gain, grad_skip = call(
        partial(gate_back_kernel, inner_all=inner_all), (chunks,),
        [back(inner), back(inner), back(inner), stack_back(PAD, CHUNK), whole(1, inner),
         back(inner), back(2 * STATE), back(heads), back(2)],
        [back(inner), back(inner), back(inner), stack_back(STATE, inner), whole(STATE, inner),
         whole(1, inner), whole(1, inner)],
        [shape((tokens, inner), bf16), shape((tokens, inner), bf16), shape((tokens, inner), bf16),
         shape((chunks, STATE, inner), bf16), shape((STATE, inner), bf16), shape((1, inner), f32),
         shape((1, inner), f32)],
        [pltpu.VMEM((STATE, inner), f32)],
        2 * tokens * inner * STATE, 20 * tokens * inner, name="gate_back",
    )(mixed, gate_in, grad_gate, sums, gain_row, acts_x, acts_bc, logs, info)

    from_later = [along(grad_leaving, "seq", -hop) for hop in range(1, reach + 1)]
    fades = [along(fade, "seq", -hop) for hop in range(1, reach)]
    grad_in = from_later[-1].astype(f32)
    for hop in range(reach - 2, -1, -1):
        low = fades[hop].astype(f32)
        grad_in = from_later[hop].astype(f32) + (low[0:1] + low[PAD : PAD + 1]) * grad_in

    grad_w_out_t = lax.dot_general(
        cotangent, gate_normed, weight_dims, preferred_element_type=f32
    ).astype(bf16)
    grad_w_out_sum = lax.psum_scatter(grad_w_out_t, "seq", scatter_dimension=0, tiled=True)
    grad_z_here = lax.dot_general(
        normed, grad_gate_in, weight_dims, preferred_element_type=f32
    ).astype(bf16)
    grad_z_sum = ring_scatter(grad_z_here, "seq")
    branch = jnp.dot(gate_normed, w_out, preferred_element_type=f32).astype(bf16)
    branch_part = scatter_columns(branch, "tensor")
    slice_width = grad_out.shape[1]
    x_part = lax.dynamic_slice_in_dim(x_in, member * slice_width, slice_width, 1).astype(f32)
    block_out = (x_part + branch_part).astype(bf16)

    halo_before = lambda wide: pl.BlockSpec(
        (HALO, wide),
        lambda i: (jnp.maximum((chunks - 1 - i) * (CHUNK // HALO) - 1, 0), 0),
    )
    total_cols = inner + 2 * STATE
    (grad_ux, grad_ubc, grad_dt, tail_x, tail_bc, sent_x, sent_bc, grad_cx, grad_cbc, grad_heads) = call(
        bwd_kernel, (chunks,),
        [back(inner), back(inner), back(2 * STATE), back(heads), back(heads), back(heads),
         stack_back(STATE, inner), stack_back(STATE, inner), whole(STATE, inner),
         back(inner), back(2 * STATE), halo_before(inner), halo_before(2 * STATE),
         whole(HALO, inner), whole(HALO, 2 * STATE), whole(WIDTH + 1, inner),
         whole(WIDTH + 1, 2 * STATE), whole(3, heads), back(2)],
        [back(inner), back(2 * STATE), back(heads), whole(HALO, inner), whole(HALO, 2 * STATE),
         whole(HALO, inner), whole(HALO, 2 * STATE), whole(PAD, inner), whole(PAD, 2 * STATE),
         whole(PAD, heads)],
        [shape((tokens, inner), bf16), shape((tokens, 2 * STATE), bf16), shape((tokens, heads), bf16),
         shape((HALO, inner), f32), shape((HALO, 2 * STATE), f32), shape((HALO, inner), f32),
         shape((HALO, 2 * STATE), f32), shape((PAD, inner), f32), shape((PAD, 2 * STATE), f32),
         shape((PAD, heads), f32)],
        [pltpu.VMEM((CHUNK + PAD, total_cols), f32), pltpu.VMEM((CHUNK + PAD, total_cols), f32),
         pltpu.VMEM((PAD, heads), f32), pltpu.VMEM((CHUNK, CHUNK), f32),
         pltpu.VMEM((2 * PAD, 256), f32)],
        12 * tokens * inner * STATE, 20 * tokens * inner, name="scan_back",
    )(grad_mixed, acts_x, acts_bc, dt, logs, dt_raw, entering, grad_local, grad_in,
      u_x, u_bc, u_x, u_bc, halo_x, halo_bc, conv_x, conv_bc, head_params, info)

    tail_x = (tail_x + along(sent_x, "seq", -1)).astype(bf16)
    tail_bc = (tail_bc + along(sent_bc, "seq", -1)).astype(bf16)
    grad_ux = lax.dynamic_update_slice_in_dim(grad_ux, tail_x, tokens - HALO, 0)
    grad_ubc = lax.dynamic_update_slice_in_dim(grad_ubc, tail_bc, tokens - HALO, 0)

    spare = 128 - heads
    grad_bcdt = jnp.concatenate([grad_ubc, grad_dt, jnp.zeros((tokens, spare), bf16)], axis=1)
    grad_x_here = lax.dot_general(normed, grad_ux, weight_dims, preferred_element_type=f32).astype(bf16)
    grad_bcdt_here = lax.dot_general(
        normed, grad_bcdt, weight_dims, preferred_element_type=f32
    ).astype(bf16)
    grad_bcdt_sum = ring_scatter(
        jnp.concatenate([grad_bcdt_here, jnp.zeros((width, 128), bf16)], axis=1), "seq"
    )
    grad_x_sum = ring_scatter(grad_x_here, "seq")

    grad_normed_here = (
        lax.dot_general(grad_gate_in, w_z, back_dims, preferred_element_type=f32)
        + lax.dot_general(grad_ux, w_x, back_dims, preferred_element_type=f32)
        + lax.dot_general(grad_ubc, w_bc, back_dims, preferred_element_type=f32)
        + lax.dot_general(grad_dt, w_dt, back_dims, preferred_element_type=f32)
    )
    row_dots = all_sum(
        jnp.sum(grad_normed_here * unit * norm_gain[None, :], axis=1).reshape(tokens // 128, 128),
        "tensor",
    )
    gain_here = jnp.sum(grad_normed_here * unit, axis=0)
    grad_normed = scatter_columns(grad_normed_here.astype(bf16), "tensor")
    gain_part = lax.dynamic_slice_in_dim(norm_gain, member * slice_width, slice_width, 0)
    row_mean = row_dots.reshape(tokens, 1) * (1.0 / width)
    grad_x = x_scale * (grad_normed * gain_part[None, :] - x_part * x_scale * row_mean) + grad_out.astype(f32)

    shared = jnp.concatenate([grad_cbc[: WIDTH + 1].reshape(-1), gain_here]).reshape(-1, 128)
    shared = all_sum(shared, "tensor")
    heads_here = jnp.concatenate(
        [grad_heads[:2], jnp.sum(grad_skip.reshape(heads, HEAD_DIM), axis=1)[None, :]], axis=0
    )
    own = jnp.concatenate(
        [grad_cx[: WIDTH + 1].reshape(-1), grad_gain.reshape(-1), heads_here.reshape(-1),
         jnp.zeros((-3 * heads % 128,), f32)]
    ).reshape(-1, 128)
    small = all_sum(jnp.concatenate([shared, own], axis=0), "seq")
    shared, own = small[: shared.shape[0]].reshape(-1), small[shared.shape[0] :].reshape(-1)
    bc_size = (WIDTH + 1) * 2 * STATE
    x_size = (WIDTH + 1) * inner
    grad_conv_bc = shared[:bc_size].reshape(WIDTH + 1, 2 * STATE)
    grad_norm_gain = shared[bc_size:]
    grad_conv_x = own[:x_size].reshape(WIDTH + 1, inner)
    grad_gate_gain = own[x_size : x_size + inner]
    grad_head = own[x_size + inner : x_size + inner + 3 * heads].reshape(3, heads)

    bc_rows = all_sum_low(grad_bcdt_sum[:, : 2 * STATE], "tensor").astype(bf16)
    grad_w_bc = lax.all_gather(bc_rows, "seq", axis=0, tiled=True).astype(f32)
    grad_w_dt = grad_bcdt_sum[:, 2 * STATE : 2 * STATE + heads]
    grad_w_zx = jnp.stack([grad_z_sum, grad_x_sum], axis=1)
    grad_w_out = grad_w_out_sum.astype(f32).T
    return (
        block_out, grad_x, grad_norm_gain, grad_w_zx, grad_w_bc, grad_w_dt, grad_conv_x,
        grad_conv_bc, grad_head, grad_gate_gain, grad_w_out,
    )


def all_sum_low(value, axis):
    bit = 1
    while bit < lax.axis_size(axis):
        value = value + swapped(value.astype(bf16), axis, bit).astype(f32)
        bit *= 2
    return value


def solution(mesh):
    return jax.shard_map(
        per_device,
        mesh=mesh,
        in_specs=(
            P("seq", None), P(), P(None, None, "tensor"), P(), P(None, "tensor"),
            P(None, "tensor"), P(), P(None, "tensor"), P("tensor"), P("tensor", None), P(),
            P("seq", "tensor"),
        ),
        out_specs=(
            P("seq", "tensor"), P("seq", "tensor"), P(), P("seq", None, "tensor"), P(),
            P("seq", "tensor"), P(None, "tensor"), P(), P(None, "tensor"), P("tensor"),
            P("tensor", "seq"),
        ),
        check_vma=False,
    )
```

```python
from functools import partial

import jax
import jax.numpy as jnp
from jax import lax
from jax.experimental import pallas as pl
from jax.experimental.pallas import tpu as pltpu
from jax.sharding import PartitionSpec as P

HEAD_DIM = 64
STATE = 128
WIDTH = 4
CHUNK = 128
REACH = 4096
PAD = 8
HALO = 16

eps = 1e-05
f32 = jnp.float32
bf16 = jnp.bfloat16
vmem_limit = 56 * 1024 * 1024


def nn(a, b):
    return lax.dot_general(a, b, (((1,), (0,)), ((), ())), preferred_element_type=f32)


def nt(a, b):
    return lax.dot_general(a, b, (((1,), (1,)), ((), ())), preferred_element_type=f32)


def running(mask, v):
    wide = v.shape[1]
    high = v.astype(bf16)
    rest = v - high.astype(f32)
    mid = rest.astype(bf16)
    low = (rest - mid.astype(f32)).astype(bf16)
    out = nn(mask, jnp.concatenate([high, mid, low], axis=1))
    return out[:, 0:wide] + out[:, wide : 2 * wide] + out[:, 2 * wide : 3 * wide]


def head_map(heads):
    row = lax.broadcasted_iota(jnp.int32, (2 * heads, heads * HEAD_DIM), 0)
    col = lax.broadcasted_iota(jnp.int32, (2 * heads, heads * HEAD_DIM), 1)
    row = jnp.where(row >= heads, row - heads, row)
    return jnp.where((col >> 6) == row, 1.0, 0.0).astype(bf16)


def spread(v, member):
    high = v.astype(bf16)
    rest = (v - high.astype(f32)).astype(bf16)
    return nn(jnp.concatenate([high, rest], axis=1), member)


def spread_row(v, member):
    return spread(jnp.broadcast_to(v, (PAD, v.shape[1])), member)[0:1]


def per_head(v, member):
    return nt(v.astype(bf16), member[0 : member.shape[0] // 2])


def triangle(strict, upper):
    row = lax.broadcasted_iota(jnp.int32, (CHUNK, CHUNK), 0)
    col = lax.broadcasted_iota(jnp.int32, (CHUNK, CHUNK), 1)
    if upper:
        row, col = col, row
    keep = (row > col) if strict else (row >= col)
    return jnp.where(keep, 1.0, 0.0).astype(bf16)


def softplus(v):
    return jnp.maximum(v, 0.0) + jnp.log1p(jnp.exp(-jnp.abs(v)))


def sigmoid(v):
    return 1.0 / (1.0 + jnp.exp(-v))


def seg_bounds(info_ref, chunk):
    info = info_ref[...] - chunk * CHUNK
    return info[:, 0:1], info[:, 1:2]


def row_ids():
    return lax.broadcasted_iota(jnp.int32, (CHUNK, 1), 0)


def flag(v):
    return jnp.where(v, 1.0, 0.0).astype(f32)


def conv_pre(ext_ref, w_ref, masks, lo, wide):
    cols = taps = slice(lo, lo + wide)
    total = w_ref[WIDTH : WIDTH + 1, taps] + w_ref[WIDTH - 1 : WIDTH, taps] * ext_ref[
        PAD : PAD + CHUNK, cols
    ]
    for back in range(1, WIDTH):
        total = total + w_ref[WIDTH - 1 - back : WIDTH - back, taps] * (
            ext_ref[PAD - back : PAD - back + CHUNK, cols] * masks[back]
        )
    return total


def project_kernel(
    x_ref, gain_ref, wx_ref, wbc_ref, wdt_ref, normed_ref, scale_ref, u_ref, dtr_ref,
):
    x = x_ref[...].astype(f32)
    scale = lax.rsqrt(jnp.mean(x * x, axis=1, keepdims=True) + eps)
    normed = (x * scale * gain_ref[...]).astype(bf16)
    scale_ref[...] = scale
    normed_ref[...] = normed
    inner = wx_ref.shape[2]
    u_ref[:, 0:inner] = nn(normed, wx_ref[0]).astype(bf16)
    u_ref[:, inner:] = nn(normed, wbc_ref[...]).astype(bf16)
    dtr_ref[...] = nn(normed, wdt_ref[...])


def fwd_kernel(
    u_ref, halo_ref, cw_ref, dtr_ref, hp_ref, info_ref,
    acts_ref, dt_ref, log_ref, sloc_ref, send_ref,
    ext, held, drun,
):
    chunk = pl.program_id(0)
    heads = dtr_ref.shape[1]
    inner = heads * HEAD_DIM

    @pl.when(chunk == 0)
    def _():
        ext[0:PAD, :] = halo_ref[...].astype(f32)[HALO - PAD : HALO]
        held[...] = jnp.zeros_like(held)
        drun[...] = jnp.ones_like(drun)

    @pl.when(chunk > 0)
    def _():
        ext[0:PAD, :] = ext[CHUNK : CHUNK + PAD, :]

    ext[PAD:, :] = u_ref[...].astype(f32)
    first, last = seg_bounds(info_ref, chunk)
    rows = row_ids()
    wide = 256
    masks = [None] + [
        jnp.broadcast_to(flag(rows - back >= first), (CHUNK, wide)) for back in range(1, WIDTH)
    ]
    for lo in range(0, u_ref.shape[1], wide):
        pre = conv_pre(ext, cw_ref, masks, lo, wide)
        acts_ref[:, lo : lo + wide] = (pre * sigmoid(pre)).astype(bf16)

    member = head_map(heads)
    dt = softplus(dtr_ref[...] + hp_ref[0:1, :])
    rate = jnp.exp(hp_ref[1:2, :])
    logs = running(triangle(False, False), -dt * rate)
    dt_ref[...] = dt
    log_ref[...] = logs
    tail = logs[CHUNK - 1 : CHUNK, :]
    keep_in = flag(first < 0)
    keep_out = flag(last >= CHUNK)
    weight = jnp.exp(tail - logs) * keep_out * dt
    decay = jnp.exp(tail) * keep_in[CHUNK - 1 : CHUNK, :]
    x_in = (acts_ref[:, 0:inner].astype(f32) * spread(weight, member)).astype(bf16)
    b_cols = jnp.transpose(acts_ref[:, inner : inner + STATE].astype(f32)).astype(bf16)
    local = nn(b_cols, x_in)
    decay_all = spread_row(decay, member)
    sloc_ref[...] = held[...].astype(bf16)[None]
    held[...] = decay_all * held[...] + local
    drun[...] = drun[...] * decay_all

    @pl.when(chunk == pl.num_programs(0) - 1)
    def _():
        total = drun[...]
        high = total.astype(bf16)
        send_ref[0:STATE, :] = held[...].astype(bf16)
        send_ref[STATE:, :] = jnp.concatenate(
            [total, total - high.astype(f32)], axis=0
        ).astype(bf16)


def intra_kernel(acts_ref, dt_ref, log_ref, sloc_ref, hp_ref, info_ref, y_ref):
    chunk = pl.program_id(0)
    heads = dt_ref.shape[1]
    inner = heads * HEAD_DIM
    member = head_map(heads)
    first, _ = seg_bounds(info_ref, chunk)
    rows = lax.broadcasted_iota(jnp.int32, (CHUNK, CHUNK), 0)
    cols = lax.broadcasted_iota(jnp.int32, (CHUNK, CHUNK), 1)
    b = acts_ref[:, inner : inner + STATE]
    c = acts_ref[:, inner + STATE :]
    mixed = jnp.where((cols <= rows) & (cols >= first), nt(c, b), 0.0)
    logs = log_ref[...]
    keep_in = flag(first < 0)
    logs_t = jnp.transpose(logs)
    x = acts_ref[:, 0:inner].astype(f32)
    xd = x * spread(dt_ref[...], member)
    skip = spread_row(hp_ref[2:3, :], member)
    carried = spread(jnp.exp(logs) * keep_in, member) * nn(c, sloc_ref[0]) + skip * x
    lane = lax.broadcasted_iota(jnp.int32, (1, 2 * HEAD_DIM), 1)
    left = flag(lane < HEAD_DIM)
    right = 1.0 - left
    for pair in range(heads // 2):
        mats = []
        for h in (2 * pair, 2 * pair + 1):
            gap = logs[:, h : h + 1] - logs_t[h : h + 1, :]
            mats.append((jnp.exp(jnp.minimum(gap, 0.0)) * mixed).astype(bf16))
        at = slice(2 * pair * HEAD_DIM, 2 * (pair + 1) * HEAD_DIM)
        xp = xd[:, at]
        block = jnp.concatenate([(xp * left).astype(bf16), (xp * right).astype(bf16)], axis=0)
        y_ref[:, at] = carried[:, at] + nn(jnp.concatenate(mats, axis=1), block)


def gate_sums_kernel(
    yl_ref, c_ref, log_ref, sloc_ref, sin_ref, z_ref, gg_ref, gain_ref, info_ref,
    y_ref, sent_ref, sums_ref,
    dpre,
):
    chunk = pl.program_id(0)
    heads = log_ref.shape[1]
    member = head_map(heads)

    @pl.when(chunk == 0)
    def _():
        dpre[...] = jnp.ones_like(dpre)

    first, _ = seg_bounds(info_ref, chunk)
    keep_in = flag(first < 0)
    before = dpre[0:1, :]
    gate = jnp.exp(log_ref[...]) * keep_in
    state = sin_ref[...]
    sent_ref[...] = (sloc_ref[0].astype(f32) + spread_row(before, member) * state).astype(bf16)[None]
    carried = spread(gate * before, member) * nn(c_ref[...], state.astype(bf16))
    y = yl_ref[...] + carried
    y_ref[...] = y
    z = z_ref[...].astype(f32)
    gated = y * z * sigmoid(z)
    squares = jnp.sum(gated * gated, axis=1, keepdims=True)
    dots = jnp.sum(gated * gg_ref[...].astype(f32) * gain_ref[...], axis=1, keepdims=True)
    lane = lax.broadcasted_iota(jnp.int32, (CHUNK, STATE), 1)
    both = jnp.where(lane == 0, squares, jnp.where(lane == 1, dots, 0.0))
    sums_ref[...] = jnp.transpose(both)[0:PAD][None]
    dpre[...] = dpre[...] * gate[CHUNK - 1 : CHUNK, :]


def gate_back_kernel(
    y_ref, z_ref, gg_ref, sums_ref, gain_ref, xa_ref, c_ref, log_ref, info_ref, fade_ref,
    gn_ref, gz_ref, gy_ref, lloc_ref, send_ref, ggain_ref, gskip_ref,
    held, *, inner_all,
):
    step = pl.program_id(0)
    chunk = pl.num_programs(0) - 1 - step
    heads = log_ref.shape[1]
    member = head_map(heads)

    @pl.when(step == 0)
    def _():
        held[...] = jnp.zeros_like(held)
        ggain_ref[...] = jnp.zeros_like(ggain_ref)
        gskip_ref[...] = jnp.zeros_like(gskip_ref)

    sums = jnp.transpose(jnp.concatenate([sums_ref[0]] * (CHUNK // PAD), axis=0))
    scale = lax.rsqrt(sums[:, 0:1] * (1.0 / inner_all) + eps)
    mean = sums[:, 1:2] * scale * (1.0 / inner_all)
    z = z_ref[...].astype(f32)
    y = y_ref[...]
    s = sigmoid(z)
    act = z * s
    gain = gain_ref[...]
    gg = gg_ref[...].astype(f32)
    unit = y * act * scale
    gn_ref[...] = (unit * gain).astype(bf16)
    ggain_ref[...] += jnp.sum(gg * unit, axis=0, keepdims=True)
    g_gated = scale * (gg * gain - unit * mean)
    gz_ref[...] = (g_gated * y * s * (1.0 + z * (1.0 - s))).astype(bf16)
    gy = g_gated * act
    gy_ref[...] = gy.astype(bf16)
    gskip_ref[...] += jnp.sum(gy * xa_ref[...].astype(f32), axis=0, keepdims=True)
    first, _ = seg_bounds(info_ref, chunk)
    into = jnp.exp(log_ref[...]) * flag(first < 0)
    weighted = (gy * spread(into, member)).astype(bf16)
    c_cols = jnp.transpose(c_ref[...].astype(f32)).astype(bf16)
    lloc_ref[...] = held[...].astype(bf16)[None]
    held[...] = spread_row(into[CHUNK - 1 : CHUNK, :], member) * held[...] + nn(c_cols, weighted)

    @pl.when(step == pl.num_programs(0) - 1)
    def _():
        send_ref[0:STATE, :] = held[...].astype(bf16)
        send_ref[STATE:, :] = fade_ref[...]


def bwd_kernel(*refs, top, aliased):
    (
        gy_ref, acts_ref, dt_ref, log_ref, dtr_ref, sent_ref, lloc_ref, lin_ref,
        u_ref, prev_ref, halo_ref, cw_ref, hp_ref, info_ref,
        dsuf_in, gext_in, gc_in, ghead_in,
    ) = refs[:18]
    (
        gu_ref, gdt_ref, tail_ref, hg_ref, dsuf, gext_out, gc_ref, ghead_ref,
        ext, gext, rows_scr, head_ext, xg_scr,
    ) = refs[18 + aliased :]
    step = pl.program_id(0)
    chunk = top - 1 - step
    inner = gy_ref.shape[1]
    heads = log_ref.shape[1]
    member = head_map(heads)
    total_cols = inner + 2 * STATE

    @pl.when(step == 0)
    def _():
        dsuf[...] = dsuf_in[...]
        gc_ref[...] = gc_in[...]
        ghead_ref[...] = ghead_in[...]
        gext[CHUNK:, :] = gext_in[...]

    @pl.when(step > 0)
    def _():
        gext[CHUNK:, :] = gext[0:PAD, :]

    first, last = seg_bounds(info_ref, chunk)
    logs = log_ref[...]
    logs_t = jnp.transpose(logs)
    dt = dt_ref[...]
    tail = logs[CHUNK - 1 : CHUNK, :]
    into = jnp.exp(logs) * flag(first < 0)
    out = jnp.exp(tail - logs) * flag(last >= CHUNK)
    decay = into[CHUNK - 1 : CHUNK, :]
    rate = jnp.exp(hp_ref[1:2, :])

    b = acts_ref[:, inner : inner + STATE]
    c = acts_ref[:, inner + STATE :]
    rows = lax.broadcasted_iota(jnp.int32, (CHUNK, CHUNK), 0)
    cols = lax.broadcasted_iota(jnp.int32, (CHUNK, CHUNK), 1)
    keep = (cols >= rows) & (cols < last)
    mixed = jnp.where(keep, nt(b, c), 0.0)

    lam = lloc_ref[0].astype(f32) + spread_row(dsuf[0:1, :], member) * lin_ref[...]
    lam_low = lam.astype(bf16)
    dsuf[...] = dsuf[...] * decay
    state = sent_ref[0]
    decay_sum = jnp.sum(lam * state.astype(f32), axis=0, keepdims=True) * spread_row(decay, member)
    z_head = per_head(jnp.broadcast_to(decay_sum, (PAD, inner)), member)[0:1]

    x = acts_ref[:, 0:inner].astype(f32)
    gy_low = gy_ref[...]
    gy = gy_low.astype(f32)
    dt_all = spread(dt, member)
    xd = x * dt_all
    out_all = spread(out, member)
    g_out = out_all * nn(b, lam_low)
    into_all = spread(into, member)
    e_head = per_head(xd * g_out, member)
    gy_in = gy * into_all
    f_head = per_head(gy_in * nn(c, state), member)
    g_c = nt(gy_in.astype(bf16), state)
    g_b = nt((xd * out_all).astype(bf16), lam_low)
    skip = spread_row(hp_ref[2:3, :], member)

    lane = lax.broadcasted_iota(jnp.int32, (1, 2 * HEAD_DIM), 1)
    left = flag(lane < HEAD_DIM).astype(bf16)
    right = flag(lane >= HEAD_DIM).astype(bf16)
    side = lax.broadcasted_iota(jnp.int32, (2 * CHUNK, CHUNK), 0) >> 7
    place = lax.broadcasted_iota(jnp.int32, (2 * CHUNK, CHUNK), 1)
    ones = jnp.ones((PAD, CHUNK), bf16)
    mixed2 = jnp.concatenate([mixed, mixed], axis=1)
    d_mixed = jnp.zeros((CHUNK, CHUNK), f32)
    k_sum = jnp.zeros((CHUNK, CHUNK), f32)
    for pair in range(heads // 2):
        at = slice(2 * pair * HEAD_DIM, 2 * (pair + 1) * HEAD_DIM)
        gyp = gy_low[:, at]
        block = jnp.concatenate([gyp * left, gyp * right], axis=0)
        d_m = nt(xd[:, at].astype(bf16), block)
        gaps = [logs_t[h : h + 1, :] - logs[:, h : h + 1] for h in (2 * pair, 2 * pair + 1)]
        decays = jnp.exp(jnp.minimum(jnp.concatenate(gaps, axis=1), 0.0))
        w = d_m * decays
        d_mixed = d_mixed + w[:, 0:CHUNK] + w[:, CHUNK:]
        g = (w * mixed2).astype(bf16)
        g_in = nn((decays * mixed2).astype(bf16), block)
        select = jnp.where(place == 2 * pair + side, 1.0, 0.0).astype(bf16)
        k_sum = k_sum + nn(g, select)
        r_pair = nn(ones, g)
        rows_scr[2 * pair : 2 * pair + 1, :] = r_pair[0:1, 0:CHUNK]
        rows_scr[2 * pair + 1 : 2 * pair + 2, :] = r_pair[0:1, CHUNK:]
        g_xd = g_in + g_out[:, at]
        gext[0:CHUNK, at] = dt_all[:, at] * g_xd + skip[:, at] * gy[:, at]
        xg_scr[:, at] = (x[:, at] * g_xd).astype(bf16)
    d_mixed = jnp.where(keep, d_mixed, 0.0)
    g_b = g_b + nn(d_mixed.astype(bf16), c)
    g_c = g_c + nn(jnp.transpose(d_mixed).astype(bf16), b)
    gext[0:CHUNK, inner : inner + STATE] = g_b
    gext[0:CHUNK, inner + STATE :] = g_c

    t_head = per_head(xg_scr[...], member)
    r_head = jnp.transpose(rows_scr[...])[:, 0:heads]
    g_log = r_head - k_sum[:, 0:heads] + f_head
    g_a = running(triangle(False, True), g_log) + running(triangle(True, False), e_head) + z_head
    g_dt = (t_head - rate * g_a) * sigmoid(dtr_ref[...] + hp_ref[0:1, :])
    gdt_ref[...] = g_dt.astype(bf16)
    ghead_ref[0:1, :] += jnp.sum(g_dt, axis=0, keepdims=True)
    ghead_ref[1:2, :] += -rate * jnp.sum(dt * g_a, axis=0, keepdims=True)

    start = chunk == 0
    ext[0:PAD, :] = jnp.where(start, halo_ref[...].astype(f32), prev_ref[...].astype(f32))[
        HALO - PAD : HALO
    ]
    ext[PAD:, :] = u_ref[...].astype(f32)
    wide = 256
    ids = row_ids()
    masks = [None] + [
        jnp.broadcast_to(flag(ids - back >= first), (CHUNK, wide)) for back in range(1, WIDTH)
    ]
    ahead = [None] + [
        jnp.broadcast_to(flag(ids + back < last), (CHUNK, wide)) for back in range(1, WIDTH)
    ]
    for lo in range(0, total_cols, wide):
        here = taps = slice(lo, lo + wide)
        w_ref = cw_ref
        pre = conv_pre(ext, w_ref, masks, lo, wide)
        s = sigmoid(pre)
        g_pre = gext[0:CHUNK, here] * s * (1.0 + pre * (1.0 - s))
        gext[0:CHUNK, here] = g_pre
        gc_ref[WIDTH : WIDTH + 1, taps] += jnp.sum(g_pre, axis=0, keepdims=True)
        gc_ref[WIDTH - 1 : WIDTH, taps] += jnp.sum(
            g_pre * ext[PAD : PAD + CHUNK, here], axis=0, keepdims=True
        )
        g_u = w_ref[WIDTH - 1 : WIDTH, taps] * g_pre
        for back in range(1, WIDTH):
            tap = WIDTH - 1 - back
            masked = g_pre * masks[back]
            gc_ref[tap : tap + 1, taps] += jnp.sum(
                masked * ext[PAD - back : PAD - back + CHUNK, here], axis=0, keepdims=True
            )
            g_u = g_u + w_ref[tap : tap + 1, taps] * (
                gext[back : back + CHUNK, here] * ahead[back]
            )
        gu_ref[:, taps] = g_u.astype(bf16)

        @pl.when(step == 0)
        def _(g_u=g_u, taps=taps):
            tail_ref[:, taps] = g_u[CHUNK - HALO :, :]

        @pl.when(start)
        def _(g_pre=g_pre, taps=taps):
            halo = jnp.zeros((PAD, wide), f32)
            head_ext[0:PAD, :] = jnp.zeros((PAD, wide), f32)
            for back in range(1, WIDTH):
                tap = WIDTH - 1 - back
                head_ext[PAD:, :] = g_pre[0:PAD, :] * masks[back][0:PAD, :]
                halo = halo + w_ref[tap : tap + 1, taps] * head_ext[back : back + PAD, :]
            hg_ref[0:PAD, taps] = jnp.zeros((PAD, wide), f32)
            hg_ref[PAD:, taps] = halo

    gext_out[...] = gext[0:PAD, :]


def put_halves(out_ref, value, parity, blocks):
    wide = value.shape[1] // blocks
    halves = [
        jnp.concatenate([value[:, i * wide : (i + 1) * wide] for i in range(odd, blocks, 2)], axis=1)
        for odd in range(2)
    ]

    @pl.when(parity == 0)
    def _():
        out_ref[0] = halves[0]
        out_ref[1] = halves[1]

    @pl.when(parity == 1)
    def _():
        out_ref[0] = halves[1]
        out_ref[1] = halves[0]


def branch_kernel(parity_ref, gn_ref, w_ref, out_ref, *, blocks):
    put_halves(out_ref, nn(gn_ref[...], w_ref[...]).astype(bf16), parity_ref[0], blocks)


def normed_back_kernel(
    parity_ref, gu_ref, gdt_ref, gz_ref, x_ref, scale_ref, gain_ref, wx_ref, wbc_ref, wdt_ref,
    out_ref, dots_ref, ggain_ref, *, blocks,
):
    inner = wx_ref.shape[2]

    @pl.when(pl.program_id(0) == 0)
    def _():
        ggain_ref[...] = jnp.zeros_like(ggain_ref)

    total = gz_ref[...].astype(f32) + nt(gu_ref[:, 0:inner], wx_ref[0])
    total = total + nt(gu_ref[:, inner:], wbc_ref[...]) + nt(gdt_ref[...], wdt_ref[...])
    unit = x_ref[...].astype(f32) * scale_ref[...]
    with_unit = total * unit
    ggain_ref[...] += jnp.sum(with_unit, axis=0, keepdims=True)
    dots = jnp.sum(with_unit * gain_ref[...], axis=1, keepdims=True)
    dots_ref[...] = jnp.transpose(jnp.broadcast_to(dots, (dots.shape[0], 128)))[0:PAD][None]
    put_halves(out_ref, total.astype(bf16), parity_ref[0], blocks)


def along(value, axis, distance):
    count = lax.axis_size(axis)
    route = [(i, i + distance) for i in range(count) if 0 <= i + distance < count]
    return lax.ppermute(value, axis, route)


def swapped(value, axis, bit):
    return lax.ppermute(value, axis, [(i, i ^ bit) for i in range(lax.axis_size(axis))])


def all_sum(value, axis):
    bit = 1
    while bit < lax.axis_size(axis):
        value = value + swapped(value, axis, bit)
        bit *= 2
    return value


def sum_pairs(value, axis):
    parts = [swapped(value, axis, mask) for mask in range(1, lax.axis_size(axis))]
    return value + sum(parts[1:], parts[0])


def summed(blocks):
    total = blocks[0].astype(f32)
    for block in blocks[1:]:
        total = total + block.astype(f32)
    return total


def halves_of(parts, axis, bit):
    upper = (lax.axis_index(axis) & bit) != 0
    kept = [jnp.where(upper, b, a) for a, b in zip(parts[0::2], parts[1::2])]
    given = [jnp.where(upper, a, b) for a, b in zip(parts[0::2], parts[1::2])]
    return kept, given


class Last:

    def __init__(self, kept, arrived, axis, pieces):
        parts = jnp.split(kept.astype(f32) + arrived.astype(f32), lax.axis_size(axis) // 2, axis=1)
        bit = 2
        while True:
            keep, give = halves_of(parts, axis, bit)
            give = jnp.concatenate(give, axis=1).astype(bf16)
            if 2 * bit >= lax.axis_size(axis):
                break
            other = jnp.split(swapped(give, axis, bit), len(keep), axis=1)
            parts = [k + o.astype(f32) for k, o in zip(keep, other)]
            bit *= 2
        self.axis, self.bit, self.keep = axis, bit, keep[0]
        rows = give.shape[0] // pieces
        self.give = [give[i * rows : (i + 1) * rows] for i in range(pieces)]

    def send(self, piece):
        return swapped(self.give[piece], self.axis, self.bit)

    def total(self, arrived):
        return self.keep + jnp.concatenate(arrived, axis=0).astype(f32)


def ring_order(count):
    return list(range(0, count, 2)) + list(range(count - 1, 0, -2))


def dealt(value, axis):
    return lax.all_to_all(value, axis, 0, 0, tiled=True)


def repeated(value, count):
    return jnp.broadcast_to(value[None], (count,) + value.shape)


def grouped_send(value, axis):
    count = lax.axis_size(axis) // 2
    me = lax.axis_index(axis) >> 1
    rows = value.shape[0] // count
    own = lax.dynamic_slice_in_dim(value, me * rows, rows, 0)
    return [own] + [
        swapped(lax.dynamic_slice_in_dim(value, (me ^ mask) * rows, rows, 0), axis, 2 * mask)
        for mask in range(1, count)
    ]


class Ring:

    def __init__(self, values, axis):
        count = lax.axis_size(axis)
        self.values, self.axis, self.count, self.hop = values, axis, count, 0
        self.order = ring_order(count)
        me = lax.axis_index(axis)
        self.spot = jnp.where(me % 2 == 0, me // 2, count - (me + 1) // 2)
        self.moving = self.mine()

    def signs(self):
        return [1 - 2 * (i % 2) for i in range(len(self.values))]

    def mine(self):
        blocks = []
        for value, sign in zip(self.values, self.signs()):
            rows = value.shape[0] // self.count
            ahead = sign * (self.count - 1 - self.hop)
            spot = (self.spot + ahead + 2 * self.count) % self.count
            owner = jnp.where(spot < self.count // 2, 2 * spot, 2 * (self.count - spot) - 1)
            blocks.append(lax.dynamic_slice_in_dim(value, owner * rows, rows, 0))
        return blocks

    def send(self):
        arrived = []
        for block, sign in zip(self.moving, self.signs()):
            route = [
                (self.order[i], self.order[(i + sign) % self.count]) for i in range(self.count)
            ]
            arrived.append(lax.ppermute(block, self.axis, route))
        return arrived

    def add(self, arrived):
        self.hop += 1
        blocks = [a.astype(f32) + b.astype(f32) for a, b in zip(arrived, self.mine())]
        done = self.hop == self.count - 1
        self.moving = blocks if done else [block.astype(bf16) for block in blocks]
        return done


def scatter_direct(value, axis):
    count = lax.axis_size(axis)
    me = lax.axis_index(axis)
    wide = value.shape[1] // count
    own = lax.dynamic_slice_in_dim(value, me * wide, wide, 1)
    return summed([own] + [
        swapped(lax.dynamic_slice_in_dim(value, (me ^ mask) * wide, wide, 1), axis, mask)
        for mask in range(1, count)
    ])


def gather_direct(value, axis):
    count = lax.axis_size(axis)
    me = lax.axis_index(axis)
    whole = jnp.stack([value] + [swapped(value, axis, mask) for mask in range(1, count)])
    return jnp.take(whole, jnp.arange(count) ^ me, axis=0)


def all_sum_low(value, axis):
    bit = 1
    while bit < lax.axis_size(axis):
        value = value + swapped(value.astype(bf16), axis, bit).astype(f32)
        bit *= 2
    return value


def call(kernel, grid, in_specs, out_specs, out_shape, scratch, micros, **names):
    return pl.pallas_call(
        kernel,
        grid=grid,
        in_specs=in_specs,
        out_specs=out_specs,
        out_shape=out_shape,
        scratch_shapes=scratch,
        compiler_params=pltpu.CompilerParams(
            dimension_semantics=("arbitrary",), vmem_limit_bytes=vmem_limit
        ),
        cost_estimate=pl.CostEstimate(
            flops=micros * 10**9, bytes_accessed=micros * 10**6, transcendentals=0
        ),
        **names,
    )


def together(*values):
    return lax.optimization_barrier(values)


def per_device(
    x_in, norm_gain, w_zx, w_bc, w_dt, conv_x, conv_bc, head_params, gate_gain, w_out, lengths,
    grad_out,
):
    tokens, width = x_in.shape
    heads = head_params.shape[1]
    inner = gate_gain.shape[0]
    members = lax.axis_size("tensor")
    devices = lax.axis_size("seq")
    inner_all = inner * members
    total_cols = inner + 2 * STATE
    chunks = tokens // CHUNK
    reach = min(-(-REACH // tokens), devices - 1)
    device = lax.axis_index("seq")
    member = lax.axis_index("tensor")

    shape = jax.ShapeDtypeStruct
    rows = lambda wide: pl.BlockSpec((CHUNK, wide), lambda i: (i, 0))
    back = lambda wide: pl.BlockSpec((CHUNK, wide), lambda i: (chunks - 1 - i, 0))
    whole = lambda *dims: pl.BlockSpec(dims, lambda i: (0,) * len(dims))
    stack = lambda *dims: pl.BlockSpec((1,) + dims, lambda i: (i,) + (0,) * len(dims))
    stack_back = lambda *dims: pl.BlockSpec(
        (1,) + dims, lambda i: (chunks - 1 - i,) + (0,) * len(dims)
    )
    c_at = inner // STATE + 1
    c_rows = pl.BlockSpec((CHUNK, STATE), lambda i: (i, c_at))
    c_back = pl.BlockSpec((CHUNK, STATE), lambda i: (chunks - 1 - i, c_at))

    ends = jnp.cumsum(lengths)
    starts = ends - lengths
    places = device * tokens + jnp.arange(tokens, dtype=jnp.int32)[:, None]
    seg_first = jnp.max(jnp.where(starts[None, :] <= places, starts[None, :], 0), axis=1)
    seg_last = jnp.min(
        jnp.where(ends[None, :] > places, ends[None, :], jnp.iinfo(jnp.int32).max // 2), axis=1
    )
    info = jnp.stack([seg_first, seg_last], axis=1) - device * tokens

    cotangent = lax.all_gather(grad_out, "tensor", axis=1, tiled=True)

    w_both = lax.optimization_barrier(jnp.transpose(w_zx, (1, 0, 2)))
    block = 256
    tile = lambda wide: pl.BlockSpec((block, wide), lambda i: (i, 0))
    normed, x_scale, u, dt_raw = call(
        project_kernel, (tokens // block,),
        [tile(width), whole(1, width), pl.BlockSpec((1, width, inner), lambda i: (1, 0, 0)),
         whole(width, 2 * STATE), whole(width, heads)],
        [tile(width), tile(1), tile(total_cols), tile(heads)],
        [shape((tokens, width), bf16), shape((tokens, 1), f32),
         shape((tokens, total_cols), bf16), shape((tokens, heads), f32)],
        [], 10, name="project",
    )(x_in, norm_gain[None, :], w_both, w_bc, w_dt)
    halo = along(u[tokens - HALO :], "seq", 1)
    gate_in = jnp.dot(normed, w_both[0], preferred_element_type=f32).astype(bf16)
    conv_w = jnp.concatenate([conv_x, conv_bc], axis=1)

    acts, dt, logs, local_in, leaving = call(
        fwd_kernel, (chunks,),
        [rows(total_cols), whole(HALO, total_cols), whole(WIDTH + 1, total_cols), rows(heads),
         whole(3, heads), rows(2)],
        [rows(total_cols), rows(heads), rows(heads), stack(STATE, inner),
         whole(STATE + 2 * PAD, inner)],
        [shape((tokens, total_cols), bf16), shape((tokens, heads), f32),
         shape((tokens, heads), f32), shape((chunks, STATE, inner), bf16),
         shape((STATE + 2 * PAD, inner), bf16)],
        [pltpu.VMEM((CHUNK + PAD, total_cols), f32), pltpu.VMEM((STATE, inner), f32),
         pltpu.VMEM((PAD, inner), f32)],
        12, name="conv_states",
    )(u, halo, conv_w, dt_raw, head_params, info)

    def unpacked(sent):
        low = sent[STATE:].astype(f32)
        return sent[:STATE].astype(f32), low[0:1] + low[PAD : PAD + 1]

    def joined(sent, arrived):
        state, fade = unpacked(sent)
        before, fade_before = unpacked(arrived)
        state, fade = state + fade * before, fade * fade_before
        high = fade.astype(bf16).astype(f32)
        rows = [jnp.broadcast_to(part, (PAD, inner)) for part in (high, fade - high)]
        return jnp.concatenate([state] + rows, axis=0).astype(bf16)

    def chained(sent, sign, first_work, second_work):
        arrived, first = together(along(sent, "seq", sign), first_work())
        pair = joined(sent, arrived)
        hops = [hop for hop in range(1, reach + 1, 2) if hop < devices]
        arrived, second = together(
            [along(pair, "seq", sign * hop) for hop in hops], second_work()
        )
        total = unpacked(arrived[-1])[0]
        for block in arrived[-2::-1]:
            state, fade = unpacked(block)
            total = state + fade * total
        return total, first, second

    back_dims = (((1,), (1,)), ((), ()))
    weight_dims = (((0,), (0,)), ((), ()))
    low = lambda a, b, dims: lax.dot_general(a, b, dims, preferred_element_type=f32).astype(bf16)
    wide = lambda a, b, dims: lax.dot_general(a, b, dims, preferred_element_type=f32)

    state_in, grad_gate, y_local = chained(
        leaving, 1,
        lambda: low(cotangent, w_out, back_dims),
        lambda: call(
            intra_kernel, (chunks,),
            [rows(total_cols), rows(heads), rows(heads), stack(STATE, inner), whole(3, heads),
             rows(2)],
            rows(inner), shape((tokens, inner), f32), [], 10, name="intra",
        )(acts, dt, logs, local_in, head_params, info),
    )

    gain_row = gate_gain[None, :]
    mixed, entering, sums = call(
        gate_sums_kernel, (chunks,),
        [rows(inner), c_rows, rows(heads), stack(STATE, inner), whole(STATE, inner),
         rows(inner), rows(inner), whole(1, inner), rows(2)],
        [rows(inner), stack(STATE, inner), stack(PAD, CHUNK)],
        [shape((tokens, inner), f32), shape((chunks, STATE, inner), bf16),
         shape((chunks, PAD, CHUNK), f32)],
        [pltpu.VMEM((PAD, heads), f32)], 10, name="gate_sums",
    )(y_local, acts, logs, local_in, state_in, gate_in, grad_gate, gain_row, info)

    sums = sum_pairs(sums, "tensor")

    gate_normed, grad_gate_in, grad_mixed, grad_local, grad_leaving, grad_gain, grad_skip = call(
        partial(gate_back_kernel, inner_all=inner_all), (chunks,),
        [back(inner), back(inner), back(inner), stack_back(PAD, CHUNK), whole(1, inner),
         back(inner), c_back, back(heads), back(2),
         pl.BlockSpec((2 * PAD, inner), lambda i: (STATE // (2 * PAD), 0))],
        [back(inner), back(inner), back(inner), stack_back(STATE, inner),
         whole(STATE + 2 * PAD, inner), whole(1, inner), whole(1, inner)],
        [shape((tokens, inner), bf16), shape((tokens, inner), bf16), shape((tokens, inner), bf16),
         shape((chunks, STATE, inner), bf16), shape((STATE + 2 * PAD, inner), bf16),
         shape((1, inner), f32), shape((1, inner), f32)],
        [pltpu.VMEM((STATE, inner), f32)], 12, name="gate_back",
    )(mixed, gate_in, grad_gate, sums, gain_row, acts, acts, logs, info, leaving)

    grad_in, early, grad_normed_z = chained(
        grad_leaving, -1,
        lambda: [
            low(cotangent, gate_normed, weight_dims), low(normed, grad_gate_in, weight_dims)
        ],
        lambda: low(grad_gate_in, w_both[0], back_dims),
    )
    ring = Ring(early, "seq")

    pieces = 4
    span = chunks // pieces
    state = {
        "dsuf": jnp.ones((PAD, heads), f32), "gext": jnp.zeros((PAD, total_cols), f32),
        "gc": jnp.zeros((PAD, total_cols), f32), "ghead": jnp.zeros((PAD, heads), f32),
    }

    def scan_piece(piece):
        def run(state):
            top = chunks - piece * span
            part = lambda wide: pl.BlockSpec((CHUNK, wide), lambda i: (top - 1 - i, 0))
            stack_part = lambda *dims: pl.BlockSpec(
                (1,) + dims, lambda i: (top - 1 - i,) + (0,) * len(dims)
            )
            halo_before = pl.BlockSpec(
                (HALO, total_cols),
                lambda i: (jnp.maximum((top - 1 - i) * (CHUNK // HALO) - 1, 0), 0),
            )
            again = [state["grad_u"], state["grad_dt"]] if piece else []
            outs = call(
                partial(bwd_kernel, top=top, aliased=len(again)), (span,),
                [part(inner), part(total_cols), part(heads), part(heads), part(heads),
                 stack_part(STATE, inner), stack_part(STATE, inner), whole(STATE, inner),
                 part(total_cols), halo_before, whole(HALO, total_cols),
                 whole(WIDTH + 1, total_cols), whole(3, heads), part(2), whole(PAD, heads),
                 whole(PAD, total_cols), whole(PAD, total_cols), whole(PAD, heads)]
                + [pl.BlockSpec(memory_space=pl.ANY)] * len(again),
                [part(total_cols), part(heads), whole(HALO, total_cols), whole(HALO, total_cols),
                 whole(PAD, heads), whole(PAD, total_cols), whole(PAD, total_cols),
                 whole(PAD, heads)],
                [shape((tokens, total_cols), bf16), shape((tokens, heads), bf16),
                 shape((HALO, total_cols), f32), shape((HALO, total_cols), f32),
                 shape((PAD, heads), f32), shape((PAD, total_cols), f32),
                 shape((PAD, total_cols), f32), shape((PAD, heads), f32)],
                [pltpu.VMEM((CHUNK + PAD, total_cols), f32),
                 pltpu.VMEM((CHUNK + PAD, total_cols), f32), pltpu.VMEM((CHUNK, CHUNK), f32),
                 pltpu.VMEM((2 * PAD, 256), f32), pltpu.VMEM((CHUNK, inner), bf16)],
                10, name=f"scan_back_{piece}",
                input_output_aliases={18: 0, 19: 1} if piece else {},
            )(grad_mixed, acts, dt, logs, dt_raw, entering, grad_local, grad_in, u, u, halo,
              conv_w, head_params, info, state["dsuf"], state["gext"], state["gc"],
              state["ghead"], *again)
            new = dict(state)
            new.update(grad_u=outs[0], grad_dt=outs[1], dsuf=outs[4], gext=outs[5], gc=outs[6],
                       ghead=outs[7])
            if piece == 0:
                new["tail"] = outs[2]
            if piece == pieces - 1:
                new["sent"] = outs[3]
            return new

        return run

    core = (member & 1).reshape(1)
    split_tile = pl.BlockSpec((2, block, width // 2), lambda i: (0, i, 0))
    own_bc = 2 * STATE // members

    def halo_branch(state):
        sent = along(state["sent"], "seq", -1)
        branch = call(
            partial(branch_kernel, blocks=members), (tokens // block,),
            [pl.BlockSpec(memory_space=pltpu.SMEM), tile(inner), whole(inner, width)],
            split_tile, shape((2, tokens, width // 2), bf16), [], 9, name="branch",
        )(core, state["gate_normed"], w_out)
        return dict(state, sent=sent, branch=branch)

    plans = {}
    slice_width = grad_out.shape[1]
    x_part = lax.dynamic_slice_in_dim(x_in, member * slice_width, slice_width, 1).astype(f32)

    def products(state):
        tail = (state["tail"] + state["sent"]).astype(bf16)
        grad_u = lax.dynamic_update_slice_in_dim(state["grad_u"], tail, tokens - HALO, 0)
        branch_other = swapped(state["branch"][1], "tensor", 1)
        grad_bc = scatter_direct(grad_u[:, inner:], "tensor").astype(bf16)
        late = low(normed, grad_u[:, :inner], weight_dims)
        return dict(state, grad_u=grad_u, grad_bc=grad_bc, late=late, branch_other=branch_other)

    def back_normed(state):
        late_sum = lax.psum_scatter(state["late"], "seq", scatter_dimension=0, tiled=True)
        last = Last(state["branch"][0], state["branch_other"], "tensor", 1)
        branch_sum = last.total([last.send(0)])
        both = jnp.concatenate([state["grad_bc"], state["grad_dt"]], axis=1)
        bcdt = low(both, normed, weight_dims)
        normed_back, dots, gain = call(
            partial(normed_back_kernel, blocks=members), (tokens // block,),
            [pl.BlockSpec(memory_space=pltpu.SMEM), tile(total_cols), tile(heads), tile(width),
             tile(width), tile(1), whole(1, width),
             pl.BlockSpec((1, width, inner), lambda i: (1, 0, 0)), whole(width, 2 * STATE),
             whole(width, heads)],
            [split_tile, pl.BlockSpec((1, PAD, block), lambda i: (i, 0, 0)), whole(1, width)],
            [shape((2, tokens, width // 2), bf16), shape((tokens // block, PAD, block), f32),
             shape((1, width), f32)],
            [], 15, name="normed_back",
        )(core, state["grad_u"], state["grad_dt"], grad_normed_z, x_in, x_scale,
          norm_gain[None, :], w_both, w_bc, w_dt)
        normed_other = swapped(normed_back[1], "tensor", 1)
        dots = sum_pairs(dots[:, 0], "tensor")
        shared = jnp.concatenate(
            [state["gc"][: WIDTH + 1, inner:].reshape(-1), gain.reshape(-1)]
        ).reshape(-1, 128)
        shared = sum_pairs(shared, "tensor")
        blocks = jnp.transpose(bcdt.reshape(-1, devices, width // devices), (1, 0, 2))
        bcdt = summed(dealt(blocks, "seq"))
        plans["late"] = late_sum
        return dict(state, branch_sum=branch_sum, normed_own=normed_back[0],
                    normed_other=normed_other, dots=dots, shared=shared, bcdt=bcdt)

    state["gate_normed"] = gate_normed
    tasks = [scan_piece(i) for i in range(pieces)] + [halo_branch, products, back_normed]
    done = False
    while tasks or not done:
        if not done:
            arrived = ring.send()
        task = tasks.pop(0) if tasks else None
        if task:
            state = task(state)
        if not done:
            if task is not None and tasks:
                arrived, state = together(arrived, state)
            done = ring.add(arrived)
            if done:
                early_sums = ring.moving

    last = Last(state["normed_own"], state["normed_other"], "tensor", 1)
    grad_normed = last.total([last.send(0)])
    bc_rows = dealt(repeated(state["bcdt"][:own_bc].astype(bf16), devices), "seq")
    block_out = (x_part + state["branch_sum"]).astype(bf16)
    grad_w_out = early_sums[0].T
    heads_here = jnp.concatenate(
        [state["ghead"][:2], jnp.sum(grad_skip.reshape(heads, HEAD_DIM), axis=1)[None, :]], axis=0
    )
    own_small = jnp.concatenate(
        [state["gc"][: WIDTH + 1, :inner].reshape(-1), grad_gain.reshape(-1),
         heads_here.reshape(-1), jnp.zeros((-3 * heads % 128,), f32)]
    ).reshape(-1, 128)
    small = jnp.concatenate([state["shared"], own_small], axis=0)
    bc_all = gather_direct(bc_rows, "tensor")
    small = summed(dealt(repeated(small, devices), "seq"))
    gain_part = lax.dynamic_slice_in_dim(norm_gain, member * slice_width, slice_width, 0)
    row_mean = state["dots"].reshape(tokens, 1) * (1.0 / width)
    grad_x = (
        x_scale * (grad_normed * gain_part[None, :] - x_part * x_scale * row_mean)
        + grad_out.astype(f32)
    )
    grad_w_bc = jnp.transpose(bc_all, (1, 3, 0, 2)).reshape(width, 2 * STATE).astype(f32)
    late_sum = plans["late"].astype(f32)

    shared = state["shared"]
    grad_w_dt = state["bcdt"][own_bc:].T
    grad_z_sum = early_sums[1]

    shared, own = small[: shared.shape[0]].reshape(-1), small[shared.shape[0] :].reshape(-1)
    bc_size = (WIDTH + 1) * 2 * STATE
    x_size = (WIDTH + 1) * inner
    grad_conv_bc = shared[:bc_size].reshape(WIDTH + 1, 2 * STATE)
    grad_norm_gain = shared[bc_size:]
    grad_conv_x = own[:x_size].reshape(WIDTH + 1, inner)
    grad_gate_gain = own[x_size : x_size + inner]
    grad_head = own[x_size + inner : x_size + inner + 3 * heads].reshape(3, heads)

    grad_w_zx = jnp.stack([grad_z_sum, late_sum], axis=1)
    return (
        block_out, grad_x, grad_norm_gain, grad_w_zx, grad_w_bc, grad_w_dt, grad_conv_x,
        grad_conv_bc, grad_head, grad_gate_gain, grad_w_out,
    )


def solution(mesh):
    return jax.shard_map(
        per_device,
        mesh=mesh,
        in_specs=(
            P("seq", None), P(), P(None, None, "tensor"), P(), P(None, "tensor"),
            P(None, "tensor"), P(), P(None, "tensor"), P("tensor"), P("tensor", None), P(),
            P("seq", "tensor"),
        ),
        out_specs=(
            P("seq", "tensor"), P("seq", "tensor"), P(), P("seq", None, "tensor"), P(),
            P("seq", "tensor"), P(None, "tensor"), P(), P(None, "tensor"), P("tensor"),
            P("tensor", "seq"),
        ),
        check_vma=False,
    )
```

```python
from functools import partial

import jax
import jax.numpy as jnp
from jax import lax
from jax.experimental import pallas as pl
from jax.experimental.pallas import tpu as pltpu
from jax.sharding import PartitionSpec as P

HEAD_DIM = 64
STATE = 128
WIDTH = 4
CHUNK = 128
REACH = 4096
PAD = 8
HALO = 16
LOG2E = 1.4426950408889634

eps = 1e-05
f32 = jnp.float32
bf16 = jnp.bfloat16
vmem_limit = 56 * 1024 * 1024


def nn(a, b):
    return lax.dot_general(a, b, (((1,), (0,)), ((), ())), preferred_element_type=f32)


def nt(a, b):
    return lax.dot_general(a, b, (((1,), (1,)), ((), ())), preferred_element_type=f32)


def running(mask, v):
    wide = v.shape[1]
    high = v.astype(bf16)
    rest = v - high.astype(f32)
    mid = rest.astype(bf16)
    low = (rest - mid.astype(f32)).astype(bf16)
    out = nn(mask, jnp.concatenate([high, mid, low], axis=1))
    return out[:, 0:wide] + out[:, wide : 2 * wide] + out[:, 2 * wide : 3 * wide]


def head_map(heads):
    row = lax.broadcasted_iota(jnp.int32, (2 * heads, heads * HEAD_DIM), 0)
    col = lax.broadcasted_iota(jnp.int32, (2 * heads, heads * HEAD_DIM), 1)
    row = jnp.where(row >= heads, row - heads, row)
    return jnp.where((col >> 6) == row, 1.0, 0.0).astype(bf16)


def spread(v, member):
    high = v.astype(bf16)
    rest = (v - high.astype(f32)).astype(bf16)
    return nn(jnp.concatenate([high, rest], axis=1), member)


def spread_row(v, member):
    return spread(jnp.broadcast_to(v, (PAD, v.shape[1])), member)[0:1]


def per_head(v, member):
    return nt(v.astype(bf16), member[0 : member.shape[0] // 2])


def triangle(strict, upper):
    row = lax.broadcasted_iota(jnp.int32, (CHUNK, CHUNK), 0)
    col = lax.broadcasted_iota(jnp.int32, (CHUNK, CHUNK), 1)
    if upper:
        row, col = col, row
    keep = (row > col) if strict else (row >= col)
    return jnp.where(keep, 1.0, 0.0).astype(bf16)


def softplus(v):
    return jnp.maximum(v, 0.0) + jnp.log1p(jnp.exp(-jnp.abs(v)))


def sigmoid(v):
    return 0.5 * jnp.tanh(0.5 * v) + 0.5


def seg_bounds(info_ref, chunk):
    info = info_ref[...] - chunk * CHUNK
    return info[:, 0:1], info[:, 1:2]


def row_ids():
    return lax.broadcasted_iota(jnp.int32, (CHUNK, 1), 0)


def flag(v):
    return jnp.where(v, 1.0, 0.0).astype(f32)


def conv_pre(ext_ref, w_ref, masks, lo, wide):
    cols = taps = slice(lo, lo + wide)
    total = w_ref[WIDTH : WIDTH + 1, taps] + w_ref[WIDTH - 1 : WIDTH, taps] * ext_ref[
        PAD : PAD + CHUNK, cols
    ]
    for back in range(1, WIDTH):
        total = total + w_ref[WIDTH - 1 - back : WIDTH - back, taps] * (
            ext_ref[PAD - back : PAD - back + CHUNK, cols] * masks[back]
        )
    return total


def project_kernel(
    x_ref, xh_ref, gain_ref, wx_ref, wbc_ref, wdt_ref, normed_ref, scale_ref, u_ref, halo_ref, dtr_ref,
):
    count = x_ref.shape[0]
    x = jnp.concatenate([x_ref[...], xh_ref[...]], axis=0).astype(f32)
    scale = lax.rsqrt(jnp.mean(x * x, axis=1, keepdims=True) + eps)
    normed = (x * scale * gain_ref[...]).astype(bf16)
    scale_ref[...] = scale[:count]
    normed_ref[...] = normed[:count]
    inner = wx_ref.shape[2]
    u_x = nn(normed, wx_ref[0]).astype(bf16)
    u_bc = nn(normed, wbc_ref[...]).astype(bf16)
    u_ref[:, 0:inner] = u_x[:count]
    u_ref[:, inner:] = u_bc[:count]
    halo_ref[:, 0:inner] = u_x[count:]
    halo_ref[:, inner:] = u_bc[count:]
    dtr_ref[...] = nt(normed[:count], wdt_ref[...])


def fwd_kernel(
    u_ref, halo_ref, cw_ref, dtr_ref, hp_ref, info_ref,
    acts_ref, slope_ref, dt_ref, log_ref, wide_ref, sloc_ref, send_ref,
    ext, held, drun,
):
    chunk = pl.program_id(0)
    heads = dtr_ref.shape[1]
    inner = heads * HEAD_DIM

    @pl.when(chunk == 0)
    def _():
        ext[0:PAD, :] = halo_ref[...].astype(f32)[HALO - PAD : HALO]
        held[...] = jnp.zeros_like(held)
        drun[...] = jnp.ones_like(drun)

    @pl.when(chunk > 0)
    def _():
        ext[0:PAD, :] = ext[CHUNK : CHUNK + PAD, :]

    ext[PAD:, :] = u_ref[...].astype(f32)
    first, last = seg_bounds(info_ref, chunk)
    rows = row_ids()
    wide = 256
    masks = [None] + [
        jnp.broadcast_to(flag(rows - back >= first), (CHUNK, wide)) for back in range(1, WIDTH)
    ]
    for lo in range(0, u_ref.shape[1], wide):
        pre = conv_pre(ext, cw_ref, masks, lo, wide)
        s = sigmoid(pre)
        act = pre * s
        acts_ref[:, lo : lo + wide] = act.astype(bf16)
        slope_ref[:, lo : lo + wide] = (s + act * (1.0 - s)).astype(bf16)

    member = head_map(heads)
    dt = softplus(dtr_ref[...] + hp_ref[0:1, :])
    rate = jnp.exp(hp_ref[1:2, :]) * LOG2E
    logs = running(triangle(False, False), -dt * rate)
    dt_ref[...] = dt
    log_ref[...] = logs
    tail = logs[CHUNK - 1 : CHUNK, :]
    keep_in = flag(first < 0)
    keep_out = flag(last >= CHUNK)
    dt_all = spread(dt, member)
    out_all = spread(jnp.exp2(tail - logs) * keep_out, member)
    into_all = spread(jnp.exp2(logs) * keep_in, member)
    wide_ref[:, 0:inner] = dt_all.astype(bf16)
    wide_ref[:, inner : 2 * inner] = out_all.astype(bf16)
    wide_ref[:, 2 * inner :] = into_all.astype(bf16)
    x_in = (acts_ref[:, 0:inner].astype(f32) * (dt_all * out_all)).astype(bf16)
    b_cols = jnp.transpose(acts_ref[:, inner : inner + STATE].astype(f32)).astype(bf16)
    local = nn(b_cols, x_in)
    decay_all = into_all[CHUNK - 1 : CHUNK, :]
    sloc_ref[...] = held[...].astype(bf16)[None]
    held[...] = decay_all * held[...] + local
    drun[...] = drun[...] * decay_all

    @pl.when(chunk == pl.num_programs(0) - 1)
    def _():
        total = drun[...]
        high = total.astype(bf16)
        send_ref[0:STATE, :] = held[...].astype(bf16)
        send_ref[STATE:, :] = jnp.concatenate(
            [total, total - high.astype(f32)], axis=0
        ).astype(bf16)


def mix_kernel(
    acts_ref, dt_ref, log_ref, sloc_ref, sin_ref, z_ref, gg_ref, gain_ref, hp_ref, info_ref,
    y_ref, sent_ref, sums_ref,
    dpre,
):
    chunk = pl.program_id(0)
    heads = log_ref.shape[1]
    inner = heads * HEAD_DIM
    member = head_map(heads)

    @pl.when(chunk == 0)
    def _():
        dpre[...] = jnp.ones_like(dpre)

    first, _ = seg_bounds(info_ref, chunk)
    rows = lax.broadcasted_iota(jnp.int32, (CHUNK, CHUNK), 0)
    cols = lax.broadcasted_iota(jnp.int32, (CHUNK, CHUNK), 1)
    b = acts_ref[:, inner : inner + STATE]
    c = acts_ref[:, inner + STATE :]
    mixed = jnp.where((cols <= rows) & (cols >= first), nt(c, b), 0.0)
    logs = log_ref[...]
    logs_t = jnp.transpose(logs)
    decay = jnp.exp2(logs[CHUNK - 1 : CHUNK, :]) * flag(first < 0)[CHUNK - 1 : CHUNK, :]
    state = sloc_ref[0].astype(f32) + spread_row(dpre[0:1, :], member) * sin_ref[...]
    dpre[...] = dpre[...] * decay
    state_low = state.astype(bf16)
    state_rest = (state - state_low.astype(f32)).astype(bf16)
    sent_ref[...] = state_low[None]
    x = acts_ref[:, 0:inner].astype(f32)
    xd = x * dt_ref[...].astype(f32)
    skip = spread_row(hp_ref[2:3, :], member)
    into = spread(jnp.exp2(logs) * flag(first < 0), member)
    carried = into * (nn(c, state_low) + nn(c, state_rest)) + skip * x
    lane = lax.broadcasted_iota(jnp.int32, (1, 2 * HEAD_DIM), 1)
    left = flag(lane < HEAD_DIM)
    right = 1.0 - left
    squares = jnp.zeros((CHUNK, 2 * HEAD_DIM), f32)
    dots = jnp.zeros((CHUNK, 2 * HEAD_DIM), f32)
    for pair in range(heads // 2):
        mats = []
        for h in (2 * pair, 2 * pair + 1):
            gap = logs[:, h : h + 1] - logs_t[h : h + 1, :]
            mats.append((jnp.exp2(jnp.minimum(gap, 0.0)) * mixed).astype(bf16))
        at = slice(2 * pair * HEAD_DIM, 2 * (pair + 1) * HEAD_DIM)
        xp = xd[:, at]
        block = jnp.concatenate([(xp * left).astype(bf16), (xp * right).astype(bf16)], axis=0)
        y = carried[:, at] + nn(jnp.concatenate(mats, axis=1), block)
        y_ref[:, at] = y
        z = z_ref[:, at].astype(f32)
        gated = y * (z * sigmoid(z))
        squares = squares + gated * gated
        dots = dots + gated * (gg_ref[:, at].astype(f32) * gain_ref[:, at])
    lane = lax.broadcasted_iota(jnp.int32, (CHUNK, STATE), 1)
    both = jnp.where(
        lane == 0, jnp.sum(squares, axis=1, keepdims=True),
        jnp.where(lane == 1, jnp.sum(dots, axis=1, keepdims=True), 0.0),
    )
    sums_ref[...] = jnp.transpose(both)[0:PAD][None]


def gate_back_kernel(
    y_ref, z_ref, gg_ref, sums_ref, gain_ref, xa_ref, c_ref, into_ref, log_ref, info_ref, fade_ref,
    gn_ref, gz_ref, gy_ref, lloc_ref, send_ref, ggain_ref, gskip_ref,
    held, *, inner_all,
):
    step = pl.program_id(0)
    chunk = pl.num_programs(0) - 1 - step
    heads = log_ref.shape[1]
    member = head_map(heads)

    @pl.when(step == 0)
    def _():
        held[...] = jnp.zeros_like(held)
        ggain_ref[...] = jnp.zeros_like(ggain_ref)
        gskip_ref[...] = jnp.zeros_like(gskip_ref)

    sums = jnp.transpose(jnp.concatenate([sums_ref[0]] * (CHUNK // PAD), axis=0))
    scale = lax.rsqrt(sums[:, 0:1] * (1.0 / inner_all) + eps)
    mean = sums[:, 1:2] * scale * (1.0 / inner_all)
    z = z_ref[...].astype(f32)
    y = y_ref[...]
    s = sigmoid(z)
    act = z * s
    gain = gain_ref[...]
    gg = gg_ref[...].astype(f32)
    unit = y * act * scale
    gn_ref[...] = (unit * gain).astype(bf16)
    ggain_ref[...] += jnp.sum(gg * unit, axis=0, keepdims=True)
    g_gated = scale * (gg * gain - unit * mean)
    gz_ref[...] = (g_gated * y * s * (1.0 + z * (1.0 - s))).astype(bf16)
    gy = g_gated * act
    gy_ref[...] = gy.astype(bf16)
    gskip_ref[...] += jnp.sum(gy * xa_ref[...].astype(f32), axis=0, keepdims=True)
    first, _ = seg_bounds(info_ref, chunk)
    decay = jnp.exp2(log_ref[CHUNK - 1 : CHUNK, :]) * flag(first < 0)[CHUNK - 1 : CHUNK, :]
    weighted = (gy * into_ref[...].astype(f32)).astype(bf16)
    c_cols = jnp.transpose(c_ref[...].astype(f32)).astype(bf16)
    lloc_ref[...] = held[...].astype(bf16)[None]
    held[...] = spread_row(decay, member) * held[...] + nn(c_cols, weighted)

    @pl.when(step == pl.num_programs(0) - 1)
    def _():
        send_ref[0:STATE, :] = held[...].astype(bf16)
        send_ref[STATE:, :] = fade_ref[...]


def bwd_kernel(*refs):
    (
        gy_ref, acts_ref, slope_ref, dt_ref, log_ref, dtr_ref, dtw_ref, outw_ref, into_ref,
        sent_ref, lloc_ref, lin_ref, u_ref, halo_ref, cw_ref, hp_ref, info_ref,
    ) = refs[:17]
    (
        gu_ref, gdt_ref, tail_ref, hg_ref, gc_ref, ghead_ref, dsuf, gext, rows_scr, head_ext, keys,
    ) = refs[17:]
    step = pl.program_id(0)
    chunk = pl.num_programs(0) - 1 - step
    inner = gy_ref.shape[1]
    heads = log_ref.shape[1]
    member = head_map(heads)
    total_cols = inner + 2 * STATE

    @pl.when(step == 0)
    def _():
        dsuf[...] = jnp.ones_like(dsuf)
        gc_ref[...] = jnp.zeros_like(gc_ref)
        ghead_ref[...] = jnp.zeros_like(ghead_ref)
        gext[CHUNK:, :] = jnp.zeros((PAD, total_cols), f32)

    @pl.when(step > 0)
    def _():
        gext[CHUNK:, :] = gext[0:PAD, :]

    first, last = seg_bounds(info_ref, chunk)
    logs = log_ref[...]
    logs_t = jnp.transpose(logs)
    dt = dt_ref[...]
    decay = jnp.exp2(logs[CHUNK - 1 : CHUNK, :]) * flag(first < 0)[CHUNK - 1 : CHUNK, :]
    rate = jnp.exp(hp_ref[1:2, :])

    b = acts_ref[:, inner : inner + STATE]
    c = acts_ref[:, inner + STATE :]
    rows = lax.broadcasted_iota(jnp.int32, (CHUNK, CHUNK), 0)
    cols = lax.broadcasted_iota(jnp.int32, (CHUNK, CHUNK), 1)
    keep = (cols >= rows) & (cols < last)
    mixed = jnp.where(keep, nt(b, c), 0.0)

    lam = lloc_ref[0].astype(f32) + spread_row(dsuf[0:1, :], member) * lin_ref[...]
    lam_low = lam.astype(bf16)
    dsuf[...] = dsuf[...] * decay
    state = sent_ref[0]
    decay_sum = jnp.sum(lam * state.astype(f32), axis=0, keepdims=True) * spread_row(decay, member)
    z_head = per_head(jnp.broadcast_to(decay_sum, (PAD, inner)), member)[0:1]

    gy_low = gy_ref[...]
    gy = gy_low.astype(f32)
    dt_all = dtw_ref[...].astype(f32)
    out_all = outw_ref[...].astype(f32)
    xd_low = (acts_ref[:, 0:inner].astype(f32) * dt_all).astype(bf16)
    xd = xd_low.astype(f32)
    g_out = out_all * nn(b, lam_low)
    e_head = per_head(xd * g_out, member)
    gy_in = gy * into_ref[...].astype(f32)
    f_head = per_head(gy_in * nn(c, state), member)
    g_c = nt(gy_in.astype(bf16), state)
    g_b = nt((xd * out_all).astype(bf16), lam_low)
    skip = spread_row(hp_ref[2:3, :], member)

    lane = lax.broadcasted_iota(jnp.int32, (1, 2 * HEAD_DIM), 1)
    left = flag(lane < HEAD_DIM).astype(bf16)
    right = flag(lane >= HEAD_DIM).astype(bf16)
    mixed2 = jnp.concatenate([mixed, mixed], axis=1)
    d_mixed = jnp.zeros((CHUNK, 2 * CHUNK), f32)
    for pair in range(heads // 2):
        at = slice(2 * pair * HEAD_DIM, 2 * (pair + 1) * HEAD_DIM)
        gyp = gy_low[:, at]
        block = jnp.concatenate([gyp * left, gyp * right], axis=0)
        d_m = nt(xd_low[:, at], block)
        gaps = [logs_t[h : h + 1, :] - logs[:, h : h + 1] for h in (2 * pair, 2 * pair + 1)]
        decays = jnp.exp2(jnp.minimum(jnp.concatenate(gaps, axis=1), 0.0))
        d_mixed = d_mixed + d_m * decays
        weights = (decays * mixed2).astype(bf16)
        g_in = nn(weights, block)
        r_pair = jnp.sum(weights.astype(f32) * d_m, axis=0, keepdims=True)
        rows_scr[2 * pair : 2 * pair + 1, :] = r_pair[:, 0:CHUNK]
        rows_scr[2 * pair + 1 : 2 * pair + 2, :] = r_pair[:, CHUNK:]
        k_pair = xd[:, at] * g_in
        k_high = k_pair.astype(bf16)
        keys[0:CHUNK, at] = k_high
        keys[CHUNK:, at] = (k_pair - k_high.astype(f32)).astype(bf16)
        gext[0:CHUNK, at] = dt_all[:, at] * (g_in + g_out[:, at]) + skip[:, at] * gy[:, at]
    d_mixed = jnp.where(keep, d_mixed[:, 0:CHUNK] + d_mixed[:, CHUNK:], 0.0)
    g_b = g_b + nn(d_mixed.astype(bf16), c)
    g_c = g_c + nn(jnp.transpose(d_mixed).astype(bf16), b)
    gext[0:CHUNK, inner : inner + STATE] = g_b
    gext[0:CHUNK, inner + STATE :] = g_c

    k_both = per_head(keys[...], member)
    k_head = k_both[0:CHUNK] + k_both[CHUNK:]
    r_head = jnp.transpose(rows_scr[...])[:, 0:heads]
    g_log = r_head - k_head + f_head
    g_a = running(triangle(False, True), g_log) + running(triangle(True, False), e_head) + z_head
    v = dtr_ref[...] + hp_ref[0:1, :]
    gate = sigmoid(v)
    ratio = jnp.where(v < -20.0, 1.0, gate / dt)
    g_dt = ratio * (k_head + e_head) - (rate * gate) * g_a
    gdt_ref[...] = g_dt.astype(bf16)
    ghead_ref[0:1, :] += jnp.sum(g_dt, axis=0, keepdims=True)
    ghead_ref[1:2, :] += -rate * jnp.sum(dt * g_a, axis=0, keepdims=True)

    wide = 256
    ids = row_ids()
    ahead = [None] + [
        jnp.broadcast_to(flag(ids + back < last), (CHUNK, wide)) for back in range(1, WIDTH)
    ]
    start = chunk == 0
    for lo in range(0, total_cols, wide):
        here = slice(lo, lo + wide)
        g_pre = gext[0:CHUNK, here] * slope_ref[:, here].astype(f32)
        gext[0:CHUNK, here] = g_pre
        u = u_ref[:, here].astype(f32)
        gc_ref[WIDTH : WIDTH + 1, here] += jnp.sum(g_pre, axis=0, keepdims=True)
        gc_ref[WIDTH - 1 : WIDTH, here] += jnp.sum(g_pre * u, axis=0, keepdims=True)
        g_u = cw_ref[WIDTH - 1 : WIDTH, here] * g_pre
        for back in range(1, WIDTH):
            tap = WIDTH - 1 - back
            later = gext[back : back + CHUNK, here] * ahead[back]
            gc_ref[tap : tap + 1, here] += jnp.sum(later * u, axis=0, keepdims=True)
            g_u = g_u + cw_ref[tap : tap + 1, here] * later
        gu_ref[:, here] = g_u.astype(bf16)

        @pl.when(step == 0)
        def _(g_u=g_u, here=here):
            tail_ref[:, here] = g_u[CHUNK - HALO :, :]

        @pl.when(start)
        def _(g_pre=g_pre, here=here):
            halo = jnp.zeros((PAD, wide), f32)
            u_before = halo_ref[:, here].astype(f32)[HALO - PAD : HALO]
            head_ext[0:PAD, :] = jnp.zeros((PAD, wide), f32)
            near = lax.broadcasted_iota(jnp.int32, (PAD, 1), 0)
            for back in range(1, WIDTH):
                tap = WIDTH - 1 - back
                head_ext[PAD:, :] = g_pre[0:PAD, :] * flag(near - back >= first[0:PAD, :])
                later = head_ext[back : back + PAD, :]
                gc_ref[tap : tap + 1, here] += jnp.sum(later * u_before, axis=0, keepdims=True)
                halo = halo + cw_ref[tap : tap + 1, here] * later
            hg_ref[0:PAD, here] = jnp.zeros((PAD, wide), f32)
            hg_ref[PAD:, here] = halo


def put_halves(kept_ref, given_ref, value, parity, blocks):
    wide = value.shape[1] // blocks
    halves = [
        jnp.concatenate([value[:, i * wide : (i + 1) * wide] for i in range(odd, blocks, 2)], axis=1)
        for odd in range(2)
    ]

    @pl.when(parity == 0)
    def _():
        kept_ref[...] = halves[0]
        given_ref[...] = halves[1]

    @pl.when(parity == 1)
    def _():
        kept_ref[...] = halves[1]
        given_ref[...] = halves[0]


def fold_kernel(parity_ref, kept_ref, arrived_ref, keep_ref, give_ref):
    total = kept_ref[...].astype(f32) + arrived_ref[...].astype(f32)
    half = total.shape[1] // 2

    @pl.when(parity_ref[0] == 0)
    def _():
        keep_ref[...] = total[:, :half]
        give_ref[...] = total[:, half:].astype(bf16)

    @pl.when(parity_ref[0] == 1)
    def _():
        keep_ref[...] = total[:, half:]
        give_ref[...] = total[:, :half].astype(bf16)


def tn(a, b):
    return lax.dot_general(a, b, (((0,), (0,)), ((), ())), preferred_element_type=f32)


def early_kernel(cot_ref, normed_ref, gn_ref, gz_ref, out_ref):
    inner = gn_ref.shape[1]
    out_ref[:, 0:inner] = tn(cot_ref[...], gn_ref[...]).astype(bf16)
    out_ref[:, inner:] = tn(normed_ref[...], gz_ref[...]).astype(bf16)


def branch_kernel(parity_ref, gn_ref, w_ref, kept_ref, given_ref, *, blocks):
    put_halves(kept_ref, given_ref, nn(gn_ref[...], w_ref[...]).astype(bf16), parity_ref[0], blocks)


def normed_back_kernel(
    parity_ref, gu_ref, gdt_ref, gz_ref, x_ref, scale_ref, gain_ref, wx_ref, wbc_ref, wdt_ref,
    kept_ref, given_ref, dots_ref, ggain_ref, *, blocks,
):
    inner = wx_ref.shape[2]

    @pl.when(pl.program_id(0) == 0)
    def _():
        ggain_ref[...] = jnp.zeros_like(ggain_ref)

    total = gz_ref[...].astype(f32) + nt(gu_ref[:, 0:inner], wx_ref[0])
    total = total + nt(gu_ref[:, inner:], wbc_ref[...]) + nn(gdt_ref[...], wdt_ref[...])
    unit = x_ref[...].astype(f32) * scale_ref[...]
    with_unit = total * unit
    ggain_ref[...] += jnp.sum(with_unit, axis=0, keepdims=True)
    dots = jnp.sum(with_unit * gain_ref[...], axis=1, keepdims=True)
    dots_ref[...] = jnp.transpose(jnp.broadcast_to(dots, (dots.shape[0], 128)))[0:PAD][None]
    put_halves(kept_ref, given_ref, total.astype(bf16), parity_ref[0], blocks)


def along(value, axis, distance):
    count = lax.axis_size(axis)
    route = [(i, i + distance) for i in range(count) if 0 <= i + distance < count]
    return lax.ppermute(value, axis, route)


def swapped(value, axis, bit):
    return lax.ppermute(value, axis, [(i, i ^ bit) for i in range(lax.axis_size(axis))])


def all_sum(value, axis):
    bit = 1
    while bit < lax.axis_size(axis):
        value = value + swapped(value, axis, bit)
        bit *= 2
    return value


def sum_pairs(value, axis):
    parts = [swapped(value, axis, mask) for mask in range(1, lax.axis_size(axis))]
    return value + sum(parts[1:], parts[0])


def summed(blocks):
    total = blocks[0].astype(f32)
    for block in blocks[1:]:
        total = total + block.astype(f32)
    return total


def halves_of(parts, axis, bit):
    upper = (lax.axis_index(axis) & bit) != 0
    kept = [jnp.where(upper, b, a) for a, b in zip(parts[0::2], parts[1::2])]
    given = [jnp.where(upper, a, b) for a, b in zip(parts[0::2], parts[1::2])]
    return kept, given


class Last:

    def __init__(self, kept, arrived, axis, pieces):
        parts = jnp.split(kept.astype(f32) + arrived.astype(f32), lax.axis_size(axis) // 2, axis=1)
        bit = 2
        while True:
            keep, give = halves_of(parts, axis, bit)
            give = jnp.concatenate(give, axis=1).astype(bf16)
            if 2 * bit >= lax.axis_size(axis):
                break
            other = jnp.split(swapped(give, axis, bit), len(keep), axis=1)
            parts = [k + o.astype(f32) for k, o in zip(keep, other)]
            bit *= 2
        self.axis, self.bit, self.keep = axis, bit, keep[0]
        rows = give.shape[0] // pieces
        self.give = [give[i * rows : (i + 1) * rows] for i in range(pieces)]

    def send(self, piece):
        return swapped(self.give[piece], self.axis, self.bit)

    def total(self, arrived):
        return self.keep + jnp.concatenate(arrived, axis=0).astype(f32)


def ring_order(count):
    return list(range(0, count, 2)) + list(range(count - 1, 0, -2))


def dealt(value, axis):
    return lax.all_to_all(value, axis, 0, 0, tiled=True)


def repeated(value, count):
    return jnp.broadcast_to(value[None], (count,) + value.shape)


def grouped_send(value, axis):
    count = lax.axis_size(axis) // 2
    me = lax.axis_index(axis) >> 1
    rows = value.shape[0] // count
    own = lax.dynamic_slice_in_dim(value, me * rows, rows, 0)
    return [own] + [
        swapped(lax.dynamic_slice_in_dim(value, (me ^ mask) * rows, rows, 0), axis, 2 * mask)
        for mask in range(1, count)
    ]


class Ring:

    def __init__(self, values, axis):
        count = lax.axis_size(axis)
        self.values, self.axis, self.count, self.hop = values, axis, count, 0
        self.order = ring_order(count)
        me = lax.axis_index(axis)
        self.spot = jnp.where(me % 2 == 0, me // 2, count - (me + 1) // 2)
        self.moving = self.mine()

    def signs(self):
        return [1 - 2 * (i % 2) for i in range(len(self.values))]

    def mine(self):
        blocks = []
        for value, sign in zip(self.values, self.signs()):
            rows = value.shape[0] // self.count
            ahead = sign * (self.count - 1 - self.hop)
            spot = (self.spot + ahead + 2 * self.count) % self.count
            owner = jnp.where(spot < self.count // 2, 2 * spot, 2 * (self.count - spot) - 1)
            blocks.append(lax.dynamic_slice_in_dim(value, owner * rows, rows, 0))
        return blocks

    def send(self):
        arrived = []
        for block, sign in zip(self.moving, self.signs()):
            route = [
                (self.order[i], self.order[(i + sign) % self.count]) for i in range(self.count)
            ]
            arrived.append(lax.ppermute(block, self.axis, route))
        return arrived

    def add(self, arrived):
        self.hop += 1
        blocks = [a.astype(f32) + b.astype(f32) for a, b in zip(arrived, self.mine())]
        done = self.hop == self.count - 1
        self.moving = blocks if done else [block.astype(bf16) for block in blocks]
        return done


def scatter_direct(value, axis):
    count = lax.axis_size(axis)
    me = lax.axis_index(axis)
    wide = value.shape[1] // count
    own = lax.dynamic_slice_in_dim(value, me * wide, wide, 1)
    return summed([own] + [
        swapped(lax.dynamic_slice_in_dim(value, (me ^ mask) * wide, wide, 1), axis, mask)
        for mask in range(1, count)
    ])


def gather_direct(value, axis):
    count = lax.axis_size(axis)
    me = lax.axis_index(axis)
    parts = [value] + [swapped(value, axis, mask) for mask in range(1, count)]
    ordered = []
    for place in range(count):
        part = parts[place]
        for mask in range(1, count):
            part = jnp.where(me == mask, parts[place ^ mask], part)
        ordered.append(part)
    return jnp.concatenate(ordered, axis=1)


def all_sum_low(value, axis):
    bit = 1
    while bit < lax.axis_size(axis):
        value = value + swapped(value.astype(bf16), axis, bit).astype(f32)
        bit *= 2
    return value


def call(kernel, grid, in_specs, out_specs, out_shape, scratch, micros, **names):
    return pl.pallas_call(
        kernel,
        grid=grid,
        in_specs=in_specs,
        out_specs=out_specs,
        out_shape=out_shape,
        scratch_shapes=scratch,
        compiler_params=pltpu.CompilerParams(
            dimension_semantics=("arbitrary",), vmem_limit_bytes=vmem_limit
        ),
        cost_estimate=pl.CostEstimate(
            flops=micros * 10**9, bytes_accessed=micros * 10**6, transcendentals=0
        ),
        **names,
    )


def together(*values):
    return lax.optimization_barrier(values)


def per_device(
    x_in, norm_gain, w_zx, w_bc, w_dt, conv_x, conv_bc, head_params, gate_gain, w_out, lengths,
    grad_out,
):
    tokens, width = x_in.shape
    heads = head_params.shape[1]
    inner = gate_gain.shape[0]
    members = lax.axis_size("tensor")
    devices = lax.axis_size("seq")
    inner_all = inner * members
    total_cols = inner + 2 * STATE
    chunks = tokens // CHUNK
    reach = min(-(-REACH // tokens), devices - 1)
    device = lax.axis_index("seq")
    member = lax.axis_index("tensor")

    shape = jax.ShapeDtypeStruct
    rows = lambda wide: pl.BlockSpec((CHUNK, wide), lambda i: (i, 0))
    back = lambda wide: pl.BlockSpec((CHUNK, wide), lambda i: (chunks - 1 - i, 0))
    whole = lambda *dims: pl.BlockSpec(dims, lambda i: (0,) * len(dims))
    stack = lambda *dims: pl.BlockSpec((1,) + dims, lambda i: (i,) + (0,) * len(dims))
    stack_back = lambda *dims: pl.BlockSpec(
        (1,) + dims, lambda i: (chunks - 1 - i,) + (0,) * len(dims)
    )
    c_at = inner // STATE + 1
    c_rows = pl.BlockSpec((CHUNK, STATE), lambda i: (i, c_at))
    c_back = pl.BlockSpec((CHUNK, STATE), lambda i: (chunks - 1 - i, c_at))

    ends = jnp.cumsum(lengths)
    starts = ends - lengths
    places = device * tokens + jnp.arange(tokens, dtype=jnp.int32)[:, None]
    seg_first = jnp.max(jnp.where(starts[None, :] <= places, starts[None, :], 0), axis=1)
    seg_last = jnp.min(
        jnp.where(ends[None, :] > places, ends[None, :], jnp.iinfo(jnp.int32).max // 2), axis=1
    )
    info = jnp.stack([seg_first, seg_last], axis=1) - device * tokens

    cotangent = lax.all_gather(grad_out, "tensor", axis=1, tiled=True)

    x_halo = along(x_in[tokens - HALO :], "seq", 1)
    w_both = lax.optimization_barrier(jnp.transpose(w_zx, (1, 0, 2)))
    block = 256
    tile = lambda wide: pl.BlockSpec((block, wide), lambda i: (i, 0))
    normed, x_scale, u, halo, dt_raw = call(
        project_kernel, (tokens // block,),
        [tile(width), whole(HALO, width), whole(1, width),
         pl.BlockSpec((1, width, inner), lambda i: (1, 0, 0)), whole(width, 2 * STATE),
         whole(heads, width)],
        [tile(width), tile(1), tile(total_cols), whole(HALO, total_cols), tile(heads)],
        [shape((tokens, width), bf16), shape((tokens, 1), f32),
         shape((tokens, total_cols), bf16), shape((HALO, total_cols), bf16),
         shape((tokens, heads), f32)],
        [], 10, name="project",
    )(x_in, x_halo, norm_gain[None, :], w_both, w_bc, w_dt.T)
    conv_w = jnp.concatenate([conv_x, conv_bc], axis=1)

    acts, slope, dt, logs, spread_out, local_in, leaving = call(
        fwd_kernel, (chunks,),
        [rows(total_cols), whole(HALO, total_cols), whole(WIDTH + 1, total_cols), rows(heads),
         whole(3, heads), rows(2)],
        [rows(total_cols), rows(total_cols), rows(heads), rows(heads), rows(3 * inner),
         stack(STATE, inner), whole(STATE + 2 * PAD, inner)],
        [shape((tokens, total_cols), bf16), shape((tokens, total_cols), bf16),
         shape((tokens, heads), f32), shape((tokens, heads), f32),
         shape((tokens, 3 * inner), bf16), shape((chunks, STATE, inner), bf16),
         shape((STATE + 2 * PAD, inner), bf16)],
        [pltpu.VMEM((CHUNK + PAD, total_cols), f32), pltpu.VMEM((STATE, inner), f32),
         pltpu.VMEM((PAD, inner), f32)],
        12, name="conv_states",
    )(u, halo, conv_w, dt_raw, head_params, info)
    spread_rows = lambda which: pl.BlockSpec((CHUNK, inner), lambda i: (i, which))
    spread_back = lambda which: pl.BlockSpec((CHUNK, inner), lambda i: (chunks - 1 - i, which))

    def unpacked(sent):
        low = sent[STATE:].astype(f32)
        return sent[:STATE].astype(f32), low[0:1] + low[PAD : PAD + 1]

    def joined(sent, arrived):
        state, fade = unpacked(sent)
        before, fade_before = unpacked(arrived)
        state, fade = state + fade * before, fade * fade_before
        high = fade.astype(bf16).astype(f32)
        rows = [jnp.broadcast_to(part, (PAD, inner)) for part in (high, fade - high)]
        return jnp.concatenate([state] + rows, axis=0).astype(bf16)

    def chained(sent, sign, first_work, second_work):
        arrived, first = together(along(sent, "seq", sign), first_work())
        pair = joined(sent, arrived)
        hops = [hop for hop in range(1, reach + 1, 2) if hop < devices]
        arrived, second = together(
            [along(pair, "seq", sign * hop) for hop in hops], second_work()
        )
        total = unpacked(arrived[-1])[0]
        for block in arrived[-2::-1]:
            state, fade = unpacked(block)
            total = state + fade * total
        return total, first, second

    back_dims = (((1,), (1,)), ((), ()))
    weight_dims = (((0,), (0,)), ((), ()))
    low = lambda a, b, dims: lax.dot_general(a, b, dims, preferred_element_type=f32).astype(bf16)
    wide = lambda a, b, dims: lax.dot_general(a, b, dims, preferred_element_type=f32)

    state_in, grad_gate, gate_in = chained(
        leaving, 1,
        lambda: low(cotangent, w_out, back_dims),
        lambda: low(normed, w_both[0], (((1,), (0,)), ((), ()))),
    )

    gain_row = gate_gain[None, :]
    mixed, entering, sums = call(
        mix_kernel, (chunks,),
        [rows(total_cols), spread_rows(0), rows(heads), stack(STATE, inner),
         whole(STATE, inner), rows(inner), rows(inner), whole(1, inner), whole(3, heads), rows(2)],
        [rows(inner), stack(STATE, inner), stack(PAD, CHUNK)],
        [shape((tokens, inner), f32), shape((chunks, STATE, inner), bf16),
         shape((chunks, PAD, CHUNK), f32)],
        [pltpu.VMEM((PAD, heads), f32)], 15, name="mix",
    )(acts, spread_out, logs, local_in, state_in, gate_in, grad_gate, gain_row,
      head_params, info)

    gate_rows = sum_pairs(sums, "tensor")

    gate_normed, grad_gate_in, grad_mixed, grad_local, grad_leaving, grad_gain, grad_skip = call(
        partial(gate_back_kernel, inner_all=inner_all), (chunks,),
        [back(inner), back(inner), back(inner), stack_back(PAD, CHUNK), whole(1, inner),
         back(inner), c_back, spread_back(2), back(heads), back(2),
         pl.BlockSpec((2 * PAD, inner), lambda i: (STATE // (2 * PAD), 0))],
        [back(inner), back(inner), back(inner), stack_back(STATE, inner),
         whole(STATE + 2 * PAD, inner), whole(1, inner), whole(1, inner)],
        [shape((tokens, inner), bf16), shape((tokens, inner), bf16), shape((tokens, inner), bf16),
         shape((chunks, STATE, inner), bf16), shape((STATE + 2 * PAD, inner), bf16),
         shape((1, inner), f32), shape((1, inner), f32)],
        [pltpu.VMEM((STATE, inner), f32)], 12, name="gate_back",
    )(mixed, gate_in, grad_gate, gate_rows, gain_row, acts, acts, spread_out, logs, info, leaving)

    tall = lambda cols: pl.BlockSpec((tokens, cols), lambda i: (0, i))
    grad_in, grad_normed_z, early = chained(
        grad_leaving, -1,
        lambda: low(grad_gate_in, w_both[0], back_dims),
        lambda: call(
            early_kernel, (width // 512,),
            [tall(512), tall(512), whole(tokens, inner), whole(tokens, inner)],
            pl.BlockSpec((512, 2 * inner), lambda i: (i, 0)), shape((width, 2 * inner), bf16), [],
            14, name="early",
        )(cotangent, normed, gate_normed, grad_gate_in),
    )
    early, grad_in = together(early, grad_in)
    early_sum = lax.psum_scatter(early, "seq", scatter_dimension=0, tiled=True)

    part = back
    grad_u, grad_dt, tail, sent, grad_conv, grad_heads = call(
        bwd_kernel, (chunks,),
        [part(inner), part(total_cols), part(total_cols), part(heads), part(heads),
         part(heads), spread_back(0), spread_back(1), spread_back(2),
         stack_back(STATE, inner), stack_back(STATE, inner), whole(STATE, inner),
         part(total_cols), whole(HALO, total_cols),
         whole(WIDTH + 1, total_cols), whole(3, heads), part(2)],
        [part(total_cols), part(heads), whole(HALO, total_cols), whole(HALO, total_cols),
         whole(PAD, total_cols), whole(PAD, heads)],
        [shape((tokens, total_cols), bf16), shape((tokens, heads), bf16),
         shape((HALO, total_cols), f32), shape((HALO, total_cols), f32),
         shape((PAD, total_cols), f32), shape((PAD, heads), f32)],
        [pltpu.VMEM((PAD, heads), f32), pltpu.VMEM((CHUNK + PAD, total_cols), f32),
         pltpu.VMEM((CHUNK, CHUNK), f32),
         pltpu.VMEM((2 * PAD, 256), f32), pltpu.VMEM((2 * CHUNK, inner), bf16)],
        30, name="scan_back",
    )(grad_mixed, acts, slope, dt, logs, dt_raw, spread_out, spread_out, spread_out,
      entering, grad_local, grad_in, u, halo, conv_w, head_params, info)

    core = (member & 1).reshape(1)
    split_tile = pl.BlockSpec((2, block, width // 2), lambda i: (0, i, 0))
    own_bc = 2 * STATE // members

    slice_width = grad_out.shape[1]
    x_part = lax.dynamic_slice_in_dim(x_in, member * slice_width, slice_width, 1).astype(f32)
    parity = device & 1

    sent, gate_normed = together(sent, gate_normed)
    sent = along(sent, "seq", -1)
    branch_kept, branch_given = call(
        partial(branch_kernel, blocks=members), (tokens // block,),
        [pl.BlockSpec(memory_space=pltpu.SMEM), tile(inner), whole(inner, width)],
        [tile(width // 2)] * 2, [shape((tokens, width // 2), bf16)] * 2, [], 9, name="branch",
    )(core, gate_normed, w_out)
    sent, branch_kept, branch_given = together(sent, branch_kept, branch_given)
    tail = (tail + sent).astype(bf16)
    grad_u = lax.dynamic_update_slice_in_dim(grad_u, tail, tokens - HALO, 0)

    some = inner // 2
    late = low(normed, grad_u[:, :inner], weight_dims)
    late_blocks = late.reshape(devices // 2, 2, width // devices, inner)
    half_of = lambda odd: lax.dynamic_index_in_dim(late_blocks, odd, 1, False).reshape(-1, inner)
    given, kept = half_of(1 - parity), half_of(parity)
    given, kept, grad_u, grad_dt = together(given, kept, grad_u, grad_dt)
    def first_work():
        return call(
            partial(normed_back_kernel, blocks=members), (tokens // block,),
            [pl.BlockSpec(memory_space=pltpu.SMEM), tile(total_cols), tile(heads), tile(width),
             tile(width), tile(1), whole(1, width),
             pl.BlockSpec((1, width, inner), lambda i: (1, 0, 0)), whole(width, 2 * STATE),
             whole(heads, width)],
            [tile(width // 2), tile(width // 2), pl.BlockSpec((1, PAD, block), lambda i: (i, 0, 0)), whole(1, width)],
            [shape((tokens, width // 2), bf16), shape((tokens, width // 2), bf16),
             shape((tokens // block, PAD, block), f32),
             shape((1, width), f32)],
            [], 15, name="normed_back",
        )(core, grad_u, grad_dt, grad_normed_z, x_in, x_scale, norm_gain[None, :], w_both, w_bc,
          w_dt.T)

    arrived_first, (normed_kept, normed_given, dots_here, gain) = together(
        swapped(given[:, :some], "seq", 1), first_work()
    )

    def fold(kept, arrived):
        bit = 2
        while bit < members:
            wide_now = kept.shape[1]
            kept, given = call(
                fold_kernel, (tokens // block,),
                [pl.BlockSpec(memory_space=pltpu.SMEM), tile(wide_now), tile(wide_now)],
                [tile(wide_now // 2)] * 2,
                [shape((tokens, wide_now // 2), f32), shape((tokens, wide_now // 2), bf16)],
                [], 3, name="fold",
            )(((member // bit) & 1).reshape(1), kept, arrived)
            bit *= 2
            if bit < members:
                arrived = swapped(given, "tensor", bit // 2)
        return kept, swapped(given, "tensor", bit // 2)


    def second_work():
        grad_bc = scatter_direct(grad_u[:, inner:], "tensor").astype(bf16)
        shared = jnp.concatenate(
            [grad_conv[: WIDTH + 1, inner:].reshape(-1), gain.reshape(-1)]
        ).reshape(-1, 128)
        return (
            grad_bc, sum_pairs(dots_here[:, 0], "tensor"), sum_pairs(shared, "tensor"),
            swapped(branch_given, "tensor", 1),
        )

    grad_bc, dots, shared, branch_other = together(*second_work())

    def third_work():
        both = jnp.concatenate([grad_bc, grad_dt], axis=1)
        bcdt = low(both, normed, weight_dims)
        blocks = jnp.transpose(bcdt.reshape(-1, devices, width // devices), (1, 0, 2))
        branch_keep, branch_sent = fold(branch_kept, branch_other)
        return (
            dealt(blocks, "seq"), branch_keep, branch_sent, swapped(normed_given, "tensor", 1),
        )

    bcdt, branch_keep, branch_sent, normed_other = together(*third_work())

    def fourth_work():
        total = summed(bcdt)
        normed_keep, normed_sent = fold(normed_kept, normed_other)
        block_out = (x_part + branch_keep + branch_sent.astype(f32)).astype(bf16)
        rows = repeated(total[:own_bc].astype(bf16).T, devices)
        return total, dealt(rows, "seq"), normed_keep, normed_sent, block_out

    bcdt, bc_rows, normed_keep, normed_sent, block_out, arrived_last = together(
        *fourth_work(), swapped(given[:, some:], "seq", 1)
    )
    arrived = jnp.concatenate([arrived_first, arrived_last], axis=1)
    flying = (kept.astype(f32) + arrived.astype(f32)).astype(bf16)
    flying, bc_rows, normed_keep = together(flying, bc_rows, normed_keep)

    def fifth_work():
        grad_normed = normed_keep + normed_sent.astype(f32)
        gain_part = lax.dynamic_slice_in_dim(norm_gain, member * slice_width, slice_width, 0)
        row_mean = dots.reshape(tokens, 1) * (1.0 / width)
        grad_x = (
            x_scale * (grad_normed * gain_part[None, :] - x_part * x_scale * row_mean)
            + grad_out.astype(f32)
        )
        bc_all = gather_direct(bc_rows.reshape(width, own_bc), "tensor")
        heads_here = jnp.concatenate(
            [grad_heads[:2], jnp.sum(grad_skip.reshape(heads, HEAD_DIM), axis=1)[None, :]], axis=0
        )
        own_small = jnp.concatenate(
            [grad_conv[: WIDTH + 1, :inner].reshape(-1), grad_gain.reshape(-1),
             heads_here.reshape(-1), jnp.zeros((-3 * heads % 128,), f32)]
        ).reshape(-1, 128)
        small = jnp.concatenate([shared, own_small], axis=0)
        return grad_x, bc_all, summed(dealt(repeated(small, devices), "seq"))

    sums, (grad_x, bc_all, small) = together(grouped_send(flying, "seq"), fifth_work())
    grad_w_bc = bc_all.astype(f32)
    late_sum = summed(sums)
    early_sum = early_sum.astype(f32)
    grad_z_sum = early_sum[:, inner:]
    grad_w_out = early_sum[:, :inner].T

    grad_w_dt = bcdt[own_bc:].T

    shared, own = small[: shared.shape[0]].reshape(-1), small[shared.shape[0] :].reshape(-1)
    bc_size = (WIDTH + 1) * 2 * STATE
    x_size = (WIDTH + 1) * inner
    grad_conv_bc = shared[:bc_size].reshape(WIDTH + 1, 2 * STATE)
    grad_norm_gain = shared[bc_size:]
    grad_conv_x = own[:x_size].reshape(WIDTH + 1, inner)
    grad_gate_gain = own[x_size : x_size + inner]
    grad_head = own[x_size + inner : x_size + inner + 3 * heads].reshape(3, heads)

    grad_w_zx = jnp.stack([grad_z_sum, late_sum], axis=1)
    return (
        block_out, grad_x, grad_norm_gain, grad_w_zx, grad_w_bc, grad_w_dt, grad_conv_x,
        grad_conv_bc, grad_head, grad_gate_gain, grad_w_out,
    )


def solution(mesh):
    return jax.shard_map(
        per_device,
        mesh=mesh,
        in_specs=(
            P("seq", None), P(), P(None, None, "tensor"), P(), P(None, "tensor"),
            P(None, "tensor"), P(), P(None, "tensor"), P("tensor"), P("tensor", None), P(),
            P("seq", "tensor"),
        ),
        out_specs=(
            P("seq", "tensor"), P("seq", "tensor"), P(), P("seq", None, "tensor"), P(),
            P("seq", "tensor"), P(None, "tensor"), P(), P(None, "tensor"), P("tensor"),
            P("tensor", "seq"),
        ),
        check_vma=False,
    )
```

```python
from functools import partial

import jax
import jax.numpy as jnp
from jax import lax
from jax.experimental import pallas as pl
from jax.experimental.pallas import tpu as pltpu
from jax.sharding import PartitionSpec as P

HEAD_DIM = 64
STATE = 128
WIDTH = 4
CHUNK = 128
REACH = 4096
PAD = 8
HALO = 16
LOG2E = 1.4426950408889634

eps = 1e-05
f32 = jnp.float32
bf16 = jnp.bfloat16


def nn(a, b):
    return lax.dot_general(a, b, (((1,), (0,)), ((), ())), preferred_element_type=f32)


def nt(a, b):
    return lax.dot_general(a, b, (((1,), (1,)), ((), ())), preferred_element_type=f32)


def running(mask, v):
    wide = v.shape[1]
    high = v.astype(bf16)
    rest = v - high.astype(f32)
    mid = rest.astype(bf16)
    low = (rest - mid.astype(f32)).astype(bf16)
    out = nn(mask, jnp.concatenate([high, mid, low], axis=1))
    return out[:, 0:wide] + out[:, wide : 2 * wide] + out[:, 2 * wide : 3 * wide]


def head_map(heads):
    row = lax.broadcasted_iota(jnp.int32, (2 * heads, heads * HEAD_DIM), 0)
    col = lax.broadcasted_iota(jnp.int32, (2 * heads, heads * HEAD_DIM), 1)
    row = jnp.where(row >= heads, row - heads, row)
    return jnp.where((col >> 6) == row, 1.0, 0.0).astype(bf16)


def spread(v, member):
    high = v.astype(bf16)
    rest = (v - high.astype(f32)).astype(bf16)
    return nn(jnp.concatenate([high, rest], axis=1), member)


def spread_row(v, member):
    return spread(jnp.broadcast_to(v, (PAD, v.shape[1])), member)[0:1]


def per_head(v, member):
    return nt(v.astype(bf16), member[0 : member.shape[0] // 2])


def triangle(strict, upper):
    row = lax.broadcasted_iota(jnp.int32, (CHUNK, CHUNK), 0)
    col = lax.broadcasted_iota(jnp.int32, (CHUNK, CHUNK), 1)
    if upper:
        row, col = col, row
    keep = (row > col) if strict else (row >= col)
    return jnp.where(keep, 1.0, 0.0).astype(bf16)


def softplus(v):
    return jnp.maximum(v, 0.0) + jnp.log1p(jnp.exp(-jnp.abs(v)))


def sigmoid(v):
    return 0.5 * jnp.tanh(0.5 * v) + 0.5


def seg_bounds(info_ref, chunk):
    info = info_ref[...] - chunk * CHUNK
    return info[:, 0:1], info[:, 1:2]


def row_ids():
    return lax.broadcasted_iota(jnp.int32, (CHUNK, 1), 0)


def flag(v):
    return jnp.where(v, 1.0, 0.0).astype(f32)


def conv_pre(ext_ref, w_ref, masks, lo, wide):
    cols = taps = slice(lo, lo + wide)
    total = w_ref[WIDTH : WIDTH + 1, taps] + w_ref[WIDTH - 1 : WIDTH, taps] * ext_ref[
        PAD : PAD + CHUNK, cols
    ]
    for back in range(1, WIDTH):
        total = total + w_ref[WIDTH - 1 - back : WIDTH - back, taps] * (
            ext_ref[PAD - back : PAD - back + CHUNK, cols] * masks[back]
        )
    return total


def project_kernel(
    x_ref, xh_ref, gain_ref, wx_ref, wbc_ref, wdt_ref, normed_ref, scale_ref, u_ref, halo_ref, dtr_ref,
):
    count = x_ref.shape[0]
    x = jnp.concatenate([x_ref[...], xh_ref[...]], axis=0).astype(f32)
    scale = lax.rsqrt(jnp.mean(x * x, axis=1, keepdims=True) + eps)
    normed = (x * scale * gain_ref[...]).astype(bf16)
    scale_ref[...] = scale[:count]
    normed_ref[...] = normed[:count]
    inner = wx_ref.shape[2]
    u_x = nn(normed, wx_ref[0]).astype(bf16)
    u_bc = nn(normed, wbc_ref[...]).astype(bf16)
    u_ref[:, 0:inner] = u_x[:count]
    u_ref[:, inner:] = u_bc[:count]
    halo_ref[:, 0:inner] = u_x[count:]
    halo_ref[:, inner:] = u_bc[count:]
    dtr_ref[...] = nt(normed[:count], wdt_ref[...])


def fwd_kernel(
    u_ref, halo_ref, cw_ref, dtr_ref, hp_ref, info_ref,
    acts_ref, slope_ref, dt_ref, log_ref, wide_ref, sloc_ref, send_ref,
    ext, held, drun,
):
    chunk = pl.program_id(0)
    heads = dtr_ref.shape[1]
    inner = heads * HEAD_DIM

    @pl.when(chunk == 0)
    def _():
        ext[0:PAD, :] = halo_ref[...].astype(f32)[HALO - PAD : HALO]
        held[...] = jnp.zeros_like(held)
        drun[...] = jnp.ones_like(drun)

    @pl.when(chunk > 0)
    def _():
        ext[0:PAD, :] = ext[CHUNK : CHUNK + PAD, :]

    ext[PAD:, :] = u_ref[...].astype(f32)
    first, last = seg_bounds(info_ref, chunk)
    rows = row_ids()
    wide = 256
    masks = [None] + [
        jnp.broadcast_to(flag(rows - back >= first), (CHUNK, wide)) for back in range(1, WIDTH)
    ]
    for lo in range(0, u_ref.shape[1], wide):
        pre = conv_pre(ext, cw_ref, masks, lo, wide)
        s = sigmoid(pre)
        act = pre * s
        acts_ref[:, lo : lo + wide] = act.astype(bf16)
        slope_ref[:, lo : lo + wide] = (s + act * (1.0 - s)).astype(bf16)

    member = head_map(heads)
    dt = softplus(dtr_ref[...] + hp_ref[0:1, :])
    rate = jnp.exp(hp_ref[1:2, :]) * LOG2E
    logs = running(triangle(False, False), -dt * rate)
    dt_ref[...] = dt
    log_ref[...] = logs
    tail = logs[CHUNK - 1 : CHUNK, :]
    keep_in = flag(first < 0)
    keep_out = flag(last >= CHUNK)
    dt_all = spread(dt, member)
    out_all = spread(jnp.exp2(tail - logs) * keep_out, member)
    into_all = spread(jnp.exp2(logs) * keep_in, member)
    wide_ref[:, 0:inner] = dt_all.astype(bf16)
    wide_ref[:, inner : 2 * inner] = out_all.astype(bf16)
    wide_ref[:, 2 * inner :] = into_all.astype(bf16)
    x_in = (acts_ref[:, 0:inner].astype(f32) * (dt_all * out_all)).astype(bf16)
    b_cols = jnp.transpose(acts_ref[:, inner : inner + STATE].astype(f32)).astype(bf16)
    local = nn(b_cols, x_in)
    decay_all = into_all[CHUNK - 1 : CHUNK, :]
    sloc_ref[...] = held[...].astype(bf16)[None]
    held[...] = decay_all * held[...] + local
    drun[...] = drun[...] * decay_all

    @pl.when(chunk == pl.num_programs(0) - 1)
    def _():
        total = drun[...]
        high = total.astype(bf16)
        send_ref[0:STATE, :] = held[...].astype(bf16)
        send_ref[STATE:, :] = jnp.concatenate(
            [total, total - high.astype(f32)], axis=0
        ).astype(bf16)


def mix_kernel(
    acts_ref, dt_ref, log_ref, sloc_ref, sin_ref, z_ref, gg_ref, gain_ref, hp_ref, info_ref,
    y_ref, sent_ref, sums_ref,
    dpre,
):
    chunk = pl.program_id(0)
    heads = log_ref.shape[1]
    inner = heads * HEAD_DIM
    member = head_map(heads)

    @pl.when(chunk == 0)
    def _():
        dpre[...] = jnp.ones_like(dpre)

    first, _ = seg_bounds(info_ref, chunk)
    rows = lax.broadcasted_iota(jnp.int32, (CHUNK, CHUNK), 0)
    cols = lax.broadcasted_iota(jnp.int32, (CHUNK, CHUNK), 1)
    b = acts_ref[:, inner : inner + STATE]
    c = acts_ref[:, inner + STATE :]
    mixed = jnp.where((cols <= rows) & (cols >= first), nt(c, b), 0.0)
    logs = log_ref[...]
    logs_t = jnp.transpose(logs)
    decay = jnp.exp2(logs[CHUNK - 1 : CHUNK, :]) * flag(first < 0)[CHUNK - 1 : CHUNK, :]
    state = sloc_ref[0].astype(f32) + spread_row(dpre[0:1, :], member) * sin_ref[...]
    dpre[...] = dpre[...] * decay
    state_low = state.astype(bf16)
    state_rest = (state - state_low.astype(f32)).astype(bf16)
    sent_ref[...] = state_low[None]
    x = acts_ref[:, 0:inner].astype(f32)
    xd = x * dt_ref[...].astype(f32)
    skip = spread_row(hp_ref[2:3, :], member)
    into = spread(jnp.exp2(logs) * flag(first < 0), member)
    carried = into * (nn(c, state_low) + nn(c, state_rest)) + skip * x
    lane = lax.broadcasted_iota(jnp.int32, (1, 2 * HEAD_DIM), 1)
    left = flag(lane < HEAD_DIM)
    right = 1.0 - left
    squares = jnp.zeros((CHUNK, 2 * HEAD_DIM), f32)
    dots = jnp.zeros((CHUNK, 2 * HEAD_DIM), f32)
    for pair in range(heads // 2):
        mats = []
        for h in (2 * pair, 2 * pair + 1):
            gap = logs[:, h : h + 1] - logs_t[h : h + 1, :]
            mats.append((jnp.exp2(jnp.minimum(gap, 0.0)) * mixed).astype(bf16))
        at = slice(2 * pair * HEAD_DIM, 2 * (pair + 1) * HEAD_DIM)
        xp = xd[:, at]
        block = jnp.concatenate([(xp * left).astype(bf16), (xp * right).astype(bf16)], axis=0)
        y = carried[:, at] + nn(jnp.concatenate(mats, axis=1), block)
        y_ref[:, at] = y
        z = z_ref[:, at].astype(f32)
        gated = y * (z * sigmoid(z))
        squares = squares + gated * gated
        dots = dots + gated * (gg_ref[:, at].astype(f32) * gain_ref[:, at])
    lane = lax.broadcasted_iota(jnp.int32, (CHUNK, STATE), 1)
    both = jnp.where(
        lane == 0, jnp.sum(squares, axis=1, keepdims=True),
        jnp.where(lane == 1, jnp.sum(dots, axis=1, keepdims=True), 0.0),
    )
    sums_ref[...] = jnp.transpose(both)[0:PAD][None]


def gate_back_kernel(
    y_ref, z_ref, gg_ref, sums_ref, gain_ref, xa_ref, c_ref, into_ref, log_ref, info_ref, fade_ref,
    gn_ref, gz_ref, gy_ref, lloc_ref, send_ref, ggain_ref, gskip_ref,
    held, *, inner_all,
):
    step = pl.program_id(0)
    chunk = pl.num_programs(0) - 1 - step
    heads = log_ref.shape[1]
    member = head_map(heads)

    @pl.when(step == 0)
    def _():
        held[...] = jnp.zeros_like(held)
        ggain_ref[...] = jnp.zeros_like(ggain_ref)
        gskip_ref[...] = jnp.zeros_like(gskip_ref)

    sums = jnp.transpose(jnp.concatenate([sums_ref[0]] * (CHUNK // PAD), axis=0))
    scale = lax.rsqrt(sums[:, 0:1] * (1.0 / inner_all) + eps)
    mean = sums[:, 1:2] * scale * (1.0 / inner_all)
    z = z_ref[...].astype(f32)
    y = y_ref[...]
    s = sigmoid(z)
    act = z * s
    gain = gain_ref[...]
    gg = gg_ref[...].astype(f32)
    unit = y * act * scale
    gn_ref[...] = (unit * gain).astype(bf16)
    ggain_ref[...] += jnp.sum(gg * unit, axis=0, keepdims=True)
    g_gated = scale * (gg * gain - unit * mean)
    gz_ref[...] = (g_gated * y * s * (1.0 + z * (1.0 - s))).astype(bf16)
    gy = g_gated * act
    gy_ref[...] = gy.astype(bf16)
    gskip_ref[...] += jnp.sum(gy * xa_ref[...].astype(f32), axis=0, keepdims=True)
    first, _ = seg_bounds(info_ref, chunk)
    decay = jnp.exp2(log_ref[CHUNK - 1 : CHUNK, :]) * flag(first < 0)[CHUNK - 1 : CHUNK, :]
    weighted = (gy * into_ref[...].astype(f32)).astype(bf16)
    c_cols = jnp.transpose(c_ref[...].astype(f32)).astype(bf16)
    lloc_ref[...] = held[...].astype(bf16)[None]
    held[...] = spread_row(decay, member) * held[...] + nn(c_cols, weighted)

    @pl.when(step == pl.num_programs(0) - 1)
    def _():
        send_ref[0:STATE, :] = held[...].astype(bf16)
        send_ref[STATE:, :] = fade_ref[...]


def bwd_kernel(*refs):
    (
        gy_ref, acts_ref, slope_ref, dt_ref, log_ref, dtr_ref, dtw_ref, outw_ref, into_ref,
        sent_ref, lloc_ref, lin_ref, u_ref, halo_ref, cw_ref, hp_ref, info_ref,
    ) = refs[:17]
    (
        gu_ref, gdt_ref, tail_ref, hg_ref, gc_ref, ghead_ref, dsuf, gext, rows_scr, head_ext, keys,
    ) = refs[17:]
    step = pl.program_id(0)
    chunk = pl.num_programs(0) - 1 - step
    inner = gy_ref.shape[1]
    heads = log_ref.shape[1]
    member = head_map(heads)
    total_cols = inner + 2 * STATE

    @pl.when(step == 0)
    def _():
        dsuf[...] = jnp.ones_like(dsuf)
        gc_ref[...] = jnp.zeros_like(gc_ref)
        ghead_ref[...] = jnp.zeros_like(ghead_ref)
        gext[CHUNK:, :] = jnp.zeros((PAD, total_cols), f32)

    @pl.when(step > 0)
    def _():
        gext[CHUNK:, :] = gext[0:PAD, :]

    first, last = seg_bounds(info_ref, chunk)
    logs = log_ref[...]
    logs_t = jnp.transpose(logs)
    dt = dt_ref[...]
    decay = jnp.exp2(logs[CHUNK - 1 : CHUNK, :]) * flag(first < 0)[CHUNK - 1 : CHUNK, :]
    rate = jnp.exp(hp_ref[1:2, :])

    b = acts_ref[:, inner : inner + STATE]
    c = acts_ref[:, inner + STATE :]
    rows = lax.broadcasted_iota(jnp.int32, (CHUNK, CHUNK), 0)
    cols = lax.broadcasted_iota(jnp.int32, (CHUNK, CHUNK), 1)
    keep = (cols >= rows) & (cols < last)
    mixed = jnp.where(keep, nt(b, c), 0.0)

    lam = lloc_ref[0].astype(f32) + spread_row(dsuf[0:1, :], member) * lin_ref[...]
    lam_low = lam.astype(bf16)
    dsuf[...] = dsuf[...] * decay
    state = sent_ref[0]
    decay_sum = jnp.sum(lam * state.astype(f32), axis=0, keepdims=True) * spread_row(decay, member)
    z_head = per_head(jnp.broadcast_to(decay_sum, (PAD, inner)), member)[0:1]

    gy_low = gy_ref[...]
    gy = gy_low.astype(f32)
    dt_all = dtw_ref[...].astype(f32)
    out_all = outw_ref[...].astype(f32)
    xd_low = (acts_ref[:, 0:inner].astype(f32) * dt_all).astype(bf16)
    xd = xd_low.astype(f32)
    g_out = out_all * nn(b, lam_low)
    e_head = per_head(xd * g_out, member)
    gy_in = gy * into_ref[...].astype(f32)
    f_head = per_head(gy_in * nn(c, state), member)
    g_c = nt(gy_in.astype(bf16), state)
    g_b = nt((xd * out_all).astype(bf16), lam_low)
    skip = spread_row(hp_ref[2:3, :], member)

    lane = lax.broadcasted_iota(jnp.int32, (1, 2 * HEAD_DIM), 1)
    left = flag(lane < HEAD_DIM).astype(bf16)
    right = flag(lane >= HEAD_DIM).astype(bf16)
    mixed2 = jnp.concatenate([mixed, mixed], axis=1)
    d_mixed = jnp.zeros((CHUNK, 2 * CHUNK), f32)
    for pair in range(heads // 2):
        at = slice(2 * pair * HEAD_DIM, 2 * (pair + 1) * HEAD_DIM)
        gyp = gy_low[:, at]
        block = jnp.concatenate([gyp * left, gyp * right], axis=0)
        d_m = nt(xd_low[:, at], block)
        gaps = [logs_t[h : h + 1, :] - logs[:, h : h + 1] for h in (2 * pair, 2 * pair + 1)]
        decays = jnp.exp2(jnp.minimum(jnp.concatenate(gaps, axis=1), 0.0))
        d_mixed = d_mixed + d_m * decays
        weights = (decays * mixed2).astype(bf16)
        g_in = nn(weights, block)
        r_pair = jnp.sum(weights.astype(f32) * d_m, axis=0, keepdims=True)
        rows_scr[2 * pair : 2 * pair + 1, :] = r_pair[:, 0:CHUNK]
        rows_scr[2 * pair + 1 : 2 * pair + 2, :] = r_pair[:, CHUNK:]
        k_pair = xd[:, at] * g_in
        k_high = k_pair.astype(bf16)
        keys[0:CHUNK, at] = k_high
        keys[CHUNK:, at] = (k_pair - k_high.astype(f32)).astype(bf16)
        gext[0:CHUNK, at] = dt_all[:, at] * (g_in + g_out[:, at]) + skip[:, at] * gy[:, at]
    d_mixed = jnp.where(keep, d_mixed[:, 0:CHUNK] + d_mixed[:, CHUNK:], 0.0)
    g_b = g_b + nn(d_mixed.astype(bf16), c)
    g_c = g_c + nn(jnp.transpose(d_mixed).astype(bf16), b)
    gext[0:CHUNK, inner : inner + STATE] = g_b
    gext[0:CHUNK, inner + STATE :] = g_c

    k_both = per_head(keys[...], member)
    k_head = k_both[0:CHUNK] + k_both[CHUNK:]
    r_head = jnp.transpose(rows_scr[...])[:, 0:heads]
    g_log = r_head - k_head + f_head
    g_a = running(triangle(False, True), g_log) + running(triangle(True, False), e_head) + z_head
    v = dtr_ref[...] + hp_ref[0:1, :]
    gate = sigmoid(v)
    ratio = jnp.where(v < -20.0, 1.0, gate / dt)
    g_dt = ratio * (k_head + e_head) - (rate * gate) * g_a
    gdt_ref[...] = g_dt.astype(bf16)
    ghead_ref[0:1, :] += jnp.sum(g_dt, axis=0, keepdims=True)
    ghead_ref[1:2, :] += -rate * jnp.sum(dt * g_a, axis=0, keepdims=True)

    wide = 256
    ids = row_ids()
    ahead = [None] + [
        jnp.broadcast_to(flag(ids + back < last), (CHUNK, wide)) for back in range(1, WIDTH)
    ]
    start = chunk == 0
    for lo in range(0, total_cols, wide):
        here = slice(lo, lo + wide)
        g_pre = gext[0:CHUNK, here] * slope_ref[:, here].astype(f32)
        gext[0:CHUNK, here] = g_pre
        u = u_ref[:, here].astype(f32)
        gc_ref[WIDTH : WIDTH + 1, here] += jnp.sum(g_pre, axis=0, keepdims=True)
        gc_ref[WIDTH - 1 : WIDTH, here] += jnp.sum(g_pre * u, axis=0, keepdims=True)
        g_u = cw_ref[WIDTH - 1 : WIDTH, here] * g_pre
        for back in range(1, WIDTH):
            tap = WIDTH - 1 - back
            later = gext[back : back + CHUNK, here] * ahead[back]
            gc_ref[tap : tap + 1, here] += jnp.sum(later * u, axis=0, keepdims=True)
            g_u = g_u + cw_ref[tap : tap + 1, here] * later
        gu_ref[:, here] = g_u.astype(bf16)

        @pl.when(step == 0)
        def _(g_u=g_u, here=here):
            tail_ref[:, here] = g_u[CHUNK - HALO :, :]
            gu_ref[CHUNK - HALO :, here] = jnp.zeros((HALO, wide), bf16)

        @pl.when(start)
        def _(g_pre=g_pre, here=here):
            halo = jnp.zeros((PAD, wide), f32)
            u_before = halo_ref[:, here].astype(f32)[HALO - PAD : HALO]
            head_ext[0:PAD, :] = jnp.zeros((PAD, wide), f32)
            near = lax.broadcasted_iota(jnp.int32, (PAD, 1), 0)
            for back in range(1, WIDTH):
                tap = WIDTH - 1 - back
                head_ext[PAD:, :] = g_pre[0:PAD, :] * flag(near - back >= first[0:PAD, :])
                later = head_ext[back : back + PAD, :]
                gc_ref[tap : tap + 1, here] += jnp.sum(later * u_before, axis=0, keepdims=True)
                halo = halo + cw_ref[tap : tap + 1, here] * later
            hg_ref[0:PAD, here] = jnp.zeros((PAD, wide), f32)
            hg_ref[PAD:, here] = halo


def put_halves(kept_ref, given_ref, value, parity, blocks):
    wide = value.shape[1] // blocks
    halves = [
        jnp.concatenate([value[:, i * wide : (i + 1) * wide] for i in range(odd, blocks, 2)], axis=1)
        for odd in range(2)
    ]

    @pl.when(parity == 0)
    def _():
        kept_ref[...] = halves[0]
        given_ref[...] = halves[1]

    @pl.when(parity == 1)
    def _():
        kept_ref[...] = halves[1]
        given_ref[...] = halves[0]


def fold_kernel(parity_ref, kept_ref, arrived_ref, keep_ref, give_ref):
    total = kept_ref[...].astype(f32) + arrived_ref[...].astype(f32)
    half = total.shape[1] // 2

    @pl.when(parity_ref[0] == 0)
    def _():
        keep_ref[...] = total[:, :half]
        give_ref[...] = total[:, half:].astype(bf16)

    @pl.when(parity_ref[0] == 1)
    def _():
        keep_ref[...] = total[:, half:]
        give_ref[...] = total[:, :half].astype(bf16)


def tn(a, b):
    return lax.dot_general(a, b, (((0,), (0,)), ((), ())), preferred_element_type=f32)


def early_kernel(cot_ref, normed_ref, gn_ref, gz_ref, out_ref):
    inner = gn_ref.shape[1]
    out_ref[:, 0:inner] = tn(cot_ref[...], gn_ref[...]).astype(bf16)
    out_ref[:, inner:] = tn(normed_ref[...], gz_ref[...]).astype(bf16)


def branch_kernel(parity_ref, gn_ref, w_ref, kept_ref, given_ref, *, blocks):
    put_halves(kept_ref, given_ref, nn(gn_ref[...], w_ref[...]).astype(bf16), parity_ref[0], blocks)


def normed_back_kernel(
    parity_ref, gu_ref, gdt_ref, gz_ref, x_ref, scale_ref, gain_ref, wx_ref, wbc_ref, wdt_ref,
    kept_ref, given_ref, dots_ref, ggain_ref, *, blocks,
):
    inner = wx_ref.shape[2]

    @pl.when(pl.program_id(0) == 0)
    def _():
        ggain_ref[...] = jnp.zeros_like(ggain_ref)

    total = gz_ref[...].astype(f32) + nt(gu_ref[:, 0:inner], wx_ref[0])
    total = total + nt(gu_ref[:, inner:], wbc_ref[...]) + nn(gdt_ref[...], wdt_ref[...])
    unit = x_ref[...].astype(f32) * scale_ref[...]
    with_unit = total * unit
    ggain_ref[...] += jnp.sum(with_unit, axis=0, keepdims=True)
    dots = jnp.sum(with_unit * gain_ref[...], axis=1, keepdims=True)
    dots_ref[...] = jnp.transpose(jnp.broadcast_to(dots, (dots.shape[0], 128)))[0:PAD][None]
    put_halves(kept_ref, given_ref, total.astype(bf16), parity_ref[0], blocks)


def along(value, axis, distance):
    count = lax.axis_size(axis)
    route = [(i, i + distance) for i in range(count) if 0 <= i + distance < count]
    return lax.ppermute(value, axis, route)


def swapped(value, axis, bit):
    return lax.ppermute(value, axis, [(i, i ^ bit) for i in range(lax.axis_size(axis))])


def all_sum(value, axis):
    bit = 1
    while bit < lax.axis_size(axis):
        value = value + swapped(value, axis, bit)
        bit *= 2
    return value


def sum_pairs(value, axis):
    parts = [swapped(value, axis, mask) for mask in range(1, lax.axis_size(axis))]
    return value + sum(parts[1:], parts[0])


def summed(blocks):
    total = blocks[0].astype(f32)
    for block in blocks[1:]:
        total = total + block.astype(f32)
    return total


def halves_of(parts, axis, bit):
    upper = (lax.axis_index(axis) & bit) != 0
    kept = [jnp.where(upper, b, a) for a, b in zip(parts[0::2], parts[1::2])]
    given = [jnp.where(upper, a, b) for a, b in zip(parts[0::2], parts[1::2])]
    return kept, given


class Last:

    def __init__(self, kept, arrived, axis, pieces):
        parts = jnp.split(kept.astype(f32) + arrived.astype(f32), lax.axis_size(axis) // 2, axis=1)
        bit = 2
        while True:
            keep, give = halves_of(parts, axis, bit)
            give = jnp.concatenate(give, axis=1).astype(bf16)
            if 2 * bit >= lax.axis_size(axis):
                break
            other = jnp.split(swapped(give, axis, bit), len(keep), axis=1)
            parts = [k + o.astype(f32) for k, o in zip(keep, other)]
            bit *= 2
        self.axis, self.bit, self.keep = axis, bit, keep[0]
        rows = give.shape[0] // pieces
        self.give = [give[i * rows : (i + 1) * rows] for i in range(pieces)]

    def send(self, piece):
        return swapped(self.give[piece], self.axis, self.bit)

    def total(self, arrived):
        return self.keep + jnp.concatenate(arrived, axis=0).astype(f32)


def ring_order(count):
    return list(range(0, count, 2)) + list(range(count - 1, 0, -2))


def dealt(value, axis):
    return lax.all_to_all(value, axis, 0, 0, tiled=True)


def repeated(value, count):
    return jnp.broadcast_to(value[None], (count,) + value.shape)


def grouped_send(value, axis):
    count = lax.axis_size(axis) // 2
    me = lax.axis_index(axis) >> 1
    rows = value.shape[0] // count
    own = lax.dynamic_slice_in_dim(value, me * rows, rows, 0)
    return [own] + [
        swapped(lax.dynamic_slice_in_dim(value, (me ^ mask) * rows, rows, 0), axis, 2 * mask)
        for mask in range(1, count)
    ]


class Ring:

    def __init__(self, values, axis):
        count = lax.axis_size(axis)
        self.values, self.axis, self.count, self.hop = values, axis, count, 0
        self.order = ring_order(count)
        me = lax.axis_index(axis)
        self.spot = jnp.where(me % 2 == 0, me // 2, count - (me + 1) // 2)
        self.moving = self.mine()

    def signs(self):
        return [1 - 2 * (i % 2) for i in range(len(self.values))]

    def mine(self):
        blocks = []
        for value, sign in zip(self.values, self.signs()):
            rows = value.shape[0] // self.count
            ahead = sign * (self.count - 1 - self.hop)
            spot = (self.spot + ahead + 2 * self.count) % self.count
            owner = jnp.where(spot < self.count // 2, 2 * spot, 2 * (self.count - spot) - 1)
            blocks.append(lax.dynamic_slice_in_dim(value, owner * rows, rows, 0))
        return blocks

    def send(self):
        arrived = []
        for block, sign in zip(self.moving, self.signs()):
            route = [
                (self.order[i], self.order[(i + sign) % self.count]) for i in range(self.count)
            ]
            arrived.append(lax.ppermute(block, self.axis, route))
        return arrived

    def add(self, arrived):
        self.hop += 1
        blocks = [a.astype(f32) + b.astype(f32) for a, b in zip(arrived, self.mine())]
        done = self.hop == self.count - 1
        self.moving = blocks if done else [block.astype(bf16) for block in blocks]
        return done


def scatter_direct(value, axis):
    count = lax.axis_size(axis)
    me = lax.axis_index(axis)
    wide = value.shape[1] // count
    own = lax.dynamic_slice_in_dim(value, me * wide, wide, 1)
    return summed([own] + [
        swapped(lax.dynamic_slice_in_dim(value, (me ^ mask) * wide, wide, 1), axis, mask)
        for mask in range(1, count)
    ])


def gather_direct(value, axis):
    count = lax.axis_size(axis)
    me = lax.axis_index(axis)
    parts = [value] + [swapped(value, axis, mask) for mask in range(1, count)]
    ordered = []
    for place in range(count):
        part = parts[place]
        for mask in range(1, count):
            part = jnp.where(me == mask, parts[place ^ mask], part)
        ordered.append(part)
    return jnp.concatenate(ordered, axis=1)


def all_sum_low(value, axis):
    bit = 1
    while bit < lax.axis_size(axis):
        value = value + swapped(value.astype(bf16), axis, bit).astype(f32)
        bit *= 2
    return value


def call(kernel, grid, in_specs, out_specs, out_shape, scratch, micros, vmem, **names):
    return pl.pallas_call(
        kernel,
        grid=grid,
        in_specs=in_specs,
        out_specs=out_specs,
        out_shape=out_shape,
        scratch_shapes=scratch,
        compiler_params=pltpu.CompilerParams(
            dimension_semantics=("arbitrary",), vmem_limit_bytes=vmem * 1024 * 1024
        ),
        cost_estimate=pl.CostEstimate(
            flops=micros * 10**9, bytes_accessed=micros * 10**6, transcendentals=0
        ),
        **names,
    )


def together(*values):
    return lax.optimization_barrier(values)


def per_device(
    x_in, norm_gain, w_zx, w_bc, w_dt, conv_x, conv_bc, head_params, gate_gain, w_out, lengths,
    grad_out,
):
    tokens, width = x_in.shape
    heads = head_params.shape[1]
    inner = gate_gain.shape[0]
    members = lax.axis_size("tensor")
    devices = lax.axis_size("seq")
    inner_all = inner * members
    total_cols = inner + 2 * STATE
    chunks = tokens // CHUNK
    reach = min(-(-REACH // tokens), devices - 1)
    device = lax.axis_index("seq")
    member = lax.axis_index("tensor")

    shape = jax.ShapeDtypeStruct
    rows = lambda wide: pl.BlockSpec((CHUNK, wide), lambda i: (i, 0))
    back = lambda wide: pl.BlockSpec((CHUNK, wide), lambda i: (chunks - 1 - i, 0))
    whole = lambda *dims: pl.BlockSpec(dims, lambda i: (0,) * len(dims))
    stack = lambda *dims: pl.BlockSpec((1,) + dims, lambda i: (i,) + (0,) * len(dims))
    stack_back = lambda *dims: pl.BlockSpec(
        (1,) + dims, lambda i: (chunks - 1 - i,) + (0,) * len(dims)
    )
    c_at = inner // STATE + 1
    c_rows = pl.BlockSpec((CHUNK, STATE), lambda i: (i, c_at))
    c_back = pl.BlockSpec((CHUNK, STATE), lambda i: (chunks - 1 - i, c_at))

    ends = jnp.cumsum(lengths)
    starts = ends - lengths
    places = device * tokens + jnp.arange(tokens, dtype=jnp.int32)[:, None]
    seg_first = jnp.max(jnp.where(starts[None, :] <= places, starts[None, :], 0), axis=1)
    seg_last = jnp.min(
        jnp.where(ends[None, :] > places, ends[None, :], jnp.iinfo(jnp.int32).max // 2), axis=1
    )
    info = jnp.stack([seg_first, seg_last], axis=1) - device * tokens

    cotangent = lax.all_gather(grad_out, "tensor", axis=1, tiled=True)

    x_halo = along(x_in[tokens - HALO :], "seq", 1)
    w_both = lax.optimization_barrier(jnp.transpose(w_zx, (1, 0, 2)))
    block = 256
    tile = lambda wide: pl.BlockSpec((block, wide), lambda i: (i, 0))
    normed, x_scale, u, halo, dt_raw = call(
        project_kernel, (tokens // block,),
        [tile(width), whole(HALO, width), whole(1, width),
         pl.BlockSpec((1, width, inner), lambda i: (1, 0, 0)), whole(width, 2 * STATE),
         whole(heads, width)],
        [tile(width), tile(1), tile(total_cols), whole(HALO, total_cols), tile(heads)],
        [shape((tokens, width), bf16), shape((tokens, 1), f32),
         shape((tokens, total_cols), bf16), shape((HALO, total_cols), bf16),
         shape((tokens, heads), f32)],
        [], 10, 56, name="project",
    )(x_in, x_halo, norm_gain[None, :], w_both, w_bc, w_dt.T)
    conv_w = jnp.concatenate([conv_x, conv_bc], axis=1)

    acts, slope, dt, logs, spread_out, local_in, leaving = call(
        fwd_kernel, (chunks,),
        [rows(total_cols), whole(HALO, total_cols), whole(WIDTH + 1, total_cols), rows(heads),
         whole(3, heads), rows(2)],
        [rows(total_cols), rows(total_cols), rows(heads), rows(heads), rows(3 * inner),
         stack(STATE, inner), whole(STATE + 2 * PAD, inner)],
        [shape((tokens, total_cols), bf16), shape((tokens, total_cols), bf16),
         shape((tokens, heads), f32), shape((tokens, heads), f32),
         shape((tokens, 3 * inner), bf16), shape((chunks, STATE, inner), bf16),
         shape((STATE + 2 * PAD, inner), bf16)],
        [pltpu.VMEM((CHUNK + PAD, total_cols), f32), pltpu.VMEM((STATE, inner), f32),
         pltpu.VMEM((PAD, inner), f32)],
        12, 56, name="conv_states",
    )(u, halo, conv_w, dt_raw, head_params, info)
    spread_rows = lambda which: pl.BlockSpec((CHUNK, inner), lambda i: (i, which))
    spread_back = lambda which: pl.BlockSpec((CHUNK, inner), lambda i: (chunks - 1 - i, which))

    def unpacked(sent):
        low = sent[STATE:].astype(f32)
        return sent[:STATE].astype(f32), low[0:1] + low[PAD : PAD + 1]

    def joined(sent, arrived):
        state, fade = unpacked(sent)
        before, fade_before = unpacked(arrived)
        state, fade = state + fade * before, fade * fade_before
        high = fade.astype(bf16).astype(f32)
        rows = [jnp.broadcast_to(part, (PAD, inner)) for part in (high, fade - high)]
        return jnp.concatenate([state] + rows, axis=0).astype(bf16)

    def chained(sent, sign, first_work, second_work):
        arrived, first = together(along(sent, "seq", sign), first_work())
        pair = joined(sent, arrived)
        hops = [hop for hop in range(1, reach + 1, 2) if hop < devices]
        arrived, second = together(
            [along(pair, "seq", sign * hop) for hop in hops], second_work()
        )
        total = unpacked(arrived[-1])[0]
        for block in arrived[-2::-1]:
            state, fade = unpacked(block)
            total = state + fade * total
        return total, first, second

    back_dims = (((1,), (1,)), ((), ()))
    weight_dims = (((0,), (0,)), ((), ()))
    low = lambda a, b, dims: lax.dot_general(a, b, dims, preferred_element_type=f32).astype(bf16)
    wide = lambda a, b, dims: lax.dot_general(a, b, dims, preferred_element_type=f32)

    state_in, grad_gate, gate_in = chained(
        leaving, 1,
        lambda: low(cotangent, w_out, back_dims),
        lambda: low(normed, w_both[0], (((1,), (0,)), ((), ()))),
    )

    gain_row = gate_gain[None, :]
    mixed, entering, sums = call(
        mix_kernel, (chunks,),
        [rows(total_cols), spread_rows(0), rows(heads), stack(STATE, inner),
         whole(STATE, inner), rows(inner), rows(inner), whole(1, inner), whole(3, heads), rows(2)],
        [rows(inner), stack(STATE, inner), stack(PAD, CHUNK)],
        [shape((tokens, inner), f32), shape((chunks, STATE, inner), bf16),
         shape((chunks, PAD, CHUNK), f32)],
        [pltpu.VMEM((PAD, heads), f32)], 15, 14, name="mix",
    )(acts, spread_out, logs, local_in, state_in, gate_in, grad_gate, gain_row,
      head_params, info)

    gate_rows = sum_pairs(sums, "tensor")

    gate_normed, grad_gate_in, grad_mixed, grad_local, grad_leaving, grad_gain, grad_skip = call(
        partial(gate_back_kernel, inner_all=inner_all), (chunks,),
        [back(inner), back(inner), back(inner), stack_back(PAD, CHUNK), whole(1, inner),
         back(inner), c_back, spread_back(2), back(heads), back(2),
         pl.BlockSpec((2 * PAD, inner), lambda i: (STATE // (2 * PAD), 0))],
        [back(inner), back(inner), back(inner), stack_back(STATE, inner),
         whole(STATE + 2 * PAD, inner), whole(1, inner), whole(1, inner)],
        [shape((tokens, inner), bf16), shape((tokens, inner), bf16), shape((tokens, inner), bf16),
         shape((chunks, STATE, inner), bf16), shape((STATE + 2 * PAD, inner), bf16),
         shape((1, inner), f32), shape((1, inner), f32)],
        [pltpu.VMEM((STATE, inner), f32)], 12, 14, name="gate_back",
    )(mixed, gate_in, grad_gate, gate_rows, gain_row, acts, acts, spread_out, logs, info, leaving)

    tall = lambda cols: pl.BlockSpec((tokens, cols), lambda i: (0, i))
    grad_in, grad_normed_z, early = chained(
        grad_leaving, -1,
        lambda: low(grad_gate_in, w_both[0], back_dims),
        lambda: call(
            early_kernel, (width // 512,),
            [tall(512), tall(512), whole(tokens, inner), whole(tokens, inner)],
            pl.BlockSpec((512, 2 * inner), lambda i: (i, 0)), shape((width, 2 * inner), bf16), [],
            14, 20, name="early",
        )(cotangent, normed, gate_normed, grad_gate_in),
    )
    early, grad_in = together(early, grad_in)
    early_sum = lax.psum_scatter(early, "seq", scatter_dimension=0, tiled=True)

    part = back
    grad_u, grad_dt, tail, sent, grad_conv, grad_heads = call(
        bwd_kernel, (chunks,),
        [part(inner), part(total_cols), part(total_cols), part(heads), part(heads),
         part(heads), spread_back(0), spread_back(1), spread_back(2),
         stack_back(STATE, inner), stack_back(STATE, inner), whole(STATE, inner),
         part(total_cols), whole(HALO, total_cols),
         whole(WIDTH + 1, total_cols), whole(3, heads), part(2)],
        [part(total_cols), part(heads), whole(HALO, total_cols), whole(HALO, total_cols),
         whole(PAD, total_cols), whole(PAD, heads)],
        [shape((tokens, total_cols), bf16), shape((tokens, heads), bf16),
         shape((HALO, total_cols), f32), shape((HALO, total_cols), f32),
         shape((PAD, total_cols), f32), shape((PAD, heads), f32)],
        [pltpu.VMEM((PAD, heads), f32), pltpu.VMEM((CHUNK + PAD, total_cols), f32),
         pltpu.VMEM((CHUNK, CHUNK), f32),
         pltpu.VMEM((2 * PAD, 256), f32), pltpu.VMEM((2 * CHUNK, inner), bf16)],
        30, 56, name="scan_back",
    )(grad_mixed, acts, slope, dt, logs, dt_raw, spread_out, spread_out, spread_out,
      entering, grad_local, grad_in, u, halo, conv_w, head_params, info)

    core = (member & 1).reshape(1)
    split_tile = pl.BlockSpec((2, block, width // 2), lambda i: (0, i, 0))
    own_bc = 2 * STATE // members

    slice_width = grad_out.shape[1]
    x_part = lax.dynamic_slice_in_dim(x_in, member * slice_width, slice_width, 1).astype(f32)
    parity = device & 1

    cuts = [0, inner // 4, inner // 2, inner]
    sent = along(sent, "seq", -1)
    late = low(normed, grad_u[:, :inner], weight_dims)
    late_blocks = late.reshape(devices // 2, 2, width // devices, inner)
    half_of = lambda odd: lax.dynamic_index_in_dim(late_blocks, odd, 1, False).reshape(-1, inner)
    given, kept = half_of(1 - parity), half_of(parity)
    given, kept, gate_normed = together(given, kept, gate_normed)
    piece_of = lambda at: swapped(given[:, cuts[at] : cuts[at + 1]], "seq", 1)
    branch_kept, branch_given = call(
        partial(branch_kernel, blocks=members), (tokens // block,),
        [pl.BlockSpec(memory_space=pltpu.SMEM), tile(inner), whole(inner, width)],
        [tile(width // 2)] * 2, [shape((tokens, width // 2), bf16)] * 2, [], 9, 56, name="branch",
    )(core, gate_normed, w_out)
    arrived_0, sent, branch_kept, branch_given = together(
        piece_of(0), sent, branch_kept, branch_given
    )
    tail = (tail + sent).astype(bf16)
    grad_u = lax.dynamic_update_slice_in_dim(grad_u, tail, tokens - HALO, 0)
    factors = jnp.concatenate([normed[tokens - HALO :], tail[:, :inner]], axis=1)
    factors = jnp.concatenate([factors, swapped(factors, "seq", 1)], axis=0)

    def first_work():
        return call(
            partial(normed_back_kernel, blocks=members), (tokens // block,),
            [pl.BlockSpec(memory_space=pltpu.SMEM), tile(total_cols), tile(heads), tile(width),
             tile(width), tile(1), whole(1, width),
             pl.BlockSpec((1, width, inner), lambda i: (1, 0, 0)), whole(width, 2 * STATE),
             whole(heads, width)],
            [tile(width // 2), tile(width // 2), pl.BlockSpec((1, PAD, block), lambda i: (i, 0, 0)), whole(1, width)],
            [shape((tokens, width // 2), bf16), shape((tokens, width // 2), bf16),
             shape((tokens // block, PAD, block), f32),
             shape((1, width), f32)],
            [], 15, 56, name="normed_back",
        )(core, grad_u, grad_dt, grad_normed_z, x_in, x_scale, norm_gain[None, :], w_both, w_bc,
          w_dt.T)

    grad_bc, arrived_1, (normed_kept, normed_given, dots_here, gain), factors = together(
        scatter_direct(grad_u[:, inner:], "tensor").astype(bf16), piece_of(1), first_work(), factors
    )

    def fold(kept, arrived):
        bit = 2
        while bit < members:
            wide_now = kept.shape[1]
            kept, given = call(
                fold_kernel, (tokens // block,),
                [pl.BlockSpec(memory_space=pltpu.SMEM), tile(wide_now), tile(wide_now)],
                [tile(wide_now // 2)] * 2,
                [shape((tokens, wide_now // 2), f32), shape((tokens, wide_now // 2), bf16)],
                [], 3, 12, name="fold",
            )(((member // bit) & 1).reshape(1), kept, arrived)
            bit *= 2
            if bit < members:
                arrived = swapped(given, "tensor", bit // 2)
        return kept, swapped(given, "tensor", bit // 2)


    def second_work():
        shared = jnp.concatenate(
            [grad_conv[: WIDTH + 1, inner:].reshape(-1), gain.reshape(-1)]
        ).reshape(-1, 128)
        return (
            sum_pairs(dots_here[:, 0], "tensor"), sum_pairs(shared, "tensor"),
            swapped(branch_given, "tensor", 1),
        )

    dots, shared, branch_other = together(*second_work())

    heads_here = jnp.concatenate(
        [grad_heads[:2], jnp.sum(grad_skip.reshape(heads, HEAD_DIM), axis=1)[None, :]], axis=0
    )
    own_small = jnp.concatenate(
        [grad_conv[: WIDTH + 1, :inner].reshape(-1), grad_gain.reshape(-1),
         heads_here.reshape(-1), jnp.zeros((-3 * heads % 128,), f32)]
    ).reshape(-1, 128)
    small = jnp.concatenate([shared, own_small], axis=0)
    high = small.astype(bf16)
    small = jnp.concatenate([high, (small - high.astype(f32)).astype(bf16)], axis=1)
    small_size = small.size
    block_cols = width // devices
    small = jnp.pad(small.reshape(-1), (0, -small_size % block_cols)).reshape(-1, block_cols)

    def third_work():
        both = jnp.concatenate([grad_bc, grad_dt], axis=1)
        bcdt = low(both, normed, weight_dims)
        blocks = jnp.transpose(bcdt.reshape(-1, devices, width // devices), (1, 0, 2))
        blocks = jnp.concatenate([blocks, repeated(small, devices)], axis=1)
        branch_keep, branch_sent = fold(branch_kept, branch_other)
        return (
            dealt(blocks, "seq"), branch_keep, branch_sent, swapped(normed_given, "tensor", 1),
        )

    bcdt, branch_keep, branch_sent, normed_other = together(*third_work())

    def fourth_work():
        total = summed(bcdt)
        normed_keep, normed_sent = fold(normed_kept, normed_other)
        block_out = (x_part + branch_keep + branch_sent.astype(f32)).astype(bf16)
        rows = repeated(total[:own_bc].astype(bf16).T, devices)
        return total, dealt(rows, "seq"), normed_keep, normed_sent, block_out

    bcdt, bc_rows, normed_keep, normed_sent, block_out, arrived_2 = together(
        *fourth_work(), piece_of(2)
    )
    arrived = jnp.concatenate([arrived_0, arrived_1, arrived_2], axis=1)
    rows_of = factors[:, :width].reshape(2 * HALO, devices // 2, 2, width // devices)
    rows_of = lax.dynamic_index_in_dim(rows_of, parity, 2, False).reshape(2 * HALO, -1)
    flying = (
        wide(rows_of, factors[:, width:], weight_dims) + kept.astype(f32) + arrived.astype(f32)
    ).astype(bf16)
    flying, bc_rows, normed_keep = together(flying, bc_rows, normed_keep)

    def fifth_work():
        grad_normed = normed_keep + normed_sent.astype(f32)
        gain_part = lax.dynamic_slice_in_dim(norm_gain, member * slice_width, slice_width, 0)
        row_mean = dots.reshape(tokens, 1) * (1.0 / width)
        grad_x = (
            x_scale * (grad_normed * gain_part[None, :] - x_part * x_scale * row_mean)
            + grad_out.astype(f32)
        )
        bc_all = gather_direct(bc_rows.reshape(width, own_bc), "tensor")
        return grad_x, bc_all

    sums, (grad_x, bc_all) = together(grouped_send(flying, "seq"), fifth_work())
    grad_w_bc = bc_all.astype(f32)
    late_sum = summed(sums)
    small = bcdt[own_bc + heads :].reshape(-1)[:small_size].reshape(-1, 256)
    small = small[:, 0:128] + small[:, 128:256]
    bcdt = bcdt[: own_bc + heads]
    early_sum = early_sum.astype(f32)
    grad_z_sum = early_sum[:, inner:]
    grad_w_out = early_sum[:, :inner].T

    grad_w_dt = bcdt[own_bc:].T

    shared, own = small[: shared.shape[0]].reshape(-1), small[shared.shape[0] :].reshape(-1)
    bc_size = (WIDTH + 1) * 2 * STATE
    x_size = (WIDTH + 1) * inner
    grad_conv_bc = shared[:bc_size].reshape(WIDTH + 1, 2 * STATE)
    grad_norm_gain = shared[bc_size:]
    grad_conv_x = own[:x_size].reshape(WIDTH + 1, inner)
    grad_gate_gain = own[x_size : x_size + inner]
    grad_head = own[x_size + inner : x_size + inner + 3 * heads].reshape(3, heads)

    grad_w_zx = jnp.stack([grad_z_sum, late_sum], axis=1)
    return (
        block_out, grad_x, grad_norm_gain, grad_w_zx, grad_w_bc, grad_w_dt, grad_conv_x,
        grad_conv_bc, grad_head, grad_gate_gain, grad_w_out,
    )


def solution(mesh):
    return jax.shard_map(
        per_device,
        mesh=mesh,
        in_specs=(
            P("seq", None), P(), P(None, None, "tensor"), P(), P(None, "tensor"),
            P(None, "tensor"), P(), P(None, "tensor"), P("tensor"), P("tensor", None), P(),
            P("seq", "tensor"),
        ),
        out_specs=(
            P("seq", "tensor"), P("seq", "tensor"), P(), P("seq", None, "tensor"), P(),
            P("seq", "tensor"), P(None, "tensor"), P(), P(None, "tensor"), P("tensor"),
            P("tensor", "seq"),
        ),
        check_vma=False,
    )
```

```python
from functools import partial

import jax
import jax.numpy as jnp
from jax import lax
from jax.experimental import pallas as pl
from jax.experimental.pallas import tpu as pltpu
from jax.sharding import PartitionSpec as P

HEAD_DIM = 64
STATE = 128
WIDTH = 4
CHUNK = 128
REACH = 4096
PAD = 8
HALO = 16
LOG2E = 1.4426950408889634

eps = 1e-05
f32 = jnp.float32
bf16 = jnp.bfloat16


def nn(a, b):
    return lax.dot_general(a, b, (((1,), (0,)), ((), ())), preferred_element_type=f32)


def nt(a, b):
    return lax.dot_general(a, b, (((1,), (1,)), ((), ())), preferred_element_type=f32)


def running(mask, v):
    wide = v.shape[1]
    high = v.astype(bf16)
    rest = v - high.astype(f32)
    mid = rest.astype(bf16)
    low = (rest - mid.astype(f32)).astype(bf16)
    out = nn(mask, jnp.concatenate([high, mid, low], axis=1))
    return out[:, 0:wide] + out[:, wide : 2 * wide] + out[:, 2 * wide : 3 * wide]


def head_map(heads):
    row = lax.broadcasted_iota(jnp.int32, (2 * heads, heads * HEAD_DIM), 0)
    col = lax.broadcasted_iota(jnp.int32, (2 * heads, heads * HEAD_DIM), 1)
    row = jnp.where(row >= heads, row - heads, row)
    return jnp.where((col >> 6) == row, 1.0, 0.0).astype(bf16)


def spread(v, member):
    high = v.astype(bf16)
    rest = (v - high.astype(f32)).astype(bf16)
    return nn(jnp.concatenate([high, rest], axis=1), member)


def spread_row(v, member):
    return spread(jnp.broadcast_to(v, (PAD, v.shape[1])), member)[0:1]


def per_head(v, member):
    return nt(v.astype(bf16), member[0 : member.shape[0] // 2])


def triangle(strict, upper):
    row = lax.broadcasted_iota(jnp.int32, (CHUNK, CHUNK), 0)
    col = lax.broadcasted_iota(jnp.int32, (CHUNK, CHUNK), 1)
    if upper:
        row, col = col, row
    keep = (row > col) if strict else (row >= col)
    return jnp.where(keep, 1.0, 0.0).astype(bf16)


def softplus(v):
    return jnp.maximum(v, 0.0) + jnp.log1p(jnp.exp(-jnp.abs(v)))


def sigmoid(v):
    return 0.5 * jnp.tanh(0.5 * v) + 0.5


def seg_bounds(info_ref, chunk):
    info = info_ref[...] - chunk * CHUNK
    return info[:, 0:1], info[:, 1:2]


def row_ids():
    return lax.broadcasted_iota(jnp.int32, (CHUNK, 1), 0)


def flag(v):
    return jnp.where(v, 1.0, 0.0).astype(f32)


def conv_pre(ext_ref, w_ref, masks, lo, wide):
    cols = taps = slice(lo, lo + wide)
    total = w_ref[WIDTH : WIDTH + 1, taps] + w_ref[WIDTH - 1 : WIDTH, taps] * ext_ref[
        PAD : PAD + CHUNK, cols
    ]
    for back in range(1, WIDTH):
        total = total + w_ref[WIDTH - 1 - back : WIDTH - back, taps] * (
            ext_ref[PAD - back : PAD - back + CHUNK, cols] * masks[back]
        )
    return total


def project_kernel(
    x_ref, xh_ref, gain_ref, wx_ref, wbc_ref, wdt_ref, normed_ref, scale_ref, u_ref, halo_ref, dtr_ref,
):
    count = x_ref.shape[0]
    x = jnp.concatenate([x_ref[...], xh_ref[...]], axis=0).astype(f32)
    scale = lax.rsqrt(jnp.mean(x * x, axis=1, keepdims=True) + eps)
    normed = (x * scale * gain_ref[...]).astype(bf16)
    scale_ref[...] = scale[:count]
    normed_ref[...] = normed[:count]
    inner = wx_ref.shape[2]
    u_x = nn(normed, wx_ref[0]).astype(bf16)
    u_bc = nn(normed, wbc_ref[...]).astype(bf16)
    u_ref[:, 0:inner] = u_x[:count]
    u_ref[:, inner:] = u_bc[:count]
    halo_ref[:, 0:inner] = u_x[count:]
    halo_ref[:, inner:] = u_bc[count:]
    dtr_ref[...] = nt(normed[:count], wdt_ref[...])


def fwd_kernel(
    u_ref, halo_ref, cw_ref, dtr_ref, hp_ref, info_ref,
    acts_ref, slope_ref, dt_ref, log_ref, wide_ref, sloc_ref, send_ref,
    ext, held, drun,
):
    chunk = pl.program_id(0)
    heads = dtr_ref.shape[1]
    inner = heads * HEAD_DIM

    @pl.when(chunk == 0)
    def _():
        ext[0:PAD, :] = halo_ref[...].astype(f32)[HALO - PAD : HALO]
        held[...] = jnp.zeros_like(held)
        drun[...] = jnp.ones_like(drun)

    @pl.when(chunk > 0)
    def _():
        ext[0:PAD, :] = ext[CHUNK : CHUNK + PAD, :]

    ext[PAD:, :] = u_ref[...].astype(f32)
    first, last = seg_bounds(info_ref, chunk)
    rows = row_ids()
    wide = 256
    masks = [None] + [
        jnp.broadcast_to(flag(rows - back >= first), (CHUNK, wide)) for back in range(1, WIDTH)
    ]
    for lo in range(0, u_ref.shape[1], wide):
        pre = conv_pre(ext, cw_ref, masks, lo, wide)
        s = sigmoid(pre)
        act = pre * s
        acts_ref[:, lo : lo + wide] = act.astype(bf16)
        slope_ref[:, lo : lo + wide] = (s + act * (1.0 - s)).astype(bf16)

    member = head_map(heads)
    dt = softplus(dtr_ref[...] + hp_ref[0:1, :])
    rate = jnp.exp(hp_ref[1:2, :]) * LOG2E
    logs = running(triangle(False, False), -dt * rate)
    dt_ref[...] = dt
    log_ref[...] = logs
    tail = logs[CHUNK - 1 : CHUNK, :]
    keep_in = flag(first < 0)
    keep_out = flag(last >= CHUNK)
    dt_all = spread(dt, member)
    out_all = spread(jnp.exp2(tail - logs) * keep_out, member)
    into_all = spread(jnp.exp2(logs) * keep_in, member)
    wide_ref[:, 0:inner] = dt_all.astype(bf16)
    wide_ref[:, inner : 2 * inner] = out_all.astype(bf16)
    wide_ref[:, 2 * inner :] = into_all.astype(bf16)
    x_in = (acts_ref[:, 0:inner].astype(f32) * (dt_all * out_all)).astype(bf16)
    b_cols = jnp.transpose(acts_ref[:, inner : inner + STATE].astype(f32)).astype(bf16)
    local = nn(b_cols, x_in)
    decay_all = into_all[CHUNK - 1 : CHUNK, :]
    sloc_ref[...] = held[...].astype(bf16)[None]
    held[...] = decay_all * held[...] + local
    drun[...] = drun[...] * decay_all

    @pl.when(chunk == pl.num_programs(0) - 1)
    def _():
        total = drun[...]
        high = total.astype(bf16)
        send_ref[0:STATE, :] = held[...].astype(bf16)
        send_ref[STATE:, :] = jnp.concatenate(
            [total, total - high.astype(f32)], axis=0
        ).astype(bf16)


def mix_kernel(
    acts_ref, dt_ref, log_ref, sloc_ref, sin_ref, z_ref, gg_ref, gain_ref, hp_ref, info_ref,
    y_ref, sent_ref, sums_ref,
    dpre,
):
    chunk = pl.program_id(0)
    heads = log_ref.shape[1]
    inner = heads * HEAD_DIM
    member = head_map(heads)

    @pl.when(chunk == 0)
    def _():
        dpre[...] = jnp.ones_like(dpre)

    first, _ = seg_bounds(info_ref, chunk)
    rows = lax.broadcasted_iota(jnp.int32, (CHUNK, CHUNK), 0)
    cols = lax.broadcasted_iota(jnp.int32, (CHUNK, CHUNK), 1)
    b = acts_ref[:, inner : inner + STATE]
    c = acts_ref[:, inner + STATE :]
    mixed = jnp.where((cols <= rows) & (cols >= first), nt(c, b), 0.0)
    logs = log_ref[...]
    logs_t = jnp.transpose(logs)
    decay = jnp.exp2(logs[CHUNK - 1 : CHUNK, :]) * flag(first < 0)[CHUNK - 1 : CHUNK, :]
    state = sloc_ref[0].astype(f32) + spread_row(dpre[0:1, :], member) * sin_ref[...]
    dpre[...] = dpre[...] * decay
    state_low = state.astype(bf16)
    state_rest = (state - state_low.astype(f32)).astype(bf16)
    sent_ref[...] = state_low[None]
    x = acts_ref[:, 0:inner].astype(f32)
    xd = x * dt_ref[...].astype(f32)
    skip = spread_row(hp_ref[2:3, :], member)
    into = spread(jnp.exp2(logs) * flag(first < 0), member)
    carried = into * (nn(c, state_low) + nn(c, state_rest)) + skip * x
    lane = lax.broadcasted_iota(jnp.int32, (1, 2 * HEAD_DIM), 1)
    left = flag(lane < HEAD_DIM)
    right = 1.0 - left
    squares = jnp.zeros((CHUNK, 2 * HEAD_DIM), f32)
    dots = jnp.zeros((CHUNK, 2 * HEAD_DIM), f32)
    for pair in range(heads // 2):
        mats = []
        for h in (2 * pair, 2 * pair + 1):
            gap = logs[:, h : h + 1] - logs_t[h : h + 1, :]
            mats.append((jnp.exp2(jnp.minimum(gap, 0.0)) * mixed).astype(bf16))
        at = slice(2 * pair * HEAD_DIM, 2 * (pair + 1) * HEAD_DIM)
        xp = xd[:, at]
        block = jnp.concatenate([(xp * left).astype(bf16), (xp * right).astype(bf16)], axis=0)
        y = carried[:, at] + nn(jnp.concatenate(mats, axis=1), block)
        y_ref[:, at] = y
        z = z_ref[:, at].astype(f32)
        gated = y * (z * sigmoid(z))
        squares = squares + gated * gated
        dots = dots + gated * (gg_ref[:, at].astype(f32) * gain_ref[:, at])
    lane = lax.broadcasted_iota(jnp.int32, (CHUNK, STATE), 1)
    both = jnp.where(
        lane == 0, jnp.sum(squares, axis=1, keepdims=True),
        jnp.where(lane == 1, jnp.sum(dots, axis=1, keepdims=True), 0.0),
    )
    sums_ref[...] = jnp.transpose(both)[0:PAD][None]


def gate_back_kernel(
    y_ref, z_ref, gg_ref, sums_ref, gain_ref, xa_ref, c_ref, into_ref, log_ref, info_ref, fade_ref,
    gn_ref, gz_ref, gy_ref, lloc_ref, send_ref, ggain_ref, gskip_ref,
    held, *, inner_all,
):
    step = pl.program_id(0)
    chunk = pl.num_programs(0) - 1 - step
    heads = log_ref.shape[1]
    member = head_map(heads)

    @pl.when(step == 0)
    def _():
        held[...] = jnp.zeros_like(held)
        ggain_ref[...] = jnp.zeros_like(ggain_ref)
        gskip_ref[...] = jnp.zeros_like(gskip_ref)

    sums = jnp.transpose(jnp.concatenate([sums_ref[0]] * (CHUNK // PAD), axis=0))
    scale = lax.rsqrt(sums[:, 0:1] * (1.0 / inner_all) + eps)
    mean = sums[:, 1:2] * scale * (1.0 / inner_all)
    z = z_ref[...].astype(f32)
    y = y_ref[...]
    s = sigmoid(z)
    act = z * s
    gain = gain_ref[...]
    gg = gg_ref[...].astype(f32)
    unit = y * act * scale
    gn_ref[...] = (unit * gain).astype(bf16)
    ggain_ref[...] += jnp.sum(gg * unit, axis=0, keepdims=True)
    g_gated = scale * (gg * gain - unit * mean)
    gz_ref[...] = (g_gated * y * s * (1.0 + z * (1.0 - s))).astype(bf16)
    gy = g_gated * act
    gy_ref[...] = gy.astype(bf16)
    gskip_ref[...] += jnp.sum(gy * xa_ref[...].astype(f32), axis=0, keepdims=True)
    first, _ = seg_bounds(info_ref, chunk)
    decay = jnp.exp2(log_ref[CHUNK - 1 : CHUNK, :]) * flag(first < 0)[CHUNK - 1 : CHUNK, :]
    weighted = (gy * into_ref[...].astype(f32)).astype(bf16)
    c_cols = jnp.transpose(c_ref[...].astype(f32)).astype(bf16)
    lloc_ref[...] = held[...].astype(bf16)[None]
    held[...] = spread_row(decay, member) * held[...] + nn(c_cols, weighted)

    @pl.when(step == pl.num_programs(0) - 1)
    def _():
        send_ref[0:STATE, :] = held[...].astype(bf16)
        send_ref[STATE:, :] = fade_ref[...]


def bwd_kernel(*refs):
    (
        gy_ref, acts_ref, slope_ref, dt_ref, log_ref, dtr_ref, dtw_ref, outw_ref, into_ref,
        sent_ref, lloc_ref, lin_ref, u_ref, halo_ref, cw_ref, hp_ref, info_ref,
    ) = refs[:17]
    (
        gu_ref, gdt_ref, tail_ref, hg_ref, gc_ref, ghead_ref, dsuf, gext, rows_scr, head_ext, keys,
    ) = refs[17:]
    step = pl.program_id(0)
    chunk = pl.num_programs(0) - 1 - step
    inner = gy_ref.shape[1]
    heads = log_ref.shape[1]
    member = head_map(heads)
    total_cols = inner + 2 * STATE

    @pl.when(step == 0)
    def _():
        dsuf[...] = jnp.ones_like(dsuf)
        gc_ref[...] = jnp.zeros_like(gc_ref)
        ghead_ref[...] = jnp.zeros_like(ghead_ref)
        gext[CHUNK:, :] = jnp.zeros((PAD, total_cols), f32)

    @pl.when(step > 0)
    def _():
        gext[CHUNK:, :] = gext[0:PAD, :]

    first, last = seg_bounds(info_ref, chunk)
    logs = log_ref[...]
    logs_t = jnp.transpose(logs)
    dt = dt_ref[...]
    decay = jnp.exp2(logs[CHUNK - 1 : CHUNK, :]) * flag(first < 0)[CHUNK - 1 : CHUNK, :]
    rate = jnp.exp(hp_ref[1:2, :])

    b = acts_ref[:, inner : inner + STATE]
    c = acts_ref[:, inner + STATE :]
    rows = lax.broadcasted_iota(jnp.int32, (CHUNK, CHUNK), 0)
    cols = lax.broadcasted_iota(jnp.int32, (CHUNK, CHUNK), 1)
    keep = (cols >= rows) & (cols < last)
    mixed = jnp.where(keep, nt(b, c), 0.0)

    lam = lloc_ref[0].astype(f32) + spread_row(dsuf[0:1, :], member) * lin_ref[...]
    lam_low = lam.astype(bf16)
    dsuf[...] = dsuf[...] * decay
    state = sent_ref[0]
    decay_sum = jnp.sum(lam * state.astype(f32), axis=0, keepdims=True) * spread_row(decay, member)
    z_head = per_head(jnp.broadcast_to(decay_sum, (PAD, inner)), member)[0:1]

    gy_low = gy_ref[...]
    gy = gy_low.astype(f32)
    dt_all = dtw_ref[...].astype(f32)
    out_all = outw_ref[...].astype(f32)
    xd_low = (acts_ref[:, 0:inner].astype(f32) * dt_all).astype(bf16)
    xd = xd_low.astype(f32)
    g_out = out_all * nn(b, lam_low)
    e_head = per_head(xd * g_out, member)
    gy_in = gy * into_ref[...].astype(f32)
    f_head = per_head(gy_in * nn(c, state), member)
    g_c = nt(gy_in.astype(bf16), state)
    g_b = nt((xd * out_all).astype(bf16), lam_low)
    skip = spread_row(hp_ref[2:3, :], member)

    lane = lax.broadcasted_iota(jnp.int32, (1, 2 * HEAD_DIM), 1)
    left = flag(lane < HEAD_DIM).astype(bf16)
    right = flag(lane >= HEAD_DIM).astype(bf16)
    mixed2 = jnp.concatenate([mixed, mixed], axis=1)
    d_mixed = jnp.zeros((CHUNK, 2 * CHUNK), f32)
    for pair in range(heads // 2):
        at = slice(2 * pair * HEAD_DIM, 2 * (pair + 1) * HEAD_DIM)
        gyp = gy_low[:, at]
        block = jnp.concatenate([gyp * left, gyp * right], axis=0)
        d_m = nt(xd_low[:, at], block)
        gaps = [logs_t[h : h + 1, :] - logs[:, h : h + 1] for h in (2 * pair, 2 * pair + 1)]
        decays = jnp.exp2(jnp.minimum(jnp.concatenate(gaps, axis=1), 0.0))
        d_mixed = d_mixed + d_m * decays
        weights = (decays * mixed2).astype(bf16)
        g_in = nn(weights, block)
        r_pair = jnp.sum(weights.astype(f32) * d_m, axis=0, keepdims=True)
        rows_scr[2 * pair : 2 * pair + 1, :] = r_pair[:, 0:CHUNK]
        rows_scr[2 * pair + 1 : 2 * pair + 2, :] = r_pair[:, CHUNK:]
        k_pair = xd[:, at] * g_in
        k_high = k_pair.astype(bf16)
        keys[0:CHUNK, at] = k_high
        keys[CHUNK:, at] = (k_pair - k_high.astype(f32)).astype(bf16)
        gext[0:CHUNK, at] = dt_all[:, at] * (g_in + g_out[:, at]) + skip[:, at] * gy[:, at]
    d_mixed = jnp.where(keep, d_mixed[:, 0:CHUNK] + d_mixed[:, CHUNK:], 0.0)
    g_b = g_b + nn(d_mixed.astype(bf16), c)
    g_c = g_c + nn(jnp.transpose(d_mixed).astype(bf16), b)
    gext[0:CHUNK, inner : inner + STATE] = g_b
    gext[0:CHUNK, inner + STATE :] = g_c

    k_both = per_head(keys[...], member)
    k_head = k_both[0:CHUNK] + k_both[CHUNK:]
    r_head = jnp.transpose(rows_scr[...])[:, 0:heads]
    g_log = r_head - k_head + f_head
    g_a = running(triangle(False, True), g_log) + running(triangle(True, False), e_head) + z_head
    v = dtr_ref[...] + hp_ref[0:1, :]
    gate = sigmoid(v)
    ratio = jnp.where(v < -20.0, 1.0, gate / dt)
    g_dt = ratio * (k_head + e_head) - (rate * gate) * g_a
    gdt_ref[...] = g_dt.astype(bf16)
    ghead_ref[0:1, :] += jnp.sum(g_dt, axis=0, keepdims=True)
    ghead_ref[1:2, :] += -rate * jnp.sum(dt * g_a, axis=0, keepdims=True)

    wide = 256
    ids = row_ids()
    ahead = [None] + [
        jnp.broadcast_to(flag(ids + back < last), (CHUNK, wide)) for back in range(1, WIDTH)
    ]
    start = chunk == 0
    for lo in range(0, total_cols, wide):
        here = slice(lo, lo + wide)
        g_pre = gext[0:CHUNK, here] * slope_ref[:, here].astype(f32)
        gext[0:CHUNK, here] = g_pre
        u = u_ref[:, here].astype(f32)
        gc_ref[WIDTH : WIDTH + 1, here] += jnp.sum(g_pre, axis=0, keepdims=True)
        gc_ref[WIDTH - 1 : WIDTH, here] += jnp.sum(g_pre * u, axis=0, keepdims=True)
        g_u = cw_ref[WIDTH - 1 : WIDTH, here] * g_pre
        for back in range(1, WIDTH):
            tap = WIDTH - 1 - back
            later = gext[back : back + CHUNK, here] * ahead[back]
            gc_ref[tap : tap + 1, here] += jnp.sum(later * u, axis=0, keepdims=True)
            g_u = g_u + cw_ref[tap : tap + 1, here] * later
        gu_ref[:, here] = g_u.astype(bf16)

        @pl.when(step == 0)
        def _(g_u=g_u, here=here):
            tail_ref[:, here] = g_u[CHUNK - HALO :, :]
            gu_ref[CHUNK - HALO :, here] = jnp.zeros((HALO, wide), bf16)

        @pl.when(start)
        def _(g_pre=g_pre, here=here):
            halo = jnp.zeros((PAD, wide), f32)
            u_before = halo_ref[:, here].astype(f32)[HALO - PAD : HALO]
            head_ext[0:PAD, :] = jnp.zeros((PAD, wide), f32)
            near = lax.broadcasted_iota(jnp.int32, (PAD, 1), 0)
            for back in range(1, WIDTH):
                tap = WIDTH - 1 - back
                head_ext[PAD:, :] = g_pre[0:PAD, :] * flag(near - back >= first[0:PAD, :])
                later = head_ext[back : back + PAD, :]
                gc_ref[tap : tap + 1, here] += jnp.sum(later * u_before, axis=0, keepdims=True)
                halo = halo + cw_ref[tap : tap + 1, here] * later
            hg_ref[0:PAD, here] = jnp.zeros((PAD, wide), f32)
            hg_ref[PAD:, here] = halo


def put_halves(kept_ref, given_ref, value, parity, blocks):
    wide = value.shape[1] // blocks
    halves = [
        jnp.concatenate([value[:, i * wide : (i + 1) * wide] for i in range(odd, blocks, 2)], axis=1)
        for odd in range(2)
    ]

    @pl.when(parity == 0)
    def _():
        kept_ref[...] = halves[0]
        given_ref[...] = halves[1]

    @pl.when(parity == 1)
    def _():
        kept_ref[...] = halves[1]
        given_ref[...] = halves[0]


def fold_kernel(parity_ref, kept_ref, arrived_ref, keep_ref, give_ref):
    total = kept_ref[...].astype(f32) + arrived_ref[...].astype(f32)
    half = total.shape[1] // 2

    @pl.when(parity_ref[0] == 0)
    def _():
        keep_ref[...] = total[:, :half]
        give_ref[...] = total[:, half:].astype(bf16)

    @pl.when(parity_ref[0] == 1)
    def _():
        keep_ref[...] = total[:, half:]
        give_ref[...] = total[:, :half].astype(bf16)


def tn(a, b):
    return lax.dot_general(a, b, (((0,), (0,)), ((), ())), preferred_element_type=f32)


def early_kernel(cot_ref, normed_ref, gn_ref, gz_ref, out_ref):
    inner = gn_ref.shape[1]
    out_ref[:, 0:inner] = tn(cot_ref[...], gn_ref[...]).astype(bf16)
    out_ref[:, inner:] = tn(normed_ref[...], gz_ref[...]).astype(bf16)


def branch_kernel(parity_ref, gn_ref, w_ref, kept_ref, given_ref, *, blocks):
    put_halves(kept_ref, given_ref, nn(gn_ref[...], w_ref[...]).astype(bf16), parity_ref[0], blocks)


def normed_back_kernel(
    parity_ref, gu_ref, gdt_ref, gz_ref, x_ref, scale_ref, gain_ref, wx_ref, wbc_ref, wdt_ref,
    kept_ref, given_ref, dots_ref, ggain_ref, *, blocks,
):
    inner = wx_ref.shape[2]

    @pl.when(pl.program_id(0) == 0)
    def _():
        ggain_ref[...] = jnp.zeros_like(ggain_ref)

    total = gz_ref[...].astype(f32) + nt(gu_ref[:, 0:inner], wx_ref[0])
    total = total + nt(gu_ref[:, inner:], wbc_ref[...]) + nn(gdt_ref[...], wdt_ref[...])
    unit = x_ref[...].astype(f32) * scale_ref[...]
    with_unit = total * unit
    ggain_ref[...] += jnp.sum(with_unit, axis=0, keepdims=True)
    dots = jnp.sum(with_unit * gain_ref[...], axis=1, keepdims=True)
    dots_ref[...] = jnp.transpose(jnp.broadcast_to(dots, (dots.shape[0], 128)))[0:PAD][None]
    put_halves(kept_ref, given_ref, total.astype(bf16), parity_ref[0], blocks)


def along(value, axis, distance):
    count = lax.axis_size(axis)
    route = [(i, i + distance) for i in range(count) if 0 <= i + distance < count]
    return lax.ppermute(value, axis, route)


def swapped(value, axis, bit):
    return lax.ppermute(value, axis, [(i, i ^ bit) for i in range(lax.axis_size(axis))])


def all_sum(value, axis):
    bit = 1
    while bit < lax.axis_size(axis):
        value = value + swapped(value, axis, bit)
        bit *= 2
    return value


def sum_pairs(value, axis):
    parts = [swapped(value, axis, mask) for mask in range(1, lax.axis_size(axis))]
    return value + sum(parts[1:], parts[0])


def summed(blocks):
    total = blocks[0].astype(f32)
    for block in blocks[1:]:
        total = total + block.astype(f32)
    return total


def halves_of(parts, axis, bit):
    upper = (lax.axis_index(axis) & bit) != 0
    kept = [jnp.where(upper, b, a) for a, b in zip(parts[0::2], parts[1::2])]
    given = [jnp.where(upper, a, b) for a, b in zip(parts[0::2], parts[1::2])]
    return kept, given


class Last:

    def __init__(self, kept, arrived, axis, pieces):
        parts = jnp.split(kept.astype(f32) + arrived.astype(f32), lax.axis_size(axis) // 2, axis=1)
        bit = 2
        while True:
            keep, give = halves_of(parts, axis, bit)
            give = jnp.concatenate(give, axis=1).astype(bf16)
            if 2 * bit >= lax.axis_size(axis):
                break
            other = jnp.split(swapped(give, axis, bit), len(keep), axis=1)
            parts = [k + o.astype(f32) for k, o in zip(keep, other)]
            bit *= 2
        self.axis, self.bit, self.keep = axis, bit, keep[0]
        rows = give.shape[0] // pieces
        self.give = [give[i * rows : (i + 1) * rows] for i in range(pieces)]

    def send(self, piece):
        return swapped(self.give[piece], self.axis, self.bit)

    def total(self, arrived):
        return self.keep + jnp.concatenate(arrived, axis=0).astype(f32)


def ring_order(count):
    return list(range(0, count, 2)) + list(range(count - 1, 0, -2))


def dealt(value, axis):
    return lax.all_to_all(value, axis, 0, 0, tiled=True)


def repeated(value, count):
    return jnp.broadcast_to(value[None], (count,) + value.shape)


def grouped_send(value, axis):
    count = lax.axis_size(axis) // 2
    me = lax.axis_index(axis) >> 1
    rows = value.shape[0] // count
    own = lax.dynamic_slice_in_dim(value, me * rows, rows, 0)
    return [own] + [
        swapped(lax.dynamic_slice_in_dim(value, (me ^ mask) * rows, rows, 0), axis, 2 * mask)
        for mask in range(1, count)
    ]


class Ring:

    def __init__(self, values, axis):
        count = lax.axis_size(axis)
        self.values, self.axis, self.count, self.hop = values, axis, count, 0
        self.order = ring_order(count)
        me = lax.axis_index(axis)
        self.spot = jnp.where(me % 2 == 0, me // 2, count - (me + 1) // 2)
        self.moving = self.mine()

    def signs(self):
        return [1 - 2 * (i % 2) for i in range(len(self.values))]

    def mine(self):
        blocks = []
        for value, sign in zip(self.values, self.signs()):
            rows = value.shape[0] // self.count
            ahead = sign * (self.count - 1 - self.hop)
            spot = (self.spot + ahead + 2 * self.count) % self.count
            owner = jnp.where(spot < self.count // 2, 2 * spot, 2 * (self.count - spot) - 1)
            blocks.append(lax.dynamic_slice_in_dim(value, owner * rows, rows, 0))
        return blocks

    def send(self):
        arrived = []
        for block, sign in zip(self.moving, self.signs()):
            route = [
                (self.order[i], self.order[(i + sign) % self.count]) for i in range(self.count)
            ]
            arrived.append(lax.ppermute(block, self.axis, route))
        return arrived

    def add(self, arrived):
        self.hop += 1
        blocks = [a.astype(f32) + b.astype(f32) for a, b in zip(arrived, self.mine())]
        done = self.hop == self.count - 1
        self.moving = blocks if done else [block.astype(bf16) for block in blocks]
        return done


def scatter_direct(value, axis):
    count = lax.axis_size(axis)
    me = lax.axis_index(axis)
    wide = value.shape[1] // count
    own = lax.dynamic_slice_in_dim(value, me * wide, wide, 1)
    return summed([own] + [
        swapped(lax.dynamic_slice_in_dim(value, (me ^ mask) * wide, wide, 1), axis, mask)
        for mask in range(1, count)
    ])


def gather_direct(value, axis):
    count = lax.axis_size(axis)
    me = lax.axis_index(axis)
    parts = [value] + [swapped(value, axis, mask) for mask in range(1, count)]
    ordered = []
    for place in range(count):
        part = parts[place]
        for mask in range(1, count):
            part = jnp.where(me == mask, parts[place ^ mask], part)
        ordered.append(part)
    return jnp.concatenate(ordered, axis=1)


def all_sum_low(value, axis):
    bit = 1
    while bit < lax.axis_size(axis):
        value = value + swapped(value.astype(bf16), axis, bit).astype(f32)
        bit *= 2
    return value


def call(kernel, grid, in_specs, out_specs, out_shape, scratch, micros, vmem, **names):
    return pl.pallas_call(
        kernel,
        grid=grid,
        in_specs=in_specs,
        out_specs=out_specs,
        out_shape=out_shape,
        scratch_shapes=scratch,
        compiler_params=pltpu.CompilerParams(
            dimension_semantics=("arbitrary",), vmem_limit_bytes=vmem * 1024 * 1024
        ),
        cost_estimate=pl.CostEstimate(
            flops=micros * 10**9, bytes_accessed=micros * 10**6, transcendentals=0
        ),
        **names,
    )


def together(*values):
    return lax.optimization_barrier(values)


def per_device(
    x_in, norm_gain, w_zx, w_bc, w_dt, conv_x, conv_bc, head_params, gate_gain, w_out, lengths,
    grad_out,
):
    tokens, width = x_in.shape
    heads = head_params.shape[1]
    inner = gate_gain.shape[0]
    members = lax.axis_size("tensor")
    devices = lax.axis_size("seq")
    inner_all = inner * members
    total_cols = inner + 2 * STATE
    chunks = tokens // CHUNK
    reach = min(-(-REACH // tokens), devices - 1)
    device = lax.axis_index("seq")
    member = lax.axis_index("tensor")

    shape = jax.ShapeDtypeStruct
    rows = lambda wide: pl.BlockSpec((CHUNK, wide), lambda i: (i, 0))
    back = lambda wide: pl.BlockSpec((CHUNK, wide), lambda i: (chunks - 1 - i, 0))
    whole = lambda *dims: pl.BlockSpec(dims, lambda i: (0,) * len(dims))
    stack = lambda *dims: pl.BlockSpec((1,) + dims, lambda i: (i,) + (0,) * len(dims))
    stack_back = lambda *dims: pl.BlockSpec(
        (1,) + dims, lambda i: (chunks - 1 - i,) + (0,) * len(dims)
    )
    c_at = inner // STATE + 1
    c_rows = pl.BlockSpec((CHUNK, STATE), lambda i: (i, c_at))
    c_back = pl.BlockSpec((CHUNK, STATE), lambda i: (chunks - 1 - i, c_at))

    ends = jnp.cumsum(lengths)
    starts = ends - lengths
    places = device * tokens + jnp.arange(tokens, dtype=jnp.int32)[:, None]
    seg_first = jnp.max(jnp.where(starts[None, :] <= places, starts[None, :], 0), axis=1)
    seg_last = jnp.min(
        jnp.where(ends[None, :] > places, ends[None, :], jnp.iinfo(jnp.int32).max // 2), axis=1
    )
    info = jnp.stack([seg_first, seg_last], axis=1) - device * tokens

    cotangent = lax.all_gather(grad_out, "tensor", axis=1, tiled=True)

    x_halo = along(x_in[tokens - HALO :], "seq", 1)
    w_both = lax.optimization_barrier(jnp.transpose(w_zx, (1, 0, 2)))
    block = 256
    tile = lambda wide: pl.BlockSpec((block, wide), lambda i: (i, 0))
    normed, x_scale, u, halo, dt_raw = call(
        project_kernel, (tokens // block,),
        [tile(width), whole(HALO, width), whole(1, width),
         pl.BlockSpec((1, width, inner), lambda i: (1, 0, 0)), whole(width, 2 * STATE),
         whole(heads, width)],
        [tile(width), tile(1), tile(total_cols), whole(HALO, total_cols), tile(heads)],
        [shape((tokens, width), bf16), shape((tokens, 1), f32),
         shape((tokens, total_cols), bf16), shape((HALO, total_cols), bf16),
         shape((tokens, heads), f32)],
        [], 10, 56, name="project",
    )(x_in, x_halo, norm_gain[None, :], w_both, w_bc, w_dt.T)
    conv_w = jnp.concatenate([conv_x, conv_bc], axis=1)

    acts, slope, dt, logs, spread_out, local_in, leaving = call(
        fwd_kernel, (chunks,),
        [rows(total_cols), whole(HALO, total_cols), whole(WIDTH + 1, total_cols), rows(heads),
         whole(3, heads), rows(2)],
        [rows(total_cols), rows(total_cols), rows(heads), rows(heads), rows(3 * inner),
         stack(STATE, inner), whole(STATE + 2 * PAD, inner)],
        [shape((tokens, total_cols), bf16), shape((tokens, total_cols), bf16),
         shape((tokens, heads), f32), shape((tokens, heads), f32),
         shape((tokens, 3 * inner), bf16), shape((chunks, STATE, inner), bf16),
         shape((STATE + 2 * PAD, inner), bf16)],
        [pltpu.VMEM((CHUNK + PAD, total_cols), f32), pltpu.VMEM((STATE, inner), f32),
         pltpu.VMEM((PAD, inner), f32)],
        12, 56, name="conv_states",
    )(u, halo, conv_w, dt_raw, head_params, info)
    spread_rows = lambda which: pl.BlockSpec((CHUNK, inner), lambda i: (i, which))
    spread_back = lambda which: pl.BlockSpec((CHUNK, inner), lambda i: (chunks - 1 - i, which))

    def unpacked(sent):
        low = sent[STATE:].astype(f32)
        return sent[:STATE].astype(f32), low[0:1] + low[PAD : PAD + 1]

    def joined(sent, arrived):
        state, fade = unpacked(sent)
        before, fade_before = unpacked(arrived)
        state, fade = state + fade * before, fade * fade_before
        high = fade.astype(bf16).astype(f32)
        rows = [jnp.broadcast_to(part, (PAD, inner)) for part in (high, fade - high)]
        return jnp.concatenate([state] + rows, axis=0).astype(bf16)

    def chained(sent, sign, first_work, second_work):
        arrived, first = together(along(sent, "seq", sign), first_work())
        pair = joined(sent, arrived)
        hops = [hop for hop in range(1, reach + 1, 2) if hop < devices]
        arrived, second = together(
            [along(pair, "seq", sign * hop) for hop in hops], second_work()
        )
        total = unpacked(arrived[-1])[0]
        for block in arrived[-2::-1]:
            state, fade = unpacked(block)
            total = state + fade * total
        return total, first, second

    back_dims = (((1,), (1,)), ((), ()))
    weight_dims = (((0,), (0,)), ((), ()))
    low = lambda a, b, dims: lax.dot_general(a, b, dims, preferred_element_type=f32).astype(bf16)
    wide = lambda a, b, dims: lax.dot_general(a, b, dims, preferred_element_type=f32)

    state_in, grad_gate, gate_in = chained(
        leaving, 1,
        lambda: low(cotangent, w_out, back_dims),
        lambda: low(normed, w_both[0], (((1,), (0,)), ((), ()))),
    )

    gain_row = gate_gain[None, :]
    mixed, entering, sums = call(
        mix_kernel, (chunks,),
        [rows(total_cols), spread_rows(0), rows(heads), stack(STATE, inner),
         whole(STATE, inner), rows(inner), rows(inner), whole(1, inner), whole(3, heads), rows(2)],
        [rows(inner), stack(STATE, inner), stack(PAD, CHUNK)],
        [shape((tokens, inner), f32), shape((chunks, STATE, inner), bf16),
         shape((chunks, PAD, CHUNK), f32)],
        [pltpu.VMEM((PAD, heads), f32)], 15, 14, name="mix",
    )(acts, spread_out, logs, local_in, state_in, gate_in, grad_gate, gain_row,
      head_params, info)

    gate_rows = sum_pairs(sums, "tensor")

    gate_normed, grad_gate_in, grad_mixed, grad_local, grad_leaving, grad_gain, grad_skip = call(
        partial(gate_back_kernel, inner_all=inner_all), (chunks,),
        [back(inner), back(inner), back(inner), stack_back(PAD, CHUNK), whole(1, inner),
         back(inner), c_back, spread_back(2), back(heads), back(2),
         pl.BlockSpec((2 * PAD, inner), lambda i: (STATE // (2 * PAD), 0))],
        [back(inner), back(inner), back(inner), stack_back(STATE, inner),
         whole(STATE + 2 * PAD, inner), whole(1, inner), whole(1, inner)],
        [shape((tokens, inner), bf16), shape((tokens, inner), bf16), shape((tokens, inner), bf16),
         shape((chunks, STATE, inner), bf16), shape((STATE + 2 * PAD, inner), bf16),
         shape((1, inner), f32), shape((1, inner), f32)],
        [pltpu.VMEM((STATE, inner), f32)], 12, 14, name="gate_back",
    )(mixed, gate_in, grad_gate, gate_rows, gain_row, acts, acts, spread_out, logs, info, leaving)

    tall = lambda cols: pl.BlockSpec((tokens, cols), lambda i: (0, i))
    grad_in, grad_normed_z, early = chained(
        grad_leaving, -1,
        lambda: low(grad_gate_in, w_both[0], back_dims),
        lambda: call(
            early_kernel, (width // 512,),
            [tall(512), tall(512), whole(tokens, inner), whole(tokens, inner)],
            pl.BlockSpec((512, 2 * inner), lambda i: (i, 0)), shape((width, 2 * inner), bf16), [],
            14, 20, name="early",
        )(cotangent, normed, gate_normed, grad_gate_in),
    )
    early, grad_in = together(early, grad_in)
    early_sum = lax.psum_scatter(early, "seq", scatter_dimension=0, tiled=True)

    part = back
    grad_u, grad_dt, tail, sent, grad_conv, grad_heads = call(
        bwd_kernel, (chunks,),
        [part(inner), part(total_cols), part(total_cols), part(heads), part(heads),
         part(heads), spread_back(0), spread_back(1), spread_back(2),
         stack_back(STATE, inner), stack_back(STATE, inner), whole(STATE, inner),
         part(total_cols), whole(HALO, total_cols),
         whole(WIDTH + 1, total_cols), whole(3, heads), part(2)],
        [part(total_cols), part(heads), whole(HALO, total_cols), whole(HALO, total_cols),
         whole(PAD, total_cols), whole(PAD, heads)],
        [shape((tokens, total_cols), bf16), shape((tokens, heads), bf16),
         shape((HALO, total_cols), f32), shape((HALO, total_cols), f32),
         shape((PAD, total_cols), f32), shape((PAD, heads), f32)],
        [pltpu.VMEM((PAD, heads), f32), pltpu.VMEM((CHUNK + PAD, total_cols), f32),
         pltpu.VMEM((CHUNK, CHUNK), f32),
         pltpu.VMEM((2 * PAD, 256), f32), pltpu.VMEM((2 * CHUNK, inner), bf16)],
        30, 56, name="scan_back",
    )(grad_mixed, acts, slope, dt, logs, dt_raw, spread_out, spread_out, spread_out,
      entering, grad_local, grad_in, u, halo, conv_w, head_params, info)

    core = (member & 1).reshape(1)
    split_tile = pl.BlockSpec((2, block, width // 2), lambda i: (0, i, 0))
    own_bc = 2 * STATE // members

    slice_width = grad_out.shape[1]
    x_part = lax.dynamic_slice_in_dim(x_in, member * slice_width, slice_width, 1).astype(f32)
    parity = device & 1

    cuts = [0, inner // 4, inner // 2, inner]
    sent = along(sent, "seq", -1)
    late = low(normed, grad_u[:, :inner], weight_dims)
    late_blocks = late.reshape(devices // 2, 2, width // devices, inner)
    half_of = lambda odd: lax.dynamic_index_in_dim(late_blocks, odd, 1, False).reshape(-1, inner)
    given, kept = half_of(1 - parity), half_of(parity)
    given, kept, gate_normed = together(given, kept, gate_normed)
    piece_of = lambda at: swapped(given[:, cuts[at] : cuts[at + 1]], "seq", 1)
    branch_kept, branch_given = call(
        partial(branch_kernel, blocks=members), (tokens // block,),
        [pl.BlockSpec(memory_space=pltpu.SMEM), tile(inner), whole(inner, width)],
        [tile(width // 2)] * 2, [shape((tokens, width // 2), bf16)] * 2, [], 9, 56, name="branch",
    )(core, gate_normed, w_out)
    arrived_0, sent, branch_kept, branch_given = together(
        piece_of(0), sent, branch_kept, branch_given
    )
    tail = (tail + sent).astype(bf16)
    grad_u = lax.dynamic_update_slice_in_dim(grad_u, tail, tokens - HALO, 0)
    factors = jnp.concatenate([normed[tokens - HALO :], tail[:, :inner]], axis=1)
    factors = jnp.concatenate([factors, swapped(factors, "seq", 1)], axis=0)

    def first_work():
        return call(
            partial(normed_back_kernel, blocks=members), (tokens // block,),
            [pl.BlockSpec(memory_space=pltpu.SMEM), tile(total_cols), tile(heads), tile(width),
             tile(width), tile(1), whole(1, width),
             pl.BlockSpec((1, width, inner), lambda i: (1, 0, 0)), whole(width, 2 * STATE),
             whole(heads, width)],
            [tile(width // 2), tile(width // 2), pl.BlockSpec((1, PAD, block), lambda i: (i, 0, 0)), whole(1, width)],
            [shape((tokens, width // 2), bf16), shape((tokens, width // 2), bf16),
             shape((tokens // block, PAD, block), f32),
             shape((1, width), f32)],
            [], 15, 56, name="normed_back",
        )(core, grad_u, grad_dt, grad_normed_z, x_in, x_scale, norm_gain[None, :], w_both, w_bc,
          w_dt.T)

    grad_bc, arrived_1, (normed_kept, normed_given, dots_here, gain), factors = together(
        scatter_direct(grad_u[:, inner:], "tensor").astype(bf16), piece_of(1), first_work(), factors
    )

    def fold(kept, arrived):
        bit = 2
        while bit < members:
            wide_now = kept.shape[1]
            kept, given = call(
                fold_kernel, (tokens // block,),
                [pl.BlockSpec(memory_space=pltpu.SMEM), tile(wide_now), tile(wide_now)],
                [tile(wide_now // 2)] * 2,
                [shape((tokens, wide_now // 2), f32), shape((tokens, wide_now // 2), bf16)],
                [], 3, 12, name="fold",
            )(((member // bit) & 1).reshape(1), kept, arrived)
            bit *= 2
            if bit < members:
                arrived = swapped(given, "tensor", bit // 2)
        return kept, swapped(given, "tensor", bit // 2)


    def second_work():
        shared = jnp.concatenate(
            [grad_conv[: WIDTH + 1, inner:].reshape(-1), gain.reshape(-1)]
        ).reshape(-1, 128)
        return (
            sum_pairs(dots_here[:, 0], "tensor"), sum_pairs(shared, "tensor"),
            swapped(branch_given, "tensor", 1),
        )

    dots, shared, branch_other = together(*second_work())

    heads_here = jnp.concatenate(
        [grad_heads[:2], jnp.sum(grad_skip.reshape(heads, HEAD_DIM), axis=1)[None, :]], axis=0
    )
    own_small = jnp.concatenate(
        [grad_conv[: WIDTH + 1, :inner].reshape(-1), grad_gain.reshape(-1),
         heads_here.reshape(-1), jnp.zeros((-3 * heads % 128,), f32)]
    ).reshape(-1, 128)
    small = jnp.concatenate([shared, own_small], axis=0)
    high = small.astype(bf16)
    small = jnp.concatenate([high, (small - high.astype(f32)).astype(bf16)], axis=1)
    small_size = small.size
    block_cols = width // devices
    small = jnp.pad(small.reshape(-1), (0, -small_size % block_cols)).reshape(-1, block_cols)

    def third_work():
        both = jnp.concatenate([grad_bc, grad_dt], axis=1)
        bcdt = low(both, normed, weight_dims)
        blocks = jnp.transpose(bcdt.reshape(-1, devices, width // devices), (1, 0, 2))
        blocks = jnp.concatenate([blocks, repeated(small, devices)], axis=1)
        branch_keep, branch_sent = fold(branch_kept, branch_other)
        return (
            dealt(blocks, "seq"), branch_keep, branch_sent, swapped(normed_given, "tensor", 1),
        )

    bcdt, branch_keep, branch_sent, normed_other = together(*third_work())

    def fourth_work():
        total = summed(bcdt)
        normed_keep, normed_sent = fold(normed_kept, normed_other)
        block_out = (x_part + branch_keep + branch_sent.astype(f32)).astype(bf16)
        rows = repeated(total[:own_bc].astype(bf16).T, devices)
        return total, dealt(rows, "seq"), normed_keep, normed_sent, block_out

    bcdt, bc_rows, normed_keep, normed_sent, block_out, arrived_2 = together(
        *fourth_work(), piece_of(2)
    )
    arrived = jnp.concatenate([arrived_0, arrived_1, arrived_2], axis=1)
    rows_of = factors[:, :width].reshape(2 * HALO, devices // 2, 2, width // devices)
    rows_of = lax.dynamic_index_in_dim(rows_of, parity, 2, False).reshape(2 * HALO, -1)
    flying = (
        wide(rows_of, factors[:, width:], weight_dims) + kept.astype(f32) + arrived.astype(f32)
    ).astype(bf16)
    flying, bc_rows, normed_keep = together(flying, bc_rows, normed_keep)

    def fifth_work():
        grad_normed = normed_keep + normed_sent.astype(f32)
        gain_part = lax.dynamic_slice_in_dim(norm_gain, member * slice_width, slice_width, 0)
        row_mean = dots.reshape(tokens, 1) * (1.0 / width)
        grad_x = (
            x_scale * (grad_normed * gain_part[None, :] - x_part * x_scale * row_mean)
            + grad_out.astype(f32)
        )
        bc_all = gather_direct(bc_rows.reshape(width, own_bc), "tensor")
        return grad_x, bc_all

    sums, (grad_x, bc_all) = (grouped_send(flying, "seq"), fifth_work())
    grad_w_bc = bc_all.astype(f32)
    small = bcdt[own_bc + heads :].reshape(-1)[:small_size].reshape(-1, 256)
    small = small[:, 0:128] + small[:, 128:256]
    bcdt = bcdt[: own_bc + heads]
    early_sum = early_sum.astype(f32)
    grad_z_sum = early_sum[:, inner:]
    grad_w_out = early_sum[:, :inner].T

    grad_w_dt = bcdt[own_bc:].T

    shared, own = small[: shared.shape[0]].reshape(-1), small[shared.shape[0] :].reshape(-1)
    bc_size = (WIDTH + 1) * 2 * STATE
    x_size = (WIDTH + 1) * inner
    grad_conv_bc = shared[:bc_size].reshape(WIDTH + 1, 2 * STATE)
    grad_norm_gain = shared[bc_size:]
    grad_conv_x = own[:x_size].reshape(WIDTH + 1, inner)
    grad_gate_gain = own[x_size : x_size + inner]
    grad_head = own[x_size + inner : x_size + inner + 3 * heads].reshape(3, heads)

    (sums, grad_z_sum, grad_w_out, grad_w_bc, grad_w_dt, grad_x, block_out, grad_conv_x,
     grad_conv_bc, grad_head, grad_gate_gain, grad_norm_gain) = together(
        sums, grad_z_sum, grad_w_out, grad_w_bc, grad_w_dt, grad_x, block_out, grad_conv_x,
        grad_conv_bc, grad_head, grad_gate_gain, grad_norm_gain)
    grad_w_zx = jnp.stack([grad_z_sum, summed(sums)], axis=1)
    return (
        block_out, grad_x, grad_norm_gain, grad_w_zx, grad_w_bc, grad_w_dt, grad_conv_x,
        grad_conv_bc, grad_head, grad_gate_gain, grad_w_out,
    )


def solution(mesh):
    return jax.shard_map(
        per_device,
        mesh=mesh,
        in_specs=(
            P("seq", None), P(), P(None, None, "tensor"), P(), P(None, "tensor"),
            P(None, "tensor"), P(), P(None, "tensor"), P("tensor"), P("tensor", None), P(),
            P("seq", "tensor"),
        ),
        out_specs=(
            P("seq", "tensor"), P("seq", "tensor"), P(), P("seq", None, "tensor"), P(),
            P("seq", "tensor"), P(None, "tensor"), P(), P(None, "tensor"), P("tensor"),
            P("tensor", "seq"),
        ),
        check_vma=False,
    )
```

```python
from functools import partial

import jax
import jax.numpy as jnp
from jax import lax
from jax.experimental import pallas as pl
from jax.experimental.pallas import tpu as pltpu
from jax.sharding import PartitionSpec as P

HEAD_DIM = 64
STATE = 128
WIDTH = 4
CHUNK = 128
REACH = 4096
PAD = 8
HALO = 16
LOG2E = 1.4426950408889634

eps = 1e-05
f32 = jnp.float32
bf16 = jnp.bfloat16


def nn(a, b):
    return lax.dot_general(a, b, (((1,), (0,)), ((), ())), preferred_element_type=f32)


def nt(a, b):
    return lax.dot_general(a, b, (((1,), (1,)), ((), ())), preferred_element_type=f32)


def running(mask, v):
    wide = v.shape[1]
    high = v.astype(bf16)
    rest = v - high.astype(f32)
    mid = rest.astype(bf16)
    low = (rest - mid.astype(f32)).astype(bf16)
    out = nn(mask, jnp.concatenate([high, mid, low], axis=1))
    return out[:, 0:wide] + out[:, wide : 2 * wide] + out[:, 2 * wide : 3 * wide]


def head_map(heads):
    row = lax.broadcasted_iota(jnp.int32, (2 * heads, heads * HEAD_DIM), 0)
    col = lax.broadcasted_iota(jnp.int32, (2 * heads, heads * HEAD_DIM), 1)
    row = jnp.where(row >= heads, row - heads, row)
    return jnp.where((col >> 6) == row, 1.0, 0.0).astype(bf16)


def spread(v, member):
    high = v.astype(bf16)
    rest = (v - high.astype(f32)).astype(bf16)
    return nn(jnp.concatenate([high, rest], axis=1), member)


def spread_row(v, member):
    return spread(jnp.broadcast_to(v, (PAD, v.shape[1])), member)[0:1]


def per_head(v, member):
    return nt(v.astype(bf16), member[0 : member.shape[0] // 2])


def triangle(strict, upper):
    row = lax.broadcasted_iota(jnp.int32, (CHUNK, CHUNK), 0)
    col = lax.broadcasted_iota(jnp.int32, (CHUNK, CHUNK), 1)
    if upper:
        row, col = col, row
    keep = (row > col) if strict else (row >= col)
    return jnp.where(keep, 1.0, 0.0).astype(bf16)


def softplus(v):
    return jnp.maximum(v, 0.0) + jnp.log1p(jnp.exp(-jnp.abs(v)))


def sigmoid(v):
    return 0.5 * jnp.tanh(0.5 * v) + 0.5


def seg_bounds(info_ref, chunk):
    info = info_ref[...] - chunk * CHUNK
    return info[:, 0:1], info[:, 1:2]


def row_ids():
    return lax.broadcasted_iota(jnp.int32, (CHUNK, 1), 0)


def flag(v):
    return jnp.where(v, 1.0, 0.0).astype(f32)


def conv_pre(ext_ref, w_ref, masks, lo, wide):
    cols = taps = slice(lo, lo + wide)
    total = w_ref[WIDTH : WIDTH + 1, taps] + w_ref[WIDTH - 1 : WIDTH, taps] * ext_ref[
        PAD : PAD + CHUNK, cols
    ]
    for back in range(1, WIDTH):
        total = total + w_ref[WIDTH - 1 - back : WIDTH - back, taps] * (
            ext_ref[PAD - back : PAD - back + CHUNK, cols] * masks[back]
        )
    return total


def project_kernel(
    x_ref, xh_ref, gain_ref, wx_ref, wbc_ref, wdt_ref, normed_ref, scale_ref, u_ref, halo_ref, dtr_ref,
):
    count = x_ref.shape[0]
    x = jnp.concatenate([x_ref[...], xh_ref[...]], axis=0).astype(f32)
    scale = lax.rsqrt(jnp.mean(x * x, axis=1, keepdims=True) + eps)
    normed = (x * scale * gain_ref[...]).astype(bf16)
    scale_ref[...] = scale[:count]
    normed_ref[...] = normed[:count]
    inner = wx_ref.shape[2]
    u_x = nn(normed, wx_ref[0]).astype(bf16)
    u_bc = nn(normed, wbc_ref[...]).astype(bf16)
    u_ref[:, 0:inner] = u_x[:count]
    u_ref[:, inner:] = u_bc[:count]
    halo_ref[:, 0:inner] = u_x[count:]
    halo_ref[:, inner:] = u_bc[count:]
    dtr_ref[...] = nt(normed[:count], wdt_ref[...])


def fwd_kernel(
    u_ref, halo_ref, cw_ref, dtr_ref, hp_ref, info_ref,
    acts_ref, slope_ref, dt_ref, log_ref, wide_ref, sloc_ref, send_ref,
    ext, held, drun,
):
    chunk = pl.program_id(0)
    heads = dtr_ref.shape[1]
    inner = heads * HEAD_DIM

    @pl.when(chunk == 0)
    def _():
        ext[0:PAD, :] = halo_ref[...].astype(f32)[HALO - PAD : HALO]
        held[...] = jnp.zeros_like(held)
        drun[...] = jnp.ones_like(drun)

    @pl.when(chunk > 0)
    def _():
        ext[0:PAD, :] = ext[CHUNK : CHUNK + PAD, :]

    ext[PAD:, :] = u_ref[...].astype(f32)
    first, last = seg_bounds(info_ref, chunk)
    rows = row_ids()
    wide = 256
    masks = [None] + [
        jnp.broadcast_to(flag(rows - back >= first), (CHUNK, wide)) for back in range(1, WIDTH)
    ]
    for lo in range(0, u_ref.shape[1], wide):
        pre = conv_pre(ext, cw_ref, masks, lo, wide)
        s = sigmoid(pre)
        act = pre * s
        acts_ref[:, lo : lo + wide] = act.astype(bf16)
        slope_ref[:, lo : lo + wide] = (s + act * (1.0 - s)).astype(bf16)

    member = head_map(heads)
    dt = softplus(dtr_ref[...] + hp_ref[0:1, :])
    rate = jnp.exp(hp_ref[1:2, :]) * LOG2E
    logs = running(triangle(False, False), -dt * rate)
    dt_ref[...] = dt
    log_ref[...] = logs
    tail = logs[CHUNK - 1 : CHUNK, :]
    keep_in = flag(first < 0)
    keep_out = flag(last >= CHUNK)
    dt_all = spread(dt, member)
    out_all = spread(jnp.exp2(tail - logs) * keep_out, member)
    into_all = spread(jnp.exp2(logs) * keep_in, member)
    wide_ref[:, 0:inner] = dt_all.astype(bf16)
    wide_ref[:, inner : 2 * inner] = out_all.astype(bf16)
    wide_ref[:, 2 * inner :] = into_all.astype(bf16)
    x_in = (acts_ref[:, 0:inner].astype(f32) * (dt_all * out_all)).astype(bf16)
    b_cols = jnp.transpose(acts_ref[:, inner : inner + STATE].astype(f32)).astype(bf16)
    local = nn(b_cols, x_in)
    decay_all = into_all[CHUNK - 1 : CHUNK, :]
    sloc_ref[...] = held[...].astype(bf16)[None]
    held[...] = decay_all * held[...] + local
    drun[...] = drun[...] * decay_all

    @pl.when(chunk == pl.num_programs(0) - 1)
    def _():
        total = drun[...]
        high = total.astype(bf16)
        send_ref[0:STATE, :] = held[...].astype(bf16)
        send_ref[STATE:, :] = jnp.concatenate(
            [total, total - high.astype(f32)], axis=0
        ).astype(bf16)


def mix_kernel(
    acts_ref, dt_ref, log_ref, sloc_ref, sin_ref, z_ref, gg_ref, gain_ref, hp_ref, info_ref,
    y_ref, sent_ref, sums_ref,
    dpre,
):
    chunk = pl.program_id(0)
    heads = log_ref.shape[1]
    inner = heads * HEAD_DIM
    member = head_map(heads)

    @pl.when(chunk == 0)
    def _():
        dpre[...] = jnp.ones_like(dpre)

    first, _ = seg_bounds(info_ref, chunk)
    rows = lax.broadcasted_iota(jnp.int32, (CHUNK, CHUNK), 0)
    cols = lax.broadcasted_iota(jnp.int32, (CHUNK, CHUNK), 1)
    b = acts_ref[:, inner : inner + STATE]
    c = acts_ref[:, inner + STATE :]
    mixed = jnp.where((cols <= rows) & (cols >= first), nt(c, b), 0.0)
    logs = log_ref[...]
    logs_t = jnp.transpose(logs)
    decay = jnp.exp2(logs[CHUNK - 1 : CHUNK, :]) * flag(first < 0)[CHUNK - 1 : CHUNK, :]
    state = sloc_ref[0].astype(f32) + spread_row(dpre[0:1, :], member) * sin_ref[...]
    dpre[...] = dpre[...] * decay
    state_low = state.astype(bf16)
    state_rest = (state - state_low.astype(f32)).astype(bf16)
    sent_ref[...] = state_low[None]
    x = acts_ref[:, 0:inner].astype(f32)
    xd = x * dt_ref[...].astype(f32)
    skip = spread_row(hp_ref[2:3, :], member)
    into = spread(jnp.exp2(logs) * flag(first < 0), member)
    carried = into * (nn(c, state_low) + nn(c, state_rest)) + skip * x
    lane = lax.broadcasted_iota(jnp.int32, (1, 2 * HEAD_DIM), 1)
    left = flag(lane < HEAD_DIM)
    right = 1.0 - left
    squares = jnp.zeros((CHUNK, 2 * HEAD_DIM), f32)
    dots = jnp.zeros((CHUNK, 2 * HEAD_DIM), f32)
    for pair in range(heads // 2):
        mats = []
        for h in (2 * pair, 2 * pair + 1):
            gap = logs[:, h : h + 1] - logs_t[h : h + 1, :]
            mats.append((jnp.exp2(jnp.minimum(gap, 0.0)) * mixed).astype(bf16))
        at = slice(2 * pair * HEAD_DIM, 2 * (pair + 1) * HEAD_DIM)
        xp = xd[:, at]
        block = jnp.concatenate([(xp * left).astype(bf16), (xp * right).astype(bf16)], axis=0)
        y = carried[:, at] + nn(jnp.concatenate(mats, axis=1), block)
        y_ref[:, at] = y
        z = z_ref[:, at].astype(f32)
        gated = y * (z * sigmoid(z))
        squares = squares + gated * gated
        dots = dots + gated * (gg_ref[:, at].astype(f32) * gain_ref[:, at])
    lane = lax.broadcasted_iota(jnp.int32, (CHUNK, STATE), 1)
    both = jnp.where(
        lane == 0, jnp.sum(squares, axis=1, keepdims=True),
        jnp.where(lane == 1, jnp.sum(dots, axis=1, keepdims=True), 0.0),
    )
    sums_ref[...] = jnp.transpose(both)[0:PAD][None]


def gate_back_kernel(
    y_ref, z_ref, gg_ref, sums_ref, gain_ref, xa_ref, c_ref, into_ref, log_ref, info_ref, fade_ref,
    gn_ref, gz_ref, gy_ref, lloc_ref, send_ref, ggain_ref, gskip_ref,
    held, *, inner_all,
):
    step = pl.program_id(0)
    chunk = pl.num_programs(0) - 1 - step
    heads = log_ref.shape[1]
    member = head_map(heads)

    @pl.when(step == 0)
    def _():
        held[...] = jnp.zeros_like(held)
        ggain_ref[...] = jnp.zeros_like(ggain_ref)
        gskip_ref[...] = jnp.zeros_like(gskip_ref)

    sums = jnp.transpose(jnp.concatenate([sums_ref[0]] * (CHUNK // PAD), axis=0))
    scale = lax.rsqrt(sums[:, 0:1] * (1.0 / inner_all) + eps)
    mean = sums[:, 1:2] * scale * (1.0 / inner_all)
    z = z_ref[...].astype(f32)
    y = y_ref[...]
    s = sigmoid(z)
    act = z * s
    gain = gain_ref[...]
    gg = gg_ref[...].astype(f32)
    unit = y * act * scale
    gn_ref[...] = (unit * gain).astype(bf16)
    ggain_ref[...] += jnp.sum(gg * unit, axis=0, keepdims=True)
    g_gated = scale * (gg * gain - unit * mean)
    gz_ref[...] = (g_gated * y * s * (1.0 + z * (1.0 - s))).astype(bf16)
    gy = g_gated * act
    gy_ref[...] = gy.astype(bf16)
    gskip_ref[...] += jnp.sum(gy * xa_ref[...].astype(f32), axis=0, keepdims=True)
    first, _ = seg_bounds(info_ref, chunk)
    decay = jnp.exp2(log_ref[CHUNK - 1 : CHUNK, :]) * flag(first < 0)[CHUNK - 1 : CHUNK, :]
    weighted = (gy * into_ref[...].astype(f32)).astype(bf16)
    c_cols = jnp.transpose(c_ref[...].astype(f32)).astype(bf16)
    lloc_ref[...] = held[...].astype(bf16)[None]
    held[...] = spread_row(decay, member) * held[...] + nn(c_cols, weighted)

    @pl.when(step == pl.num_programs(0) - 1)
    def _():
        send_ref[0:STATE, :] = held[...].astype(bf16)
        send_ref[STATE:, :] = fade_ref[...]


def bwd_kernel(*refs):
    (
        gy_ref, acts_ref, slope_ref, dt_ref, log_ref, dtr_ref, dtw_ref, outw_ref, into_ref,
        sent_ref, lloc_ref, lin_ref, u_ref, halo_ref, cw_ref, hp_ref, info_ref,
    ) = refs[:17]
    (
        gu_ref, gdt_ref, tail_ref, hg_ref, gc_ref, ghead_ref, dsuf, gext, rows_scr, head_ext, keys,
    ) = refs[17:]
    step = pl.program_id(0)
    chunk = pl.num_programs(0) - 1 - step
    inner = gy_ref.shape[1]
    heads = log_ref.shape[1]
    member = head_map(heads)
    total_cols = inner + 2 * STATE

    @pl.when(step == 0)
    def _():
        dsuf[...] = jnp.ones_like(dsuf)
        gc_ref[...] = jnp.zeros_like(gc_ref)
        ghead_ref[...] = jnp.zeros_like(ghead_ref)
        gext[CHUNK:, :] = jnp.zeros((PAD, total_cols), f32)

    @pl.when(step > 0)
    def _():
        gext[CHUNK:, :] = gext[0:PAD, :]

    first, last = seg_bounds(info_ref, chunk)
    logs = log_ref[...]
    logs_t = jnp.transpose(logs)
    dt = dt_ref[...]
    decay = jnp.exp2(logs[CHUNK - 1 : CHUNK, :]) * flag(first < 0)[CHUNK - 1 : CHUNK, :]
    rate = jnp.exp(hp_ref[1:2, :])

    b = acts_ref[:, inner : inner + STATE]
    c = acts_ref[:, inner + STATE :]
    rows = lax.broadcasted_iota(jnp.int32, (CHUNK, CHUNK), 0)
    cols = lax.broadcasted_iota(jnp.int32, (CHUNK, CHUNK), 1)
    keep = (cols >= rows) & (cols < last)
    mixed = jnp.where(keep, nt(b, c), 0.0)

    lam = lloc_ref[0].astype(f32) + spread_row(dsuf[0:1, :], member) * lin_ref[...]
    lam_low = lam.astype(bf16)
    dsuf[...] = dsuf[...] * decay
    state = sent_ref[0]
    decay_sum = jnp.sum(lam * state.astype(f32), axis=0, keepdims=True) * spread_row(decay, member)
    z_head = per_head(jnp.broadcast_to(decay_sum, (PAD, inner)), member)[0:1]

    gy_low = gy_ref[...]
    gy = gy_low.astype(f32)
    dt_all = dtw_ref[...].astype(f32)
    out_all = outw_ref[...].astype(f32)
    xd_low = (acts_ref[:, 0:inner].astype(f32) * dt_all).astype(bf16)
    xd = xd_low.astype(f32)
    g_out = out_all * nn(b, lam_low)
    e_head = per_head(xd * g_out, member)
    gy_in = gy * into_ref[...].astype(f32)
    f_head = per_head(gy_in * nn(c, state), member)
    g_c = nt(gy_in.astype(bf16), state)
    g_b = nt((xd * out_all).astype(bf16), lam_low)
    skip = spread_row(hp_ref[2:3, :], member)

    lane = lax.broadcasted_iota(jnp.int32, (1, 2 * HEAD_DIM), 1)
    left = flag(lane < HEAD_DIM).astype(bf16)
    right = flag(lane >= HEAD_DIM).astype(bf16)
    mixed2 = jnp.concatenate([mixed, mixed], axis=1)
    d_mixed = jnp.zeros((CHUNK, 2 * CHUNK), f32)
    for pair in range(heads // 2):
        at = slice(2 * pair * HEAD_DIM, 2 * (pair + 1) * HEAD_DIM)
        gyp = gy_low[:, at]
        block = jnp.concatenate([gyp * left, gyp * right], axis=0)
        d_m = nt(xd_low[:, at], block)
        gaps = [logs_t[h : h + 1, :] - logs[:, h : h + 1] for h in (2 * pair, 2 * pair + 1)]
        decays = jnp.exp2(jnp.minimum(jnp.concatenate(gaps, axis=1), 0.0))
        d_mixed = d_mixed + d_m * decays
        weights = (decays * mixed2).astype(bf16)
        g_in = nn(weights, block)
        r_pair = jnp.sum(weights.astype(f32) * d_m, axis=0, keepdims=True)
        rows_scr[2 * pair : 2 * pair + 1, :] = r_pair[:, 0:CHUNK]
        rows_scr[2 * pair + 1 : 2 * pair + 2, :] = r_pair[:, CHUNK:]
        k_pair = xd[:, at] * g_in
        k_high = k_pair.astype(bf16)
        keys[0:CHUNK, at] = k_high
        keys[CHUNK:, at] = (k_pair - k_high.astype(f32)).astype(bf16)
        gext[0:CHUNK, at] = dt_all[:, at] * (g_in + g_out[:, at]) + skip[:, at] * gy[:, at]
    d_mixed = jnp.where(keep, d_mixed[:, 0:CHUNK] + d_mixed[:, CHUNK:], 0.0)
    g_b = g_b + nn(d_mixed.astype(bf16), c)
    g_c = g_c + nn(jnp.transpose(d_mixed).astype(bf16), b)
    gext[0:CHUNK, inner : inner + STATE] = g_b
    gext[0:CHUNK, inner + STATE :] = g_c

    k_both = per_head(keys[...], member)
    k_head = k_both[0:CHUNK] + k_both[CHUNK:]
    r_head = jnp.transpose(rows_scr[...])[:, 0:heads]
    g_log = r_head - k_head + f_head
    g_a = running(triangle(False, True), g_log) + running(triangle(True, False), e_head) + z_head
    v = dtr_ref[...] + hp_ref[0:1, :]
    gate = sigmoid(v)
    ratio = jnp.where(v < -20.0, 1.0, gate / dt)
    g_dt = ratio * (k_head + e_head) - (rate * gate) * g_a
    gdt_ref[...] = g_dt.astype(bf16)
    ghead_ref[0:1, :] += jnp.sum(g_dt, axis=0, keepdims=True)
    ghead_ref[1:2, :] += -rate * jnp.sum(dt * g_a, axis=0, keepdims=True)

    wide = 256
    ids = row_ids()
    ahead = [None] + [
        jnp.broadcast_to(flag(ids + back < last), (CHUNK, wide)) for back in range(1, WIDTH)
    ]
    start = chunk == 0
    for lo in range(0, total_cols, wide):
        here = slice(lo, lo + wide)
        g_pre = gext[0:CHUNK, here] * slope_ref[:, here].astype(f32)
        gext[0:CHUNK, here] = g_pre
        u = u_ref[:, here].astype(f32)
        gc_ref[WIDTH : WIDTH + 1, here] += jnp.sum(g_pre, axis=0, keepdims=True)
        gc_ref[WIDTH - 1 : WIDTH, here] += jnp.sum(g_pre * u, axis=0, keepdims=True)
        g_u = cw_ref[WIDTH - 1 : WIDTH, here] * g_pre
        for back in range(1, WIDTH):
            tap = WIDTH - 1 - back
            later = gext[back : back + CHUNK, here] * ahead[back]
            gc_ref[tap : tap + 1, here] += jnp.sum(later * u, axis=0, keepdims=True)
            g_u = g_u + cw_ref[tap : tap + 1, here] * later
        gu_ref[:, here] = g_u.astype(bf16)

        @pl.when(step == 0)
        def _(g_u=g_u, here=here):
            tail_ref[:, here] = g_u[CHUNK - HALO :, :]
            gu_ref[CHUNK - HALO :, here] = jnp.zeros((HALO, wide), bf16)

        @pl.when(start)
        def _(g_pre=g_pre, here=here):
            halo = jnp.zeros((PAD, wide), f32)
            u_before = halo_ref[:, here].astype(f32)[HALO - PAD : HALO]
            head_ext[0:PAD, :] = jnp.zeros((PAD, wide), f32)
            near = lax.broadcasted_iota(jnp.int32, (PAD, 1), 0)
            for back in range(1, WIDTH):
                tap = WIDTH - 1 - back
                head_ext[PAD:, :] = g_pre[0:PAD, :] * flag(near - back >= first[0:PAD, :])
                later = head_ext[back : back + PAD, :]
                gc_ref[tap : tap + 1, here] += jnp.sum(later * u_before, axis=0, keepdims=True)
                halo = halo + cw_ref[tap : tap + 1, here] * later
            hg_ref[0:PAD, here] = jnp.zeros((PAD, wide), f32)
            hg_ref[PAD:, here] = halo


def put_halves(kept_ref, given_ref, value, parity, blocks):
    wide = value.shape[1] // blocks
    halves = [
        jnp.concatenate([value[:, i * wide : (i + 1) * wide] for i in range(odd, blocks, 2)], axis=1)
        for odd in range(2)
    ]

    @pl.when(parity == 0)
    def _():
        kept_ref[...] = halves[0]
        given_ref[...] = halves[1]

    @pl.when(parity == 1)
    def _():
        kept_ref[...] = halves[1]
        given_ref[...] = halves[0]


def turn_kernel(x_ref, out_ref):
    out_ref[...] = jnp.transpose(x_ref[...].astype(f32))


def fold_kernel(parity_ref, kept_ref, arrived_ref, keep_ref, give_ref):
    total = kept_ref[...].astype(f32) + arrived_ref[...].astype(f32)
    half = total.shape[1] // 2

    @pl.when(parity_ref[0] == 0)
    def _():
        keep_ref[...] = total[:, :half]
        give_ref[...] = total[:, half:].astype(bf16)

    @pl.when(parity_ref[0] == 1)
    def _():
        keep_ref[...] = total[:, half:]
        give_ref[...] = total[:, :half].astype(bf16)


def tn(a, b):
    return lax.dot_general(a, b, (((0,), (0,)), ((), ())), preferred_element_type=f32)


def early_kernel(cot_ref, normed_ref, gn_ref, gz_ref, out_ref):
    inner = gn_ref.shape[1]
    out_ref[:, 0:inner] = tn(cot_ref[...], gn_ref[...]).astype(bf16)
    out_ref[:, inner:] = tn(normed_ref[...], gz_ref[...]).astype(bf16)


def branch_kernel(parity_ref, gn_ref, w_ref, kept_ref, given_ref, *, blocks):
    put_halves(kept_ref, given_ref, nn(gn_ref[...], w_ref[...]).astype(bf16), parity_ref[0], blocks)


def normed_back_kernel(
    parity_ref, gu_ref, gdt_ref, gz_ref, x_ref, scale_ref, gain_ref, wx_ref, wbc_ref, wdt_ref,
    kept_ref, given_ref, dots_ref, ggain_ref, *, blocks,
):
    inner = wx_ref.shape[2]

    @pl.when(pl.program_id(0) == 0)
    def _():
        ggain_ref[...] = jnp.zeros_like(ggain_ref)

    total = gz_ref[...].astype(f32) + nt(gu_ref[:, 0:inner], wx_ref[0])
    total = total + nt(gu_ref[:, inner:], wbc_ref[...]) + nn(gdt_ref[...], wdt_ref[...])
    unit = x_ref[...].astype(f32) * scale_ref[...]
    with_unit = total * unit
    ggain_ref[...] += jnp.sum(with_unit, axis=0, keepdims=True)
    dots = jnp.sum(with_unit * gain_ref[...], axis=1, keepdims=True)
    dots_ref[...] = jnp.transpose(jnp.broadcast_to(dots, (dots.shape[0], 128)))[0:PAD][None]
    put_halves(kept_ref, given_ref, total.astype(bf16), parity_ref[0], blocks)


def along(value, axis, distance):
    count = lax.axis_size(axis)
    route = [(i, i + distance) for i in range(count) if 0 <= i + distance < count]
    return lax.ppermute(value, axis, route)


def swapped(value, axis, bit):
    return lax.ppermute(value, axis, [(i, i ^ bit) for i in range(lax.axis_size(axis))])


def all_sum(value, axis):
    bit = 1
    while bit < lax.axis_size(axis):
        value = value + swapped(value, axis, bit)
        bit *= 2
    return value


def sum_pairs(value, axis):
    parts = [swapped(value, axis, mask) for mask in range(1, lax.axis_size(axis))]
    return value + sum(parts[1:], parts[0])


def summed(blocks):
    total = blocks[0].astype(f32)
    for block in blocks[1:]:
        total = total + block.astype(f32)
    return total


def halves_of(parts, axis, bit):
    upper = (lax.axis_index(axis) & bit) != 0
    kept = [jnp.where(upper, b, a) for a, b in zip(parts[0::2], parts[1::2])]
    given = [jnp.where(upper, a, b) for a, b in zip(parts[0::2], parts[1::2])]
    return kept, given


class Last:

    def __init__(self, kept, arrived, axis, pieces):
        parts = jnp.split(kept.astype(f32) + arrived.astype(f32), lax.axis_size(axis) // 2, axis=1)
        bit = 2
        while True:
            keep, give = halves_of(parts, axis, bit)
            give = jnp.concatenate(give, axis=1).astype(bf16)
            if 2 * bit >= lax.axis_size(axis):
                break
            other = jnp.split(swapped(give, axis, bit), len(keep), axis=1)
            parts = [k + o.astype(f32) for k, o in zip(keep, other)]
            bit *= 2
        self.axis, self.bit, self.keep = axis, bit, keep[0]
        rows = give.shape[0] // pieces
        self.give = [give[i * rows : (i + 1) * rows] for i in range(pieces)]

    def send(self, piece):
        return swapped(self.give[piece], self.axis, self.bit)

    def total(self, arrived):
        return self.keep + jnp.concatenate(arrived, axis=0).astype(f32)


def ring_order(count):
    return list(range(0, count, 2)) + list(range(count - 1, 0, -2))


def dealt(value, axis):
    return lax.all_to_all(value, axis, 0, 0, tiled=True)


def repeated(value, count):
    return jnp.broadcast_to(value[None], (count,) + value.shape)


def grouped_send(value, axis):
    count = lax.axis_size(axis) // 2
    me = lax.axis_index(axis) >> 1
    rows = value.shape[0] // count
    own = lax.dynamic_slice_in_dim(value, me * rows, rows, 0)
    return [own] + [
        swapped(lax.dynamic_slice_in_dim(value, (me ^ mask) * rows, rows, 0), axis, 2 * mask)
        for mask in range(1, count)
    ]


class Ring:

    def __init__(self, values, axis):
        count = lax.axis_size(axis)
        self.values, self.axis, self.count, self.hop = values, axis, count, 0
        self.order = ring_order(count)
        me = lax.axis_index(axis)
        self.spot = jnp.where(me % 2 == 0, me // 2, count - (me + 1) // 2)
        self.moving = self.mine()

    def signs(self):
        return [1 - 2 * (i % 2) for i in range(len(self.values))]

    def mine(self):
        blocks = []
        for value, sign in zip(self.values, self.signs()):
            rows = value.shape[0] // self.count
            ahead = sign * (self.count - 1 - self.hop)
            spot = (self.spot + ahead + 2 * self.count) % self.count
            owner = jnp.where(spot < self.count // 2, 2 * spot, 2 * (self.count - spot) - 1)
            blocks.append(lax.dynamic_slice_in_dim(value, owner * rows, rows, 0))
        return blocks

    def send(self):
        arrived = []
        for block, sign in zip(self.moving, self.signs()):
            route = [
                (self.order[i], self.order[(i + sign) % self.count]) for i in range(self.count)
            ]
            arrived.append(lax.ppermute(block, self.axis, route))
        return arrived

    def add(self, arrived):
        self.hop += 1
        blocks = [a.astype(f32) + b.astype(f32) for a, b in zip(arrived, self.mine())]
        done = self.hop == self.count - 1
        self.moving = blocks if done else [block.astype(bf16) for block in blocks]
        return done


def scatter_direct(value, axis):
    count = lax.axis_size(axis)
    me = lax.axis_index(axis)
    wide = value.shape[1] // count
    own = lax.dynamic_slice_in_dim(value, me * wide, wide, 1)
    return summed([own] + [
        swapped(lax.dynamic_slice_in_dim(value, (me ^ mask) * wide, wide, 1), axis, mask)
        for mask in range(1, count)
    ])


def gather_direct(value, axis):
    count = lax.axis_size(axis)
    me = lax.axis_index(axis)
    parts = [value] + [swapped(value, axis, mask) for mask in range(1, count)]
    ordered = []
    for place in range(count):
        part = parts[place]
        for mask in range(1, count):
            part = jnp.where(me == mask, parts[place ^ mask], part)
        ordered.append(part)
    return jnp.concatenate(ordered, axis=1)


def all_sum_low(value, axis):
    bit = 1
    while bit < lax.axis_size(axis):
        value = value + swapped(value.astype(bf16), axis, bit).astype(f32)
        bit *= 2
    return value


def call(kernel, grid, in_specs, out_specs, out_shape, scratch, micros, vmem, **names):
    return pl.pallas_call(
        kernel,
        grid=grid,
        in_specs=in_specs,
        out_specs=out_specs,
        out_shape=out_shape,
        scratch_shapes=scratch,
        compiler_params=pltpu.CompilerParams(
            dimension_semantics=("arbitrary",), vmem_limit_bytes=vmem * 1024 * 1024
        ),
        cost_estimate=pl.CostEstimate(
            flops=micros * 10**9, bytes_accessed=micros * 10**6, transcendentals=0
        ),
        **names,
    )


def together(*values):
    return lax.optimization_barrier(values)


def per_device(
    x_in, norm_gain, w_zx, w_bc, w_dt, conv_x, conv_bc, head_params, gate_gain, w_out, lengths,
    grad_out,
):
    tokens, width = x_in.shape
    heads = head_params.shape[1]
    inner = gate_gain.shape[0]
    members = lax.axis_size("tensor")
    devices = lax.axis_size("seq")
    inner_all = inner * members
    total_cols = inner + 2 * STATE
    chunks = tokens // CHUNK
    reach = min(-(-REACH // tokens), devices - 1)
    device = lax.axis_index("seq")
    member = lax.axis_index("tensor")

    shape = jax.ShapeDtypeStruct
    rows = lambda wide: pl.BlockSpec((CHUNK, wide), lambda i: (i, 0))
    back = lambda wide: pl.BlockSpec((CHUNK, wide), lambda i: (chunks - 1 - i, 0))
    whole = lambda *dims: pl.BlockSpec(dims, lambda i: (0,) * len(dims))
    stack = lambda *dims: pl.BlockSpec((1,) + dims, lambda i: (i,) + (0,) * len(dims))
    stack_back = lambda *dims: pl.BlockSpec(
        (1,) + dims, lambda i: (chunks - 1 - i,) + (0,) * len(dims)
    )
    c_at = inner // STATE + 1
    c_rows = pl.BlockSpec((CHUNK, STATE), lambda i: (i, c_at))
    c_back = pl.BlockSpec((CHUNK, STATE), lambda i: (chunks - 1 - i, c_at))

    ends = jnp.cumsum(lengths)
    starts = ends - lengths
    places = device * tokens + jnp.arange(tokens, dtype=jnp.int32)[:, None]
    seg_first = jnp.max(jnp.where(starts[None, :] <= places, starts[None, :], 0), axis=1)
    seg_last = jnp.min(
        jnp.where(ends[None, :] > places, ends[None, :], jnp.iinfo(jnp.int32).max // 2), axis=1
    )
    info = jnp.stack([seg_first, seg_last], axis=1) - device * tokens

    cotangent = lax.all_gather(grad_out, "tensor", axis=1, tiled=True)

    x_halo = along(x_in[tokens - HALO :], "seq", 1)
    w_both = lax.optimization_barrier(jnp.transpose(w_zx, (1, 0, 2)))
    block = 256
    tile = lambda wide: pl.BlockSpec((block, wide), lambda i: (i, 0))
    normed, x_scale, u, halo, dt_raw = call(
        project_kernel, (tokens // block,),
        [tile(width), whole(HALO, width), whole(1, width),
         pl.BlockSpec((1, width, inner), lambda i: (1, 0, 0)), whole(width, 2 * STATE),
         whole(heads, width)],
        [tile(width), tile(1), tile(total_cols), whole(HALO, total_cols), tile(heads)],
        [shape((tokens, width), bf16), shape((tokens, 1), f32),
         shape((tokens, total_cols), bf16), shape((HALO, total_cols), bf16),
         shape((tokens, heads), f32)],
        [], 10, 56, name="project",
    )(x_in, x_halo, norm_gain[None, :], w_both, w_bc, w_dt.T)
    conv_w = jnp.concatenate([conv_x, conv_bc], axis=1)

    acts, slope, dt, logs, spread_out, local_in, leaving = call(
        fwd_kernel, (chunks,),
        [rows(total_cols), whole(HALO, total_cols), whole(WIDTH + 1, total_cols), rows(heads),
         whole(3, heads), rows(2)],
        [rows(total_cols), rows(total_cols), rows(heads), rows(heads), rows(3 * inner),
         stack(STATE, inner), whole(STATE + 2 * PAD, inner)],
        [shape((tokens, total_cols), bf16), shape((tokens, total_cols), bf16),
         shape((tokens, heads), f32), shape((tokens, heads), f32),
         shape((tokens, 3 * inner), bf16), shape((chunks, STATE, inner), bf16),
         shape((STATE + 2 * PAD, inner), bf16)],
        [pltpu.VMEM((CHUNK + PAD, total_cols), f32), pltpu.VMEM((STATE, inner), f32),
         pltpu.VMEM((PAD, inner), f32)],
        12, 56, name="conv_states",
    )(u, halo, conv_w, dt_raw, head_params, info)
    spread_rows = lambda which: pl.BlockSpec((CHUNK, inner), lambda i: (i, which))
    spread_back = lambda which: pl.BlockSpec((CHUNK, inner), lambda i: (chunks - 1 - i, which))

    def unpacked(sent):
        low = sent[STATE:].astype(f32)
        return sent[:STATE].astype(f32), low[0:1] + low[PAD : PAD + 1]

    def joined(sent, arrived):
        state, fade = unpacked(sent)
        before, fade_before = unpacked(arrived)
        state, fade = state + fade * before, fade * fade_before
        high = fade.astype(bf16).astype(f32)
        rows = [jnp.broadcast_to(part, (PAD, inner)) for part in (high, fade - high)]
        return jnp.concatenate([state] + rows, axis=0).astype(bf16)

    def chained(sent, sign, first_work, second_work):
        arrived, first = together(along(sent, "seq", sign), first_work())
        pair = joined(sent, arrived)
        hops = [hop for hop in range(1, reach + 1, 2) if hop < devices]
        arrived, second = together(
            [along(pair, "seq", sign * hop) for hop in hops], second_work()
        )
        total = unpacked(arrived[-1])[0]
        for block in arrived[-2::-1]:
            state, fade = unpacked(block)
            total = state + fade * total
        return total, first, second

    back_dims = (((1,), (1,)), ((), ()))
    weight_dims = (((0,), (0,)), ((), ()))
    low = lambda a, b, dims: lax.dot_general(a, b, dims, preferred_element_type=f32).astype(bf16)
    wide = lambda a, b, dims: lax.dot_general(a, b, dims, preferred_element_type=f32)

    state_in, grad_gate, gate_in = chained(
        leaving, 1,
        lambda: low(cotangent, w_out, back_dims),
        lambda: low(normed, w_both[0], (((1,), (0,)), ((), ()))),
    )

    gain_row = gate_gain[None, :]
    mixed, entering, sums = call(
        mix_kernel, (chunks,),
        [rows(total_cols), spread_rows(0), rows(heads), stack(STATE, inner),
         whole(STATE, inner), rows(inner), rows(inner), whole(1, inner), whole(3, heads), rows(2)],
        [rows(inner), stack(STATE, inner), stack(PAD, CHUNK)],
        [shape((tokens, inner), f32), shape((chunks, STATE, inner), bf16),
         shape((chunks, PAD, CHUNK), f32)],
        [pltpu.VMEM((PAD, heads), f32)], 15, 14, name="mix",
    )(acts, spread_out, logs, local_in, state_in, gate_in, grad_gate, gain_row,
      head_params, info)

    gate_rows = sum_pairs(sums, "tensor")

    gate_normed, grad_gate_in, grad_mixed, grad_local, grad_leaving, grad_gain, grad_skip = call(
        partial(gate_back_kernel, inner_all=inner_all), (chunks,),
        [back(inner), back(inner), back(inner), stack_back(PAD, CHUNK), whole(1, inner),
         back(inner), c_back, spread_back(2), back(heads), back(2),
         pl.BlockSpec((2 * PAD, inner), lambda i: (STATE // (2 * PAD), 0))],
        [back(inner), back(inner), back(inner), stack_back(STATE, inner),
         whole(STATE + 2 * PAD, inner), whole(1, inner), whole(1, inner)],
        [shape((tokens, inner), bf16), shape((tokens, inner), bf16), shape((tokens, inner), bf16),
         shape((chunks, STATE, inner), bf16), shape((STATE + 2 * PAD, inner), bf16),
         shape((1, inner), f32), shape((1, inner), f32)],
        [pltpu.VMEM((STATE, inner), f32)], 12, 14, name="gate_back",
    )(mixed, gate_in, grad_gate, gate_rows, gain_row, acts, acts, spread_out, logs, info, leaving)

    tall = lambda cols: pl.BlockSpec((tokens, cols), lambda i: (0, i))
    grad_in, grad_normed_z, early = chained(
        grad_leaving, -1,
        lambda: low(grad_gate_in, w_both[0], back_dims),
        lambda: call(
            early_kernel, (width // 512,),
            [tall(512), tall(512), whole(tokens, inner), whole(tokens, inner)],
            pl.BlockSpec((512, 2 * inner), lambda i: (i, 0)), shape((width, 2 * inner), bf16), [],
            14, 20, name="early",
        )(cotangent, normed, gate_normed, grad_gate_in),
    )
    early, grad_in = together(early, grad_in)
    early_sum = lax.psum_scatter(early, "seq", scatter_dimension=0, tiled=True)

    part = back
    grad_u, grad_dt, tail, sent, grad_conv, grad_heads = call(
        bwd_kernel, (chunks,),
        [part(inner), part(total_cols), part(total_cols), part(heads), part(heads),
         part(heads), spread_back(0), spread_back(1), spread_back(2),
         stack_back(STATE, inner), stack_back(STATE, inner), whole(STATE, inner),
         part(total_cols), whole(HALO, total_cols),
         whole(WIDTH + 1, total_cols), whole(3, heads), part(2)],
        [part(total_cols), part(heads), whole(HALO, total_cols), whole(HALO, total_cols),
         whole(PAD, total_cols), whole(PAD, heads)],
        [shape((tokens, total_cols), bf16), shape((tokens, heads), bf16),
         shape((HALO, total_cols), f32), shape((HALO, total_cols), f32),
         shape((PAD, total_cols), f32), shape((PAD, heads), f32)],
        [pltpu.VMEM((PAD, heads), f32), pltpu.VMEM((CHUNK + PAD, total_cols), f32),
         pltpu.VMEM((CHUNK, CHUNK), f32),
         pltpu.VMEM((2 * PAD, 256), f32), pltpu.VMEM((2 * CHUNK, inner), bf16)],
        30, 56, name="scan_back",
    )(grad_mixed, acts, slope, dt, logs, dt_raw, spread_out, spread_out, spread_out,
      entering, grad_local, grad_in, u, halo, conv_w, head_params, info)

    core = (member & 1).reshape(1)
    split_tile = pl.BlockSpec((2, block, width // 2), lambda i: (0, i, 0))
    own_bc = 2 * STATE // members

    slice_width = grad_out.shape[1]
    x_part = lax.dynamic_slice_in_dim(x_in, member * slice_width, slice_width, 1).astype(f32)
    parity = device & 1

    cuts = [0, inner // 4, inner // 2, inner]
    sent = along(sent, "seq", -1)
    late = low(normed, grad_u[:, :inner], weight_dims)
    late_blocks = late.reshape(devices // 2, 2, width // devices, inner)
    half_of = lambda odd: lax.dynamic_index_in_dim(late_blocks, odd, 1, False).reshape(-1, inner)
    given, kept = half_of(1 - parity), half_of(parity)
    given, kept, gate_normed = together(given, kept, gate_normed)
    piece_of = lambda at: swapped(given[:, cuts[at] : cuts[at + 1]], "seq", 1)
    branch_kept, branch_given = call(
        partial(branch_kernel, blocks=members), (tokens // block,),
        [pl.BlockSpec(memory_space=pltpu.SMEM), tile(inner), whole(inner, width)],
        [tile(width // 2)] * 2, [shape((tokens, width // 2), bf16)] * 2, [], 9, 56, name="branch",
    )(core, gate_normed, w_out)
    arrived_0, sent, branch_kept, branch_given = together(
        piece_of(0), sent, branch_kept, branch_given
    )
    tail = (tail + sent).astype(bf16)
    grad_u = lax.dynamic_update_slice_in_dim(grad_u, tail, tokens - HALO, 0)
    factors = jnp.concatenate([normed[tokens - HALO :], tail[:, :inner]], axis=1)
    factors = jnp.concatenate([factors, swapped(factors, "seq", 1)], axis=0)

    def first_work():
        return call(
            partial(normed_back_kernel, blocks=members), (tokens // block,),
            [pl.BlockSpec(memory_space=pltpu.SMEM), tile(total_cols), tile(heads), tile(width),
             tile(width), tile(1), whole(1, width),
             pl.BlockSpec((1, width, inner), lambda i: (1, 0, 0)), whole(width, 2 * STATE),
             whole(heads, width)],
            [tile(width // 2), tile(width // 2), pl.BlockSpec((1, PAD, block), lambda i: (i, 0, 0)), whole(1, width)],
            [shape((tokens, width // 2), bf16), shape((tokens, width // 2), bf16),
             shape((tokens // block, PAD, block), f32),
             shape((1, width), f32)],
            [], 15, 56, name="normed_back",
        )(core, grad_u, grad_dt, grad_normed_z, x_in, x_scale, norm_gain[None, :], w_both, w_bc,
          w_dt.T)

    grad_bc, arrived_1, (normed_kept, normed_given, dots_here, gain), factors = together(
        scatter_direct(grad_u[:, inner:], "tensor").astype(bf16), piece_of(1), first_work(), factors
    )

    def fold(kept, arrived):
        bit = 2
        while bit < members:
            wide_now = kept.shape[1]
            kept, given = call(
                fold_kernel, (tokens // block,),
                [pl.BlockSpec(memory_space=pltpu.SMEM), tile(wide_now), tile(wide_now)],
                [tile(wide_now // 2)] * 2,
                [shape((tokens, wide_now // 2), f32), shape((tokens, wide_now // 2), bf16)],
                [], 3, 12, name="fold",
            )(((member // bit) & 1).reshape(1), kept, arrived)
            bit *= 2
            if bit < members:
                arrived = swapped(given, "tensor", bit // 2)
        return kept, swapped(given, "tensor", bit // 2)


    def second_work():
        shared = jnp.concatenate(
            [grad_conv[: WIDTH + 1, inner:].reshape(-1), gain.reshape(-1)]
        ).reshape(-1, 128)
        return (
            sum_pairs(dots_here[:, 0], "tensor"), sum_pairs(shared, "tensor"),
            swapped(branch_given, "tensor", 1),
        )

    dots, shared, branch_other = together(*second_work())

    heads_here = jnp.concatenate(
        [grad_heads[:2], jnp.sum(grad_skip.reshape(heads, HEAD_DIM), axis=1)[None, :]], axis=0
    )
    own_small = jnp.concatenate(
        [grad_conv[: WIDTH + 1, :inner].reshape(-1), grad_gain.reshape(-1),
         heads_here.reshape(-1), jnp.zeros((-3 * heads % 128,), f32)]
    ).reshape(-1, 128)
    small = jnp.concatenate([shared, own_small], axis=0)
    high = small.astype(bf16)
    small = jnp.concatenate([high, (small - high.astype(f32)).astype(bf16)], axis=1)
    small_size = small.size
    block_cols = width // devices
    small = jnp.pad(small.reshape(-1), (0, -small_size % block_cols)).reshape(-1, block_cols)

    def third_work():
        both = jnp.concatenate([grad_bc, grad_dt], axis=1)
        bcdt = low(both, normed, weight_dims)
        blocks = jnp.transpose(bcdt.reshape(-1, devices, width // devices), (1, 0, 2))
        blocks = jnp.concatenate([blocks, repeated(small, devices)], axis=1)
        branch_keep, branch_sent = fold(branch_kept, branch_other)
        return (
            dealt(blocks, "seq"), branch_keep, branch_sent, swapped(normed_given, "tensor", 1),
        )

    bcdt, branch_keep, branch_sent, normed_other = together(*third_work())

    def fourth_work():
        total = summed(bcdt)
        normed_keep, normed_sent = fold(normed_kept, normed_other)
        block_out = (x_part + branch_keep + branch_sent.astype(f32)).astype(bf16)
        rows = repeated(total[:own_bc].astype(bf16).T, devices)
        return total, dealt(rows, "seq"), normed_keep, normed_sent, block_out

    bcdt, bc_rows, normed_keep, normed_sent, block_out, arrived_2 = together(
        *fourth_work(), piece_of(2)
    )
    arrived = jnp.concatenate([arrived_0, arrived_1, arrived_2], axis=1)
    rows_of = factors[:, :width].reshape(2 * HALO, devices // 2, 2, width // devices)
    rows_of = lax.dynamic_index_in_dim(rows_of, parity, 2, False).reshape(2 * HALO, -1)
    flying = (
        wide(rows_of, factors[:, width:], weight_dims) + kept.astype(f32) + arrived.astype(f32)
    ).astype(bf16)
    flying, bc_rows, normed_keep = together(flying, bc_rows, normed_keep)

    def fifth_work():
        grad_normed = normed_keep + normed_sent.astype(f32)
        gain_part = lax.dynamic_slice_in_dim(norm_gain, member * slice_width, slice_width, 0)
        row_mean = dots.reshape(tokens, 1) * (1.0 / width)
        grad_x = (
            x_scale * (grad_normed * gain_part[None, :] - x_part * x_scale * row_mean)
            + grad_out.astype(f32)
        )
        bc_all = gather_direct(bc_rows.reshape(width, own_bc), "tensor")
        return grad_x, bc_all

    sums, (grad_x, bc_all) = (grouped_send(flying, "seq"), fifth_work())
    grad_w_bc = bc_all.astype(f32)
    small = bcdt[own_bc + heads :].reshape(-1)[:small_size].reshape(-1, 256)
    small = small[:, 0:128] + small[:, 128:256]
    bcdt = bcdt[: own_bc + heads]
    early_sum = early_sum.astype(f32)
    grad_z_sum = early_sum[:, inner:]
    own_rows = width // devices
    grad_w_out = call(
        turn_kernel, (inner // 128,), [pl.BlockSpec((own_rows, 128), lambda i: (0, i))],
        pl.BlockSpec((128, own_rows), lambda i: (i, 0)), shape((inner, own_rows), f32), [], 2, 12,
        name="turn",
    )(early_sum)

    grad_w_dt = bcdt[own_bc:].T

    shared, own = small[: shared.shape[0]].reshape(-1), small[shared.shape[0] :].reshape(-1)
    bc_size = (WIDTH + 1) * 2 * STATE
    x_size = (WIDTH + 1) * inner
    grad_conv_bc = shared[:bc_size].reshape(WIDTH + 1, 2 * STATE)
    grad_norm_gain = shared[bc_size:]
    grad_conv_x = own[:x_size].reshape(WIDTH + 1, inner)
    grad_gate_gain = own[x_size : x_size + inner]
    grad_head = own[x_size + inner : x_size + inner + 3 * heads].reshape(3, heads)

    (sums, grad_z_sum, grad_w_out, grad_w_bc, grad_w_dt, grad_x, block_out, grad_conv_x,
     grad_conv_bc, grad_head, grad_gate_gain, grad_norm_gain) = together(
        sums, grad_z_sum, grad_w_out, grad_w_bc, grad_w_dt, grad_x, block_out, grad_conv_x,
        grad_conv_bc, grad_head, grad_gate_gain, grad_norm_gain)
    grad_w_zx = jnp.stack([grad_z_sum, summed(sums)], axis=1)
    return (
        block_out, grad_x, grad_norm_gain, grad_w_zx, grad_w_bc, grad_w_dt, grad_conv_x,
        grad_conv_bc, grad_head, grad_gate_gain, grad_w_out,
    )


def solution(mesh):
    return jax.shard_map(
        per_device,
        mesh=mesh,
        in_specs=(
            P("seq", None), P(), P(None, None, "tensor"), P(), P(None, "tensor"),
            P(None, "tensor"), P(), P(None, "tensor"), P("tensor"), P("tensor", None), P(),
            P("seq", "tensor"),
        ),
        out_specs=(
            P("seq", "tensor"), P("seq", "tensor"), P(), P("seq", None, "tensor"), P(),
            P("seq", "tensor"), P(None, "tensor"), P(), P(None, "tensor"), P("tensor"),
            P("tensor", "seq"),
        ),
        check_vma=False,
    )
```
